32 devices in a mesh: gran: 4 (over y, core), dp: 4 (over z), hid: 2 (over x).
Axes of the slice: x: 2, y: 2, z: 4, core: 2. Of those that a mesh axis runs over, the one named last changes fastest.
Arguments:
- tokens: bfloat16 [4096, 1536], P(('dp', 'hid')), may hold values from -6 to 6
- ln1_gain: bfloat16 [1536], P(('dp', 'hid')), may hold values from 0.5 to 1.5
- ln1_bias: bfloat16 [1536], P(('dp', 'hid')), may hold values from -1 to 1
- w_qkv: bfloat16 [1536, 4608], P(('dp', 'hid')), may hold values from -0.15625 to 0.15625
- w_attn: bfloat16 [1536, 1536], P(('dp', 'hid')), may hold values from -0.625 to 0.625
- ln2_gain: bfloat16 [1536], P(('dp', 'hid')), may hold values from 0.5 to 1.5
- ln2_bias: bfloat16 [1536], P(('dp', 'hid')), may hold values from -1 to 1
- w_in: bfloat16 [1536, 6144], P(None, 'hid'), may hold values from -0.15625 to 0.15625
- w_out: bfloat16 [6144, 1536], P('hid'), may hold values from -0.15625 to 0.15625
- cotangent: bfloat16 [4, 4096, 1536], P('gran', ('dp', 'hid')), may hold values from -6 to 6
- active_units: int32 [4], replicated, may hold values from 512 to 6144, as said below
Outputs:
- outputs: bfloat16 [4, 4096, 1536], P('gran', ('dp', 'hid'))
- x_grad: float32 [4096, 1536], P(('dp', 'hid'))
- ln1_gain_grad: float32 [1536], P(('dp', 'hid'))
- ln1_bias_grad: float32 [1536], P(('dp', 'hid'))
- w_qkv_grad: float32 [1536, 4608], P(('dp', 'hid'))
- w_attn_grad: float32 [1536, 1536], P(('dp', 'hid'))
- ln2_gain_grad: float32 [1536], P(('dp', 'hid'))
- ln2_bias_grad: float32 [1536], P(('dp', 'hid'))
- w_in_grad: float32 [1536, 6144], P(None, 'hid')
- w_out_grad: float32 [6144, 1536], P('hid')
The draws below stay inside these ranges and needn't reach their ends.
Inputs may be any that keep to these rules, and one draw needn't show every extreme that they name: Every entry of active_units is a multiple of 128 and they rise strictly. For g < 3, active_units[g] is greater than 6144 * 2^g // 16 and at most 6144 * 2^g // 8, so that granularity g uses only the first 2^g pieces of 768 hidden units; in every draw some g < 3 reaches that bound. The last entry is 6144.
All inputs are finite; a program needn't handle non-finite values.
Results may differ from the reference program's by a relative error of at most 0.012.
Values may be sent and summed in bfloat16 or wider, within the bound.
No kernel may reach another device: no remote copies, remote signals or barrier semaphores. Data moves between devices by JAX's collectives and lax.ppermute only.
A program may use at most 384 MiB of HBM per device.

```python
import math
import jax
import jax.numpy as jnp
from jax import lax

D = 1536
HEADS = 12
HD = 128
FF = 6144
LEN = 512
GRAN = 4
TOKENS = 4096


def draw_active_units(key, part):
    key = jax.random.fold_in(key, 11)
    unit_size = FF // 48
    subkeys = jax.random.split(key, 4)
    smallest = jax.random.randint(subkeys[0], (), 4, 7)
    middle = jax.random.randint(subkeys[1], (), 7, 13)
    larger = jax.random.randint(subkeys[2], (), 13, 25)
    counts = jnp.stack([smallest, middle, larger]).astype(jnp.int32)
    bounds = jnp.array([6, 12, 24], jnp.int32)
    chosen = jax.random.randint(subkeys[3], (), 0, 3)
    counts = jnp.where(jnp.arange(3, dtype=jnp.int32) == chosen, bounds, counts)
    counts = jnp.concatenate([counts, jnp.array([48], jnp.int32)])
    return (counts * unit_size).astype(jnp.int32)


def block_scale(stream_key, dims, cuts, least, top_value):
    level, own = 1.0, jax.random.fold_in(stream_key, 6)
    for position, blocks in cuts:
        steps = jnp.exp(jax.random.uniform(jax.random.fold_in(own, position), (blocks,), jnp.float32, least / len(cuts), top_value / len(cuts)))
        level = level * jnp.repeat(steps, dims[position] // blocks).reshape([-1 if axis == position else 1 for axis in range(len(dims))])
    return level


def normal_values(key, shape, width, limit, cuts=(), kind=jnp.bfloat16):
    gain = block_scale(key, shape, cuts, -0.22, 0.18) if cuts else 1.0
    values = jax.random.normal(key, shape, jnp.float32) * width * gain
    return jnp.minimum(jnp.maximum(values, -limit), limit).astype(kind)


def setup_inputs(seed: int = 0) -> dict:
    key_list = jax.random.split(jax.random.key(seed), 12)
    tokens = normal_values(key_list[0], (TOKENS, D), 1.0, 6.0, ((0, 8),))
    ln1_gain = jnp.clip(1.0 + 0.1 * jax.random.normal(key_list[1], (D,), jnp.float32), 0.5, 1.5).astype(jnp.bfloat16)
    ln1_bias = normal_values(key_list[2], (D,), 0.2, 1.0, ((0, 8),))
    w_qkv = normal_values(key_list[3], (D, 3 * D), D ** -0.5, 0.15625, ((0, 8),))
    w_attn = normal_values(key_list[4], (D, D), (D // 16) ** -0.5, 0.625, ((0, 8),))
    ln2_gain = jnp.clip(1.0 + 0.1 * jax.random.normal(key_list[5], (D,), jnp.float32), 0.5, 1.5).astype(jnp.bfloat16)
    ln2_bias = normal_values(key_list[6], (D,), 0.2, 1.0, ((0, 8),))
    w_in = normal_values(key_list[7], (D, FF), D ** -0.5, 0.15625, ((1, 2),))
    w_out = normal_values(key_list[8], (FF, D), (FF // 4) ** -0.5, 0.15625, ((0, 2),))
    cotangent = normal_values(key_list[9], (GRAN, TOKENS, D), 1.0, 6.0, ((0, 4), (1, 8)))
    active_units = draw_active_units(jax.random.fold_in(key_list[11], 71), 0)
    return {"tokens": tokens, "ln1_gain": ln1_gain, "ln1_bias": ln1_bias, "w_qkv": w_qkv, "w_attn": w_attn, "ln2_gain": ln2_gain, "ln2_bias": ln2_bias, "w_in": w_in, "w_out": w_out, "cotangent": cotangent, "active_units": active_units}


EPS = 1e-05
GELU_C = 0.7978845608028654
PRECISION_HIGH = lax.Precision.HIGHEST

@jax.custom_vjp
def low(v):
    return lax.optimization_barrier(v.astype(jnp.bfloat16)).astype(jnp.float32)

@jax.custom_vjp
def reduced_backward(v):
    return v

def low_keep(v):
    return (low(v), None)

def low_pass(kept, grad):
    return (grad,)

def back_keep(v):
    return (v, None)

def back_low(kept, grad):
    return (low(grad),)
low.defvjp(low_keep, low_pass)
reduced_backward.defvjp(back_keep, back_low)

def gelu_tanh(values):
    return 0.5 * values * (1.0 + jnp.tanh(GELU_C * (values + 0.044715 * values * values * values)))

def norm_layer(values, gain_vec, bias_vec):
    average = lax.optimization_barrier(jnp.mean(values, axis=-1, keepdims=True))
    centred = values - average
    spread = lax.optimization_barrier(jnp.mean(centred * centred, axis=-1, keepdims=True))
    return centred * lax.rsqrt(spread + EPS) * gain_vec + bias_vec

def rotary_tables(length):
    half_dim = HD // 2
    freqs = 10000.0 ** (-(jnp.arange(half_dim, dtype=jnp.float32) * 2.0 / HD))
    angles = jnp.arange(length, dtype=jnp.float32)[:, None] * freqs[None, :]
    return (jnp.cos(angles)[:, None, :], jnp.sin(angles)[:, None, :])

def rotary(tensor, cosine, sine):
    lower = tensor[..., :HD // 2]
    upper = tensor[..., HD // 2:]
    return jnp.concatenate([lower * cosine - upper * sine, upper * cosine + lower * sine], axis=-1)

def layer_forward(input_batch, gain1, bias1, query_key_value_weight, attention_weight, gain2, bias2, input_weight, output_weight, hidden_unit_mask):
    seq_block = input_batch.shape[0]
    length = input_batch.shape[1]
    normalized_rows = low(norm_layer(input_batch, gain1, bias1))
    query_key_value = reduced_backward(jnp.einsum('cwk,ki->cwi', normalized_rows, query_key_value_weight, precision=PRECISION_HIGH))
    cosine, sine = rotary_tables(length)
    shape_four = (seq_block, length, HEADS, HD)
    queries = low(rotary(query_key_value[..., :D].reshape(shape_four), cosine, sine))
    keys_rot = low(rotary(query_key_value[..., D:2 * D].reshape(shape_four), cosine, sine))
    values = low(query_key_value[..., 2 * D:].reshape(shape_four))
    scores = jnp.einsum('sqhe,skhe->shqk', queries, keys_rot, precision=PRECISION_HIGH) / math.sqrt(HD)
    causal = jnp.arange(length)[:, None] >= jnp.arange(length)[None, :]
    scores = reduced_backward(jnp.where(causal, scores, -1000000000.0))
    row_top = lax.optimization_barrier(jnp.max(scores, axis=-1, keepdims=True))
    exponent = jnp.exp(scores - row_top)
    probs = low(exponent / lax.optimization_barrier(jnp.sum(exponent, axis=-1, keepdims=True)))
    mixed_output = jnp.einsum('shqk,skhe->sqhe', probs, values, precision=PRECISION_HIGH).reshape(seq_block, length, D)
    mixed_output = low(reduced_backward(mixed_output))
    hidden_width = input_batch + reduced_backward(jnp.einsum('cwk,ki->cwi', mixed_output, attention_weight, precision=PRECISION_HIGH))
    second_normalized = low(norm_layer(hidden_width, gain2, bias2))
    preactivation = reduced_backward(jnp.einsum('jrq,qy->jry', second_normalized, input_weight, precision=PRECISION_HIGH) * hidden_unit_mask)
    activation_rows = low(gelu_tanh(preactivation))
    return hidden_width + reduced_backward(jnp.einsum('jyg,gb->jyb', activation_rows, output_weight, precision=PRECISION_HIGH))

def reference(tokens, ln1_gain, ln1_bias, w_qkv, w_attn, ln2_gain, ln2_bias, w_in, w_out, cotangent, active_units):
    weights = tuple((member.astype(jnp.float32) for member in (ln1_gain, ln1_bias, w_qkv, w_attn, ln2_gain, ln2_bias, w_in, w_out)))
    seq_count = TOKENS // LEN
    per_block = math.gcd(seq_count, max(1, 4096 // LEN))
    blocks = seq_count // per_block
    input_batch = tokens.astype(jnp.float32).reshape(blocks, per_block, LEN, D)
    unit_ids = jnp.arange(FF, dtype=jnp.int32)
    running = tuple((jnp.zeros_like(member) for member in weights))
    x_grad = jnp.zeros((TOKENS, D), jnp.float32)
    results = []
    for gran_level in range(GRAN):
        hidden_unit_mask = (unit_ids < active_units[gran_level]).astype(jnp.float32)
        cot_blocks = cotangent[gran_level].astype(jnp.float32).reshape(blocks, per_block, LEN, D)

        def one_block(carried, entry, hidden_unit_mask=hidden_unit_mask):
            block_in, block_cot = entry

            def forward(values, *params):
                return layer_forward(values, *params, hidden_unit_mask)
            layer_out, pullback = jax.vjp(forward, block_in, *weights)
            gradients = pullback(block_cot)
            carried = tuple((left + right for left, right in zip(carried, gradients[1:])))
            return (carried, (layer_out.astype(jnp.bfloat16), gradients[0]))
        running, (out_blocks, grad_blocks) = lax.scan(one_block, running, (input_batch, cot_blocks))
        results.append(out_blocks.reshape(TOKENS, D))
        x_grad = x_grad + grad_blocks.reshape(TOKENS, D)
    outputs = jnp.stack(results)
    return (outputs, x_grad, running[0], running[1], running[2], running[3], running[4], running[5], running[6], running[7])
```

```python
import math

import jax
import jax.numpy as jnp
from jax import lax
from jax.sharding import PartitionSpec as P

D = 1536
HEADS = 12
HD = 128

EPS = 1e-05
GELU_C = 0.7978845608028654
GELU_A = 0.044715
BF16 = jnp.bfloat16
F32 = jnp.float32

ALL_ROWS = ("dp", "hid")
LAYER = ("hid", "gran")


def round_low(values):
    return lax.reduce_precision(values, 8, 7).astype(BF16)


def dot(left, right, contract=((1,), (0,))):
    return lax.dot_general(left, right, (contract, ((), ())), preferred_element_type=F32)


def dot_nt(left, right):
    return dot(left, right, ((1,), (1,)))


def dot_tn(left, right):
    return dot(left, right, ((0,), (0,)))


def norm_parts(values):
    centred = values - jnp.mean(values, axis=-1, keepdims=True)
    scale = lax.rsqrt(jnp.mean(centred * centred, axis=-1, keepdims=True) + EPS)
    return centred * scale, scale


def norm_back(dout, unit, scale, gain):
    inner = dout * gain
    return scale * (
        inner
        - jnp.mean(inner, axis=-1, keepdims=True)
        - unit * jnp.mean(inner * unit, axis=-1, keepdims=True)
    )


def gelu_both(values):
    square = values * values
    bent = jnp.tanh(GELU_C * values * (1.0 + GELU_A * square))
    half = 0.5 * (1.0 + bent)
    slope = half + 0.5 * values * (1.0 - bent * bent) * (GELU_C * (1.0 + 3.0 * GELU_A * square))
    return values * half, slope


def rotary_tables(length):
    half_dim = HD // 2
    freqs = 10000.0 ** (-(jnp.arange(half_dim, dtype=F32) * 2.0 / HD))
    angles = jnp.arange(length, dtype=F32)[:, None] * freqs[None, :]
    return jnp.cos(angles), jnp.sin(angles)


def turn(block, cosine, sine):
    lower, upper = block[:, : HD // 2], block[:, HD // 2 :]
    return jnp.concatenate([lower * cosine - upper * sine, upper * cosine + lower * sine], axis=1)


def turn_back(block, cosine, sine):
    return turn(block, cosine, -sine)


def chain_sum(piece, dp_index):
    own = round_low(piece)
    inward = lax.ppermute(own, "dp", ((0, 1), (3, 2)))
    pair = round_low(own.astype(F32) + inward.astype(F32))
    other = lax.ppermute(pair, "dp", ((1, 2), (2, 1)))
    total = round_low(pair.astype(F32) + other.astype(F32))
    outward = lax.ppermute(total, "dp", ((1, 0), (2, 3)))
    middle = (dp_index == 1) | (dp_index == 2)
    return jnp.where(middle, total, outward)


def local(
    tokens,
    ln1_gain,
    ln1_bias,
    w_qkv,
    w_attn,
    ln2_gain,
    ln2_bias,
    w_in,
    w_out,
    cotangent,
    active_units,
):
    length = tokens.shape[0]
    grans = active_units.shape[0]
    hids = lax.axis_size("hid")
    gran_index = lax.axis_index("gran")
    dp_index = lax.axis_index("dp")
    hid_index = lax.axis_index("hid")
    heads = HEADS // grans
    part = heads * HD
    quarter = length // grans

    def head_columns(array, start):
        return lax.dynamic_slice_in_dim(array, start + gran_index * part, part, axis=1)

    vectors = jnp.stack([ln1_gain, ln1_bias, ln2_gain, ln2_bias], axis=1)
    qkv_rows = jnp.concatenate(
        [head_columns(w_qkv, 0), head_columns(w_qkv, D), head_columns(w_qkv, 2 * D), vectors], axis=1
    )
    qkv_all = lax.all_gather(qkv_rows, ALL_ROWS, axis=0, tiled=True)
    qkv_cols = qkv_all[:, : 3 * part]
    gains = qkv_all[:, 3 * part :].astype(F32).T
    gain_one, bias_one, gain_two, bias_two = (gains[i : i + 1] for i in range(4))
    attn_cols = lax.all_gather(head_columns(w_attn, 0), ALL_ROWS, axis=0, tiled=True)
    attn_full = lax.all_gather(attn_cols, "gran", axis=1, tiled=True)

    all_tokens = lax.all_gather(tokens, "hid", axis=0, tiled=True)
    out_grad = cotangent[0]
    all_cot = lax.all_gather(out_grad, LAYER, axis=0).reshape(hids, grans, length, D)
    slab = w_in.shape[1]
    block = slab // grans
    first_unit = hid_index * slab + gran_index * block
    total_units = slab * hids
    level = jnp.int32(0)
    for step in range(1, grans):
        bound = total_units * 2 ** (step - 1) // 8
        level = level + (first_unit >= bound).astype(jnp.int32)
    above = jnp.minimum(level + 1, grans - 1)

    def sum_from(start):
        keep = (jnp.arange(grans) >= start).astype(F32)[None, :, None, None]
        return jnp.sum(all_cot.astype(F32) * keep, axis=1).reshape(hids * length, D).astype(BF16)

    cot_lo, cot_hi = sum_from(level), sum_from(above)
    border = jnp.sum(jnp.where(jnp.arange(grans) == level, active_units, 0))
    low_unit = (first_unit + jnp.arange(block, dtype=jnp.int32)) < border
    cot_own = lax.psum_scatter(out_grad, "gran", scatter_dimension=0, tiled=True).astype(F32)

    x_rows = tokens.astype(F32)
    unit_one, scale_one = norm_parts(x_rows)
    normed_one = (unit_one * gain_one + bias_one).astype(BF16)
    qkv = dot(normed_one, qkv_cols)
    cosine, sine = rotary_tables(length)
    causal = jnp.arange(length)[:, None] >= jnp.arange(length)[None, :]
    kept, attended = [], []
    for head in range(heads):
        at = head * HD
        query = turn(qkv[:, at : at + HD], cosine, sine).astype(BF16)
        key = turn(qkv[:, part + at : part + at + HD], cosine, sine).astype(BF16)
        value = qkv[:, 2 * part + at : 2 * part + at + HD].astype(BF16)
        scores = jnp.where(causal, dot_nt(query, key) / math.sqrt(HD), -1000000000.0)
        exponent = jnp.exp(scores - jnp.max(scores, axis=-1, keepdims=True))
        probs = exponent / jnp.sum(exponent, axis=-1, keepdims=True)
        probs_low = probs.astype(BF16)
        attended.append(dot(probs_low, value).astype(BF16))
        kept.append((query, key, value, probs))
    attended = jnp.concatenate(attended, axis=1)
    everyone = lax.all_gather(attended, LAYER, axis=0).reshape(hids, grans, length, part)
    all_attended = everyone.transpose(0, 2, 1, 3).reshape(hids * length, D)
    hidden = all_tokens.astype(F32) + dot(all_attended, attn_full)
    unit_two, scale_two = norm_parts(hidden)
    normed_two = (unit_two * gain_two + bias_two).astype(BF16)

    w_in_block = lax.dynamic_slice_in_dim(w_in, gran_index * block, block, axis=1)
    w_out_block = lax.dynamic_slice_in_dim(w_out, gran_index * block, block, axis=0)
    pre = dot(normed_two, w_in_block)
    act, slope = gelu_both(pre)
    act = act.astype(BF16)
    dact = jnp.where(low_unit[None], dot_nt(cot_lo, w_out_block), dot_nt(cot_hi, w_out_block))
    dpre = (dact * slope).astype(BF16)
    out_term = jnp.where(low_unit[:, None], dot_tn(act, cot_lo), dot_tn(act, cot_hi))
    in_term = dot_tn(normed_two, dpre)
    dnormed_two = dot_nt(dpre, w_in_block).astype(BF16)

    pieces = 4
    out_chunks = [chain_sum(c, dp_index) for c in jnp.split(out_term, pieces, axis=0)]
    in_chunks = [chain_sum(c, dp_index) for c in jnp.split(in_term, pieces, axis=0)]
    w_out_grad = lax.all_gather(jnp.concatenate(out_chunks, axis=0), "gran", axis=0, tiled=True)
    w_in_grad = lax.all_gather(jnp.concatenate(in_chunks, axis=0), "gran", axis=1, tiled=True)

    dnormed_two = lax.psum_scatter(dnormed_two, LAYER, scatter_dimension=0, tiled=True).astype(F32)
    row = hid_index * length + gran_index * quarter

    def own_rows(array):
        return lax.dynamic_slice_in_dim(array, row, quarter, axis=0)

    unit_two, scale_two = own_rows(unit_two), own_rows(scale_two)
    dhidden = cot_own + norm_back(dnormed_two, unit_two, scale_two, gain_two)
    gain_two_term = jnp.sum(dnormed_two * unit_two, axis=0)
    bias_two_term = jnp.sum(dnormed_two, axis=0)
    dbranch = lax.all_gather(dhidden.astype(BF16), "gran", axis=0, tiled=True)

    attn_rows = lax.dynamic_slice_in_dim(attn_full, gran_index * part, part, axis=0)
    dattended = dot_nt(dbranch, attn_rows).astype(BF16)
    own_attended = lax.dynamic_slice_in_dim(all_attended, hid_index * length, length, axis=0)
    dbranch_cols = lax.dynamic_slice_in_dim(dbranch, gran_index * part, part, axis=1)
    attn_term = dot_tn(own_attended, dbranch_cols)
    dqueries, dkeys, dvalues = [], [], []
    for head in range(heads):
        query, key, value, probs = kept[head]
        dvec = dattended[:, head * HD : (head + 1) * HD]
        dprobs = dot_nt(dvec, value)
        inner = jnp.sum(probs * dprobs, axis=-1, keepdims=True)
        dscores = (probs * (dprobs - inner)).astype(BF16)
        dqueries.append(turn_back(dot(dscores, key) / math.sqrt(HD), cosine, sine).astype(BF16))
        dkeys.append(turn_back(dot_tn(dscores, query) / math.sqrt(HD), cosine, sine).astype(BF16))
        dvalues.append(dot_tn(probs.astype(BF16), dvec).astype(BF16))
    dqkv = jnp.concatenate(dqueries + dkeys + dvalues, axis=1)
    qkv_term = dot_tn(normed_one, dqkv)
    dnormed_one = lax.psum_scatter(
        dot_nt(dqkv, qkv_cols).astype(BF16), "gran", scatter_dimension=0, tiled=True
    ).astype(F32)

    unit_one = lax.dynamic_slice_in_dim(unit_one, gran_index * quarter, quarter, axis=0)
    scale_one = lax.dynamic_slice_in_dim(scale_one, gran_index * quarter, quarter, axis=0)
    dx = dhidden + norm_back(dnormed_one, unit_one, scale_one, gain_one)
    gain_one_term = jnp.sum(dnormed_one * unit_one, axis=0)
    bias_one_term = jnp.sum(dnormed_one, axis=0)
    x_grad = lax.all_gather(dx.astype(BF16), "gran", axis=0, tiled=True).astype(F32)

    vector_terms = jnp.stack([gain_one_term, bias_one_term, gain_two_term, bias_two_term], axis=1)
    terms = jnp.concatenate([qkv_term, attn_term, vector_terms], axis=1).astype(BF16)
    terms = lax.psum_scatter(terms, ALL_ROWS, scatter_dimension=0, tiled=True)
    terms = lax.all_gather(terms, "gran", axis=0).astype(F32)

    def grads_of(start):
        return [terms[k, :, start : start + part] for k in range(grans)]

    qkv_grad = jnp.concatenate(grads_of(0) + grads_of(part) + grads_of(2 * part), axis=1)
    attn_grad = jnp.concatenate(grads_of(3 * part), axis=1)
    vector_grads = jnp.sum(terms[:, :, 4 * part :], axis=0).T

    act_low = jnp.where(low_unit[None], act, 0)
    part_low = dot(act_low, w_out_block)
    part_all = part_low + dot(act - act_low, w_out_block)
    shares = []
    for k in range(grans):
        share = jnp.where(level < k, part_all, jnp.where(level == k, part_low, 0.0))
        shares.append(share.astype(BF16).reshape(hids, length, D))
    shares = jnp.stack(shares, axis=1).reshape(hids * grans * length, D)
    ffn = lax.psum_scatter(shares, LAYER, scatter_dimension=0, tiled=True).astype(F32)
    own_hidden = lax.dynamic_slice_in_dim(hidden, hid_index * length, length, axis=0)
    outputs = (own_hidden + ffn).astype(BF16)[None]

    return (
        outputs,
        x_grad,
        vector_grads[0],
        vector_grads[1],
        qkv_grad,
        attn_grad,
        vector_grads[2],
        vector_grads[3],
        w_in_grad.astype(F32),
        w_out_grad.astype(F32),
    )


def solution(mesh):
    return jax.shard_map(
        local,
        mesh=mesh,
        in_specs=(
            P(("dp", "hid"), None),
            P(("dp", "hid")),
            P(("dp", "hid")),
            P(("dp", "hid"), None),
            P(("dp", "hid"), None),
            P(("dp", "hid")),
            P(("dp", "hid")),
            P(None, "hid"),
            P("hid", None),
            P("gran", ("dp", "hid"), None),
            P(),
        ),
        out_specs=(
            P("gran", ("dp", "hid"), None),
            P(("dp", "hid"), None),
            P(("dp", "hid")),
            P(("dp", "hid")),
            P(("dp", "hid"), None),
            P(("dp", "hid"), None),
            P(("dp", "hid")),
            P(("dp", "hid")),
            P(None, "hid"),
            P("hid", None),
        ),
        check_vma=False,
    )
```

```python
import math

import jax
import jax.numpy as jnp
from jax import lax
from jax.experimental import pallas as pl
from jax.experimental.pallas import tpu as pltpu
from jax.sharding import PartitionSpec as P

D = 1536
HEADS = 12
HD = 128

EPS = 1e-05
GELU_C = 0.7978845608028654
GELU_A = 0.044715
BF16 = jnp.bfloat16
F32 = jnp.float32

ALL_ROWS = ("dp", "hid")
LAYER = ("hid", "gran")


def round_low(values):
    return lax.reduce_precision(values, 8, 7).astype(BF16)


def dot(left, right, contract=((1,), (0,))):
    return lax.dot_general(left, right, (contract, ((), ())), preferred_element_type=F32)


def dot_nt(left, right):
    return dot(left, right, ((1,), (1,)))


def dot_tn(left, right):
    return dot(left, right, ((0,), (0,)))


def norm_parts(values):
    centred = values - jnp.mean(values, axis=-1, keepdims=True)
    scale = lax.rsqrt(jnp.mean(centred * centred, axis=-1, keepdims=True) + EPS)
    return centred * scale, scale


def norm_back(dout, unit, scale, gain):
    inner = dout * gain
    return scale * (
        inner
        - jnp.mean(inner, axis=-1, keepdims=True)
        - unit * jnp.mean(inner * unit, axis=-1, keepdims=True)
    )


def gelu_both(values):
    square = values * values
    bent = jnp.tanh(GELU_C * values * (1.0 + GELU_A * square))
    half = 0.5 * (1.0 + bent)
    slope = half + 0.5 * values * (1.0 - bent * bent) * (GELU_C * (1.0 + 3.0 * GELU_A * square))
    return values * half, slope


def rotary_tables(length):
    half_dim = HD // 2
    freqs = 10000.0 ** (-(jnp.arange(half_dim, dtype=F32) * 2.0 / HD))
    angles = jnp.arange(length, dtype=F32)[:, None] * freqs[None, :]
    return jnp.cos(angles), jnp.sin(angles)


def turn(block, cosine, sine):
    lower, upper = block[:, : HD // 2], block[:, HD // 2 :]
    return jnp.concatenate([lower * cosine - upper * sine, upper * cosine + lower * sine], axis=1)


def turn_back(block, cosine, sine):
    return turn(block, cosine, -sine)


def after(value, *others):
    return lax.optimization_barrier((value,) + others)[0]


def swap_hid(value):
    return lax.ppermute(value, "hid", ((0, 1), (1, 0)))


def swap_near(value):
    return lax.ppermute(value, "gran", ((0, 1), (1, 0), (2, 3), (3, 2)))


def swap_far(value):
    return lax.ppermute(value, "gran", ((0, 2), (2, 0), (1, 3), (3, 1)))


def pick(index, options):
    chosen = options[-1]
    for k in range(len(options) - 2, -1, -1):
        chosen = jnp.where(index == k, options[k], chosen)
    return chosen


def split_sum(value, axis_swap, mine):
    keep = jnp.where(mine == 0, value[0], value[1])
    send = jnp.where(mine == 0, value[1], value[0])
    return keep.astype(F32) + axis_swap(round_low(send.astype(F32))).astype(F32)


def join(own, other, mine, axis=0):
    lower = jnp.where(mine == 0, own, other)
    upper = jnp.where(mine == 0, other, own)
    return jnp.concatenate([lower, upper], axis=axis)


def rows_of_line(own, dp_index):
    r1 = lax.ppermute(own, "dp", ((0, 1), (1, 2), (2, 3)))
    l1 = lax.ppermute(own, "dp", ((1, 0), (2, 1), (3, 2)))
    r2 = lax.ppermute(r1, "dp", ((1, 2), (2, 3)))
    l2 = lax.ppermute(l1, "dp", ((2, 1), (1, 0)))
    r3 = lax.ppermute(r2, "dp", ((2, 3),))
    l3 = lax.ppermute(l2, "dp", ((1, 0),))
    slots = [
        jnp.where(dp_index < 2, l1, r1),
        pick(dp_index, [l2, r1, l1, r2]),
        pick(dp_index, [l3, l2, r2, r3]),
    ]
    places = [
        pick(dp_index, [1, 2, 1, 2]),
        pick(dp_index, [2, 0, 3, 1]),
        pick(dp_index, [3, 3, 0, 0]),
    ]
    return slots, places


def gather_rows(own, dp_index, hid_index):
    slots, places = rows_of_line(own, dp_index)
    rows = own.shape[0]
    full = jnp.zeros((8 * rows,) + own.shape[1:], own.dtype)
    for block, place in zip([own] + slots, [dp_index] + places):
        other = swap_hid(block)
        start = (2 * place + hid_index) * rows
        full = lax.dynamic_update_slice_in_dim(full, block, start, axis=0)
        start = (2 * place + 1 - hid_index) * rows
        full = lax.dynamic_update_slice_in_dim(full, other, start, axis=0)
    return full


def gather_grans(own, gran_index, axis):
    core, side = gran_index % 2, gran_index // 2
    far = swap_far(own)
    both = jnp.stack([jnp.where(side == 0, own, far), jnp.where(side == 0, far, own)])
    near = swap_near(both)
    order = [jnp.where(core == 0, both[k // 2], near[k // 2]) if k % 2 == 0 else
             jnp.where(core == 0, near[k // 2], both[k // 2]) for k in range(4)]
    return jnp.concatenate(order, axis=axis)


def place_kernel(at_ref, own_ref, near_ref, far_ref, far_near_ref, *rest):
    out_ref = rest[-1]
    for k, ref in enumerate((own_ref, near_ref, far_ref, far_near_ref)):

        @pl.when(pl.program_id(0) == k)
        def _(ref=ref):
            out_ref[...] = ref[...].astype(F32)


def place_pieces(whole, shape, pieces, gran_index, where):
    block = pieces[0].shape
    order = jnp.stack([gran_index, gran_index ^ 1, gran_index ^ 2, gran_index ^ 3])
    still = pl.BlockSpec(block, lambda k, at: (0, 0))
    specs = [still] * 4
    operands = list(pieces)
    aliases = {}
    if whole is not None:
        specs.append(pl.BlockSpec(memory_space=pl.ANY))
        operands.append(whole)
        aliases = {5: 0}
    return pl.pallas_call(
        place_kernel,
        out_shape=jax.ShapeDtypeStruct(shape, F32),
        grid_spec=pltpu.PrefetchScalarGridSpec(
            num_scalar_prefetch=1,
            grid=(4,),
            in_specs=specs,
            out_specs=pl.BlockSpec(block, lambda k, at: where(at[k])),
        ),
        input_output_aliases=aliases,
        compiler_params=pltpu.CompilerParams(vmem_limit_bytes=32 * 1024 * 1024),
        cost_estimate=pl.CostEstimate(
            flops=0, bytes_accessed=4 * block[0] * block[1] * 6, transcendentals=0
        ),
    )(order.astype(jnp.int32), *operands)


def sum_lines(pieces, dp_index, lag=3):
    middle = (dp_index == 1) | (dp_index == 2)
    totals, done = [], []
    for t, piece in enumerate(pieces):
        own = round_low(piece)
        if t >= lag:
            own = after(own, totals[t - lag])
        if t >= 6:
            own = after(own, done[t - 6][3])
        inward = lax.ppermute(own, "dp", ((0, 1), (3, 2)))
        pair = round_low(own.astype(F32) + inward.astype(F32))
        other = lax.ppermute(pair, "dp", ((1, 2), (2, 1)))
        total = round_low(pair.astype(F32) + other.astype(F32))
        totals.append(total)
        outward = lax.ppermute(total, "dp", ((1, 0), (2, 3)))
        final = jnp.where(middle, total, outward)
        far = swap_far(final)
        done.append((final, swap_near(final), far, swap_near(far)))
    return done


def scatter_lines(blocks, dp_index):
    def block(index):
        return lax.dynamic_index_in_dim(blocks, jnp.clip(index, 0, 3), axis=0, keepdims=False)

    ends = block(dp_index)
    total = ends.astype(F32)
    for step_sign, hops in ((1, ((0, 1), (1, 2), (2, 3))), (-1, ((3, 2), (2, 1), (1, 0)))):
        carry = None
        for step in (1, 2, 3):
            index = dp_index + step_sign * (4 - step)
            payload = block(index)
            if carry is not None:
                payload = round_low(payload.astype(F32) + carry.astype(F32))
            carry = lax.ppermute(payload, "dp", hops)
        total = total + carry.astype(F32)
    return round_low(total)


def local(
    tokens,
    ln1_gain,
    ln1_bias,
    w_qkv,
    w_attn,
    ln2_gain,
    ln2_bias,
    w_in,
    w_out,
    cotangent,
    active_units,
):
    length = tokens.shape[0]
    grans = active_units.shape[0]
    hids = lax.axis_size("hid")
    gran_index = lax.axis_index("gran")
    dp_index = lax.axis_index("dp")
    hid_index = lax.axis_index("hid")
    heads = HEADS // grans
    part = heads * HD
    quarter = length // grans
    fast = hids == 2 and grans == 4 and lax.axis_size("dp") == 4
    core, side = gran_index % 2, gran_index // 2

    def head_columns(array, start):
        return lax.dynamic_slice_in_dim(array, start + gran_index * part, part, axis=1)

    vectors = jnp.stack([ln1_gain, ln1_bias, ln2_gain, ln2_bias], axis=1)
    qkv_rows = jnp.concatenate(
        [head_columns(w_qkv, 0), head_columns(w_qkv, D), head_columns(w_qkv, 2 * D), vectors], axis=1
    )
    attn_own = head_columns(w_attn, 0)
    if fast:
        qkv_all = gather_rows(qkv_rows, dp_index, hid_index)
        attn_own = after(attn_own, qkv_all)
        attn_cols = gather_rows(attn_own, dp_index, hid_index)
        attn_full = gather_grans(attn_cols, gran_index, axis=1)
    else:
        qkv_all = lax.all_gather(qkv_rows, ALL_ROWS, axis=0, tiled=True)
        attn_cols = lax.all_gather(attn_own, ALL_ROWS, axis=0, tiled=True)
        attn_full = lax.all_gather(attn_cols, "gran", axis=1, tiled=True)
    qkv_cols = qkv_all[:, : 3 * part]
    gains = qkv_all[:, 3 * part :].astype(F32).T
    gain_one, bias_one, gain_two, bias_two = (gains[i : i + 1] for i in range(4))

    out_grad = cotangent[0]
    slab = w_in.shape[1]
    block = slab // grans
    first_unit = hid_index * slab + gran_index * block
    total_units = slab * hids
    level = jnp.int32(0)
    for step in range(1, grans):
        bound = total_units * 2 ** (step - 1) // 8
        level = level + (first_unit >= bound).astype(jnp.int32)
    border = jnp.sum(jnp.where(jnp.arange(grans) == level, active_units, 0))
    low_unit = (first_unit + jnp.arange(block, dtype=jnp.int32)) < border
    if fast:
        mine = lax.dynamic_slice_in_dim(tokens, gran_index * quarter, quarter, axis=0)
        across = gather_grans(swap_hid(mine), gran_index, axis=0)
        all_tokens = join(tokens, across, hid_index)

        def mixed(flag, value):
            return value.astype(F32) * flag.astype(F32)

        far_hid = hid_index == 1
        both = join(out_grad, swap_hid(after(out_grad, qkv_all)), hid_index)
        mate = swap_near(both)
        even, odd = jnp.where(core == 0, both, mate), jnp.where(core == 0, mate, both)
        upper = jnp.where(far_hid, odd, round_low(even.astype(F32) + odd.astype(F32)))
        half = lax.dynamic_slice_in_dim(upper, core * length, length, axis=0)
        half = lax.ppermute(half, "gran", ((2, 0), (3, 1)))
        upper = join(half, swap_near(half), core)
        cot_lo = (
            mixed(~far_hid & ((side == 1) | (core == 0)), even)
            + mixed(~far_hid | (side == 1), odd)
            + mixed(side == 0, upper)
        ).astype(BF16)
        cot_hi = (
            mixed((side == 1) | (~far_hid & (core == 0)), odd) + mixed(side == 0, upper)
        ).astype(BF16)
    else:
        all_tokens = lax.all_gather(tokens, "hid", axis=0, tiled=True)
        all_cot = lax.all_gather(out_grad, LAYER, axis=0).reshape(hids, grans, length, D)

        def sum_from(start):
            keep = (jnp.arange(grans) >= start).astype(F32)[None, :, None, None]
            return jnp.sum(all_cot.astype(F32) * keep, axis=1).reshape(-1, D).astype(BF16)

        cot_lo, cot_hi = sum_from(level), sum_from(jnp.minimum(level + 1, grans - 1))
    cot_own = lax.psum_scatter(out_grad, "gran", scatter_dimension=0, tiled=True).astype(F32)

    x_rows = tokens.astype(F32)
    unit_one, scale_one = norm_parts(x_rows)
    normed_one = (unit_one * gain_one + bias_one).astype(BF16)
    qkv = dot(normed_one, qkv_cols)
    cosine, sine = rotary_tables(length)
    causal = jnp.arange(length)[:, None] >= jnp.arange(length)[None, :]
    kept, attended = [], []
    for head in range(heads):
        at = head * HD
        query = turn(qkv[:, at : at + HD], cosine, sine).astype(BF16)
        key = turn(qkv[:, part + at : part + at + HD], cosine, sine).astype(BF16)
        value = qkv[:, 2 * part + at : 2 * part + at + HD].astype(BF16)
        scores = jnp.where(causal, dot_nt(query, key) / math.sqrt(HD), -1000000000.0)
        exponent = jnp.exp(scores - jnp.max(scores, axis=-1, keepdims=True))
        probs = exponent / jnp.sum(exponent, axis=-1, keepdims=True)
        probs_low = probs.astype(BF16)
        attended.append(dot(probs_low, value).astype(BF16))
        kept.append((query, key, value, probs))
    attended = jnp.concatenate(attended, axis=1)
    if fast:
        across = swap_hid(attended)
        both = join(attended, across, hid_index)
        all_attended = gather_grans(both, gran_index, axis=1)
    else:
        everyone = lax.all_gather(attended, LAYER, axis=0).reshape(hids, grans, length, part)
        all_attended = everyone.transpose(0, 2, 1, 3).reshape(hids * length, D)
    hidden = all_tokens.astype(F32) + dot(all_attended, attn_full)
    unit_two, scale_two = norm_parts(hidden)
    normed_two = (unit_two * gain_two + bias_two).astype(BF16)

    w_in_block = lax.dynamic_slice_in_dim(w_in, gran_index * block, block, axis=1)
    w_out_block = lax.dynamic_slice_in_dim(w_out, gran_index * block, block, axis=0)
    pre = dot(normed_two, w_in_block)
    act, slope = gelu_both(pre)
    act = act.astype(BF16)
    dact = jnp.where(low_unit[None], dot_nt(cot_lo, w_out_block), dot_nt(cot_hi, w_out_block))
    dpre = (dact * slope).astype(BF16)
    dnormed_two = dot_nt(dpre, w_in_block).astype(BF16)

    pieces = 4
    out_pieces = []
    for k in range(pieces):
        cut = slice(k * block // pieces, (k + 1) * block // pieces)
        out_pieces.append(
            jnp.where(low_unit[cut, None], dot_tn(act[:, cut], cot_lo), dot_tn(act[:, cut], cot_hi))
        )
    in_pieces = []
    for k in range(pieces):
        cut = slice(k * D // pieces, (k + 1) * D // pieces)
        in_pieces.append(dot_tn(normed_two[:, cut], dpre))
    if fast:
        sums = sum_lines(out_pieces + in_pieces, dp_index)
        w_out_grad = w_in_grad = None
        for k in range(pieces):
            w_out_grad = place_pieces(
                w_out_grad, w_out.shape, sums[k], gran_index, lambda at, k=k: (at * pieces + k, 0)
            )
        for k in range(pieces):
            w_in_grad = place_pieces(
                w_in_grad, w_in.shape, sums[pieces + k], gran_index, lambda at, k=k: (k, at)
            )
    else:
        out_term = lax.psum(jnp.concatenate(out_pieces, axis=0).astype(BF16), "dp")
        in_term = lax.psum(jnp.concatenate(in_pieces, axis=0).astype(BF16), "dp")
        w_out_grad = lax.all_gather(out_term, "gran", axis=0, tiled=True).astype(F32)
        w_in_grad = lax.all_gather(in_term, "gran", axis=1, tiled=True).astype(F32)

    if fast:
        blocks = dnormed_two.reshape(2, 2, 2, quarter, D).transpose(2, 1, 0, 3, 4)
        blocks = split_sum(blocks, swap_near, core)
        blocks = split_sum(blocks, swap_far, side)
        dnormed_two = split_sum(blocks, swap_hid, hid_index)
    else:
        dnormed_two = lax.psum_scatter(
            dnormed_two, LAYER, scatter_dimension=0, tiled=True
        ).astype(F32)
    row = hid_index * length + gran_index * quarter

    def own_rows(array):
        return lax.dynamic_slice_in_dim(array, row, quarter, axis=0)

    unit_two, scale_two = own_rows(unit_two), own_rows(scale_two)
    dhidden = cot_own + norm_back(dnormed_two, unit_two, scale_two, gain_two)
    gain_two_term = jnp.sum(dnormed_two * unit_two, axis=0)
    bias_two_term = jnp.sum(dnormed_two, axis=0)
    if fast:
        dbranch = gather_grans(dhidden.astype(BF16), gran_index, axis=0)
    else:
        dbranch = lax.all_gather(dhidden.astype(BF16), "gran", axis=0, tiled=True)

    attn_rows = lax.dynamic_slice_in_dim(attn_full, gran_index * part, part, axis=0)
    dattended = dot_nt(dbranch, attn_rows).astype(BF16)
    own_attended = lax.dynamic_slice_in_dim(all_attended, hid_index * length, length, axis=0)
    dbranch_cols = lax.dynamic_slice_in_dim(dbranch, gran_index * part, part, axis=1)
    attn_term = dot_tn(own_attended, dbranch_cols)
    dqueries, dkeys, dvalues = [], [], []
    for head in range(heads):
        query, key, value, probs = kept[head]
        dvec = dattended[:, head * HD : (head + 1) * HD]
        dprobs = dot_nt(dvec, value)
        inner = jnp.sum(probs * dprobs, axis=-1, keepdims=True)
        dscores = (probs * (dprobs - inner)).astype(BF16)
        dqueries.append(turn_back(dot(dscores, key) / math.sqrt(HD), cosine, sine).astype(BF16))
        dkeys.append(turn_back(dot_tn(dscores, query) / math.sqrt(HD), cosine, sine).astype(BF16))
        dvalues.append(dot_tn(probs.astype(BF16), dvec).astype(BF16))
    dqkv = jnp.concatenate(dqueries + dkeys + dvalues, axis=1)
    qkv_term = dot_tn(normed_one, dqkv)
    dnormed_one = dot_nt(dqkv, qkv_cols)
    if fast:
        blocks = dnormed_one.reshape(2, 2, quarter, D).transpose(1, 0, 2, 3)
        blocks = split_sum(blocks, swap_near, core)
        dnormed_one = split_sum(blocks, swap_far, side)
    else:
        dnormed_one = lax.psum_scatter(
            dnormed_one.astype(BF16), "gran", scatter_dimension=0, tiled=True
        ).astype(F32)

    unit_one = lax.dynamic_slice_in_dim(unit_one, gran_index * quarter, quarter, axis=0)
    scale_one = lax.dynamic_slice_in_dim(scale_one, gran_index * quarter, quarter, axis=0)
    dx = dhidden + norm_back(dnormed_one, unit_one, scale_one, gain_one)
    gain_one_term = jnp.sum(dnormed_one * unit_one, axis=0)
    bias_one_term = jnp.sum(dnormed_one, axis=0)
    x_grad = lax.all_gather(dx.astype(BF16), "gran", axis=0, tiled=True).astype(F32)

    vector_terms = jnp.stack([gain_one_term, bias_one_term, gain_two_term, bias_two_term], axis=1)
    terms = jnp.concatenate([qkv_term, attn_term, vector_terms], axis=1).astype(BF16)
    if fast:
        blocks = terms.reshape(4, 2, D // 8, -1).transpose(1, 0, 2, 3)
        blocks = round_low(split_sum(blocks, swap_hid, hid_index))
        terms = scatter_lines(blocks, dp_index)
    else:
        terms = lax.psum_scatter(terms, ALL_ROWS, scatter_dimension=0, tiled=True)
    terms = lax.all_gather(terms, "gran", axis=0).astype(F32)

    def grads_of(start):
        return [terms[k, :, start : start + part] for k in range(grans)]

    qkv_grad = jnp.concatenate(grads_of(0) + grads_of(part) + grads_of(2 * part), axis=1)
    attn_grad = jnp.concatenate(grads_of(3 * part), axis=1)
    vector_grads = jnp.sum(terms[:, :, 4 * part :], axis=0).T

    act_low = jnp.where(low_unit[None], act, 0)
    part_low = dot(act_low, w_out_block)
    part_all = part_low + dot(act - act_low, w_out_block)
    if fast:
        low, full = round_low(part_low), round_low(part_all)
        near = swap_near(jnp.where(core == 0, full, low)).astype(F32)
        below = lax.ppermute(round_low(near + full.astype(F32)), "gran", ((1, 3),))
        below = below + lax.ppermute(below, "gran", ((3, 2),))
        share = jnp.where((core == 1) & (side == 1), full, low).astype(F32)
        share = share + jnp.where(gran_index == 0, 0.0, near) + below.astype(F32)
        share = jnp.where((hid_index == 1) & (gran_index < 3), 0.0, share)
        ffn = split_sum(share.reshape(2, length, D), swap_hid, hid_index)
    else:
        shares = []
        for k in range(grans):
            share = jnp.where(level < k, part_all, jnp.where(level == k, part_low, 0.0))
            shares.append(share.astype(BF16).reshape(hids, length, D))
        shares = jnp.stack(shares, axis=1).reshape(hids * grans * length, D)
        ffn = lax.psum_scatter(shares, LAYER, scatter_dimension=0, tiled=True).astype(F32)
    own_hidden = lax.dynamic_slice_in_dim(hidden, hid_index * length, length, axis=0)
    outputs = (own_hidden + ffn).astype(BF16)[None]

    return (
        outputs,
        x_grad,
        vector_grads[0],
        vector_grads[1],
        qkv_grad,
        attn_grad,
        vector_grads[2],
        vector_grads[3],
        w_in_grad,
        w_out_grad,
    )


def solution(mesh):
    return jax.shard_map(
        local,
        mesh=mesh,
        in_specs=(
            P(("dp", "hid"), None),
            P(("dp", "hid")),
            P(("dp", "hid")),
            P(("dp", "hid"), None),
            P(("dp", "hid"), None),
            P(("dp", "hid")),
            P(("dp", "hid")),
            P(None, "hid"),
            P("hid", None),
            P("gran", ("dp", "hid"), None),
            P(),
        ),
        out_specs=(
            P("gran", ("dp", "hid"), None),
            P(("dp", "hid"), None),
            P(("dp", "hid")),
            P(("dp", "hid")),
            P(("dp", "hid"), None),
            P(("dp", "hid"), None),
            P(("dp", "hid")),
            P(("dp", "hid")),
            P(None, "hid"),
            P("hid", None),
        ),
        check_vma=False,
    )
```

```python
import functools
import math

import jax
import jax.numpy as jnp
from jax import lax
from jax.experimental import pallas as pl
from jax.experimental.pallas import tpu as pltpu
from jax.sharding import PartitionSpec as P

D = 1536
HEADS = 12
HD = 128

EPS = 1e-05
GELU_C = 0.7978845608028654
GELU_A = 0.044715
BF16 = jnp.bfloat16
F32 = jnp.float32

ALL_ROWS = ("dp", "hid")
LAYER = ("hid", "gran")


def round_low(values):
    return lax.reduce_precision(values, 8, 7).astype(BF16)


def dot(left, right, contract=((1,), (0,))):
    return lax.dot_general(left, right, (contract, ((), ())), preferred_element_type=F32)


def dot_nt(left, right):
    return dot(left, right, ((1,), (1,)))


def dot_tn(left, right):
    return dot(left, right, ((0,), (0,)))


def norm_parts(values):
    centred = values - jnp.mean(values, axis=-1, keepdims=True)
    scale = lax.rsqrt(jnp.mean(centred * centred, axis=-1, keepdims=True) + EPS)
    return centred * scale, scale


def norm_back(dout, unit, scale, gain):
    inner = dout * gain
    return scale * (
        inner
        - jnp.mean(inner, axis=-1, keepdims=True)
        - unit * jnp.mean(inner * unit, axis=-1, keepdims=True)
    )


def gelu_both(values):
    square = values * values
    bent = jnp.tanh(GELU_C * values * (1.0 + GELU_A * square))
    half = 0.5 * (1.0 + bent)
    slope = half + 0.5 * values * (1.0 - bent * bent) * (GELU_C * (1.0 + 3.0 * GELU_A * square))
    return values * half, slope


def rotary_tables(length):
    half_dim = HD // 2
    freqs = 10000.0 ** (-(jnp.arange(half_dim, dtype=F32) * 2.0 / HD))
    angles = jnp.arange(length, dtype=F32)[:, None] * freqs[None, :]
    return jnp.cos(angles), jnp.sin(angles)


def turn(block, cosine, sine):
    lower, upper = block[:, : HD // 2], block[:, HD // 2 :]
    return jnp.concatenate([lower * cosine - upper * sine, upper * cosine + lower * sine], axis=1)


def turn_back(block, cosine, sine):
    return turn(block, cosine, -sine)


def after(value, *others):
    return lax.optimization_barrier((value,) + others)[0]


def swap_hid(value):
    return lax.ppermute(value, "hid", ((0, 1), (1, 0)))


def swap_near(value):
    return lax.ppermute(value, "gran", ((0, 1), (1, 0), (2, 3), (3, 2)))


def swap_far(value):
    return lax.ppermute(value, "gran", ((0, 2), (2, 0), (1, 3), (3, 1)))


def share(own):
    far = swap_far(own)
    return own, swap_near(own), far, swap_near(far)


def pick(index, options):
    chosen = options[-1]
    for k in range(len(options) - 2, -1, -1):
        chosen = jnp.where(index == k, options[k], chosen)
    return chosen


def rows_of_line(own, dp_index):
    end = (dp_index == 0) | (dp_index == 3)
    one = lax.ppermute(own, "dp", ((0, 1), (1, 0), (2, 3), (3, 2)))
    inner = lax.ppermute(own, "dp", ((1, 2), (2, 1)))
    across = lax.ppermute(one, "dp", ((1, 2), (2, 1)))
    outer = lax.ppermute(inner, "dp", ((1, 0), (2, 3)))
    last = lax.ppermute(across, "dp", ((1, 0), (2, 3)))
    slots = [one, jnp.where(end, outer, inner), jnp.where(end, last, across)]
    places = [[1, 0, 3, 2], [2, 2, 1, 1], [3, 3, 0, 0]]
    return slots, [pick(dp_index, [jnp.int32(p) for p in place]) for place in places]


def params(vmem_mib=56):
    return pltpu.CompilerParams(vmem_limit_bytes=vmem_mib * 1024 * 1024)


def cost(flops, moved):
    return pl.CostEstimate(flops=flops, bytes_accessed=moved, transcendentals=0)


def whole_spec(shape):
    return pl.BlockSpec(shape, lambda *_: (0,) * len(shape))


def once_spec(shape):
    return pl.BlockSpec(shape, lambda *_: (0,) * len(shape), pipeline_mode=pl.Buffered(1))


def place_kernel(count, at_ref, *refs):
    out_ref = refs[-1]
    for k in range(count):

        @pl.when(pl.program_id(0) == k)
        def _(k=k):
            out_ref[...] = refs[k][...].astype(out_ref.dtype)


def place(pieces, at, shape, dtype, where, whole=None, parts=1):
    count = len(pieces)
    rows, columns = pieces[0].shape
    block = (rows, columns // parts)
    specs = [pl.BlockSpec(block, lambda k, t, at: (0, t))] * count
    operands = list(pieces)
    aliases = {}
    if whole is not None:
        specs.append(pl.BlockSpec(memory_space=pl.ANY))
        operands.append(whole)
        aliases = {count + 1: 0}
    size = rows * columns * count * (2 + jnp.dtype(dtype).itemsize)
    return pl.pallas_call(
        functools.partial(place_kernel, count),
        out_shape=jax.ShapeDtypeStruct(shape, dtype),
        grid_spec=pltpu.PrefetchScalarGridSpec(
            num_scalar_prefetch=1,
            grid=(count, parts),
            in_specs=specs,
            out_specs=pl.BlockSpec(block, lambda k, t, at: where(at[k], t)),
        ),
        input_output_aliases=aliases,
        compiler_params=params(40),
        cost_estimate=cost(0, size),
    )(jnp.stack(at).astype(jnp.int32), *operands)


def rotate(block, cos_ref, sin_ref, sign):
    return block * cos_ref[...] + pltpu.roll(block, HD // 2, 1) * (sign * sin_ref[...])


def probs_of(query, key, first_row):
    scores = dot_nt(query, key) * (1.0 / math.sqrt(HD))
    rows = first_row + lax.broadcasted_iota(jnp.int32, scores.shape, 0)
    scores = jnp.where(rows >= lax.broadcasted_iota(jnp.int32, scores.shape, 1), scores, -1e9)
    exponent = jnp.exp(scores - jnp.max(scores, axis=-1, keepdims=True))
    return exponent / jnp.sum(exponent, axis=-1, keepdims=True)


def attend_kernel(x_ref, gain_ref, bias_ref, w_ref, cos_ref, sin_ref, n1_ref, qkv_ref, att_ref):
    length, part = att_ref.shape
    unit, _ = norm_parts(x_ref[...].astype(F32))
    normed = (unit * gain_ref[...] + bias_ref[...]).astype(BF16)
    n1_ref[...] = normed
    for kind in range(3):
        product = dot(normed, w_ref[:, kind * part : (kind + 1) * part])
        for head in range(part // HD):
            block = product[:, head * HD : (head + 1) * HD]
            if kind < 2:
                block = rotate(block, cos_ref, sin_ref, 1.0)
            start = kind * part + head * HD
            qkv_ref[:, start : start + HD] = block.astype(BF16)
    half = length // 2
    for head in range(part // HD):
        cut = slice(head * HD, (head + 1) * HD)
        for row in range(2):
            rows, seen = slice(row * half, (row + 1) * half), slice(0, (row + 1) * half)
            query = qkv_ref[rows, cut]
            key = qkv_ref[seen, part + head * HD : part + (head + 1) * HD]
            value = qkv_ref[seen, 2 * part + head * HD : 2 * part + (head + 1) * HD]
            probs = probs_of(query, key, row * half).astype(BF16)
            att_ref[rows, cut] = dot(probs, value).astype(BF16)


def attend(tokens, gain, bias, weights, cosine, sine, part):
    length = tokens.shape[0]
    return pl.pallas_call(
        attend_kernel,
        out_shape=[
            jax.ShapeDtypeStruct((length, D), BF16),
            jax.ShapeDtypeStruct((length, 3 * part), BF16),
            jax.ShapeDtypeStruct((length, part), BF16),
        ],
        compiler_params=params(),
        cost_estimate=cost(2 * length * D * 3 * part * 2, 10_000_000),
    )(tokens, gain, bias, weights, cosine, sine)


def hidden_kernel(keep, at_ref, a0, a1, a2, a3, w_ref, x_ref, gain_ref, bias_ref, *rest):
    out_refs, all_ref = rest[:-1], rest[-1]
    part = a0.shape[1]
    for k, ref in enumerate((a0, a1, a2, a3)):
        all_ref[:, pl.ds(pl.multiple_of(at_ref[k] * part, HD), part)] = ref[...]
    hidden = x_ref[...].astype(F32) + dot(all_ref[...], w_ref[...])
    unit, _ = norm_parts(hidden)
    out_refs[0][...] = (unit * gain_ref[...] + bias_ref[...]).astype(BF16)
    if keep:
        out_refs[1][...] = hidden


def hidden_and_norm(pieces, order, w_attn, tokens, gain, bias, keep):
    length = tokens.shape[0]
    rows, part = length // 2, pieces[0].shape[1]
    by_row = lambda columns: pl.BlockSpec((rows, columns), lambda i, at: (i, 0))
    types = [BF16, F32] if keep else [BF16]
    return pl.pallas_call(
        functools.partial(hidden_kernel, keep),
        out_shape=[jax.ShapeDtypeStruct((length, D), kind) for kind in types],
        grid_spec=pltpu.PrefetchScalarGridSpec(
            num_scalar_prefetch=1,
            grid=(2,),
            in_specs=[by_row(part)] * 4
            + [once_spec((D, D)), by_row(D), once_spec((1, D)), once_spec((1, D))],
            out_specs=[by_row(D)] * len(types),
            scratch_shapes=[pltpu.VMEM((rows, D), BF16)],
        ),
        compiler_params=params(),
        cost_estimate=cost(2 * length * D * D, 10_000_000),
    )(order, *pieces, w_attn, tokens, gain, bias)


UNITS = 256


def by_border(at_ref, low, high, mixed):
    border = at_ref[1] - pl.program_id(0) * UNITS
    pl.when(border >= UNITS)(low)
    pl.when(border <= 0)(high)
    pl.when((border > 0) & (border < UNITS))(mixed)


def up_kernel(at_ref, n_own, n_oth, s_own, s_oth, w_ref, act_ref, slope_ref, *out_refs):
    length = n_own.shape[0]
    for k, ref in enumerate((n_own, n_oth)):
        act, slope = gelu_both(dot(ref[...], w_ref[...]))
        act_ref[k * length : (k + 1) * length, :] = act.astype(BF16)
        slope_ref[k * length : (k + 1) * length, :] = slope

    def term(columns, which):
        return dot_tn(act_ref[:length, columns], s_own[which]) + dot_tn(
            act_ref[length:, columns], s_oth[which]
        )

    for k, ref in enumerate(out_refs):

        @pl.when(pl.program_id(0) == k)
        def _(ref=ref):
            def plain(which):
                def run():
                    ref[...] = term(slice(0, UNITS), which).astype(BF16)

                return run

            def mixed():
                ref[: UNITS // 2, :] = term(slice(0, UNITS // 2), 0).astype(BF16)
                ref[UNITS // 2 :, :] = term(slice(UNITS // 2, UNITS), 1).astype(BF16)

            by_border(at_ref, plain(0), plain(1), mixed)


def feed_up(at, n_own, n_oth, s_own, s_oth, w_in, block):
    length = n_own.shape[0]
    tiles = block // UNITS
    return pl.pallas_call(
        up_kernel,
        out_shape=[
            jax.ShapeDtypeStruct((2 * length, block), BF16),
            jax.ShapeDtypeStruct((2 * length, block), F32),
        ]
        + [jax.ShapeDtypeStruct((UNITS, D), BF16)] * tiles,
        grid_spec=pltpu.PrefetchScalarGridSpec(
            num_scalar_prefetch=1,
            grid=(tiles,),
            in_specs=[once_spec((length, D))] * 2
            + [once_spec((2, length, D))] * 2
            + [pl.BlockSpec((D, UNITS), lambda i, at: (0, at[0] * tiles + i))],
            out_specs=[pl.BlockSpec((2 * length, UNITS), lambda i, at: (0, i))] * 2
            + [whole_spec((UNITS, D))] * tiles,
        ),
        compiler_params=params(),
        cost_estimate=cost(8 * length * D * block, 20_000_000),
    )(at, n_own, n_oth, s_own, s_oth, w_in)


def down_kernel(at_ref, n_own, n_oth, s_own, s_oth, slope_ref, w_in, w_out, *rest):
    in_refs, (keep_ref, send_ref, total, dact) = rest[:-4], rest[-4:]
    length = n_own.shape[0]
    half = length // 2
    step = pl.program_id(0)

    def fill(columns, which):
        for k, ref in enumerate((s_own, s_oth)):
            dact[k * length : (k + 1) * length, columns] = dot_nt(ref[which], w_out[columns, :])

    def mixed():
        fill(slice(0, UNITS // 2), 0)
        fill(slice(UNITS // 2, UNITS), 1)

    by_border(
        at_ref, lambda: fill(slice(0, UNITS), 0), lambda: fill(slice(0, UNITS), 1), mixed
    )
    dpre = (dact[...] * slope_ref[...]).astype(BF16)
    term = dot_tn(n_own[...], dpre[:length]) + dot_tn(n_oth[...], dpre[length:])
    for k, ref in enumerate(in_refs):

        @pl.when(step == k)
        def _(ref=ref):
            ref[...] = term.astype(BF16)

    product = dot_nt(dpre, w_in[...])

    @pl.when(step == 0)
    def _():
        total[...] = product

    @pl.when(step > 0)
    def _():
        total[...] += product

    @pl.when(step == len(in_refs) - 1)
    def _():
        core = at_ref[2]
        for k in range(2):
            mine = pl.multiple_of(k * length + core * half, half)
            theirs = pl.multiple_of(k * length + (1 - core) * half, half)
            keep_ref[k] = total[pl.ds(mine, half), :]
            send_ref[k] = total[pl.ds(theirs, half), :].astype(BF16)


def feed_down(at, n_own, n_oth, s_own, s_oth, slope, w_in, w_out, block):
    length = n_own.shape[0]
    tiles = block // UNITS
    return pl.pallas_call(
        down_kernel,
        out_shape=[jax.ShapeDtypeStruct((D, UNITS), BF16)] * tiles
        + [
            jax.ShapeDtypeStruct((2, length // 2, D), F32),
            jax.ShapeDtypeStruct((2, length // 2, D), BF16),
        ],
        grid_spec=pltpu.PrefetchScalarGridSpec(
            num_scalar_prefetch=1,
            grid=(tiles,),
            in_specs=[once_spec((length, D))] * 2
            + [once_spec((2, length, D))] * 2
            + [
                pl.BlockSpec((2 * length, UNITS), lambda i, at: (0, i)),
                pl.BlockSpec((D, UNITS), lambda i, at: (0, at[0] * tiles + i)),
                pl.BlockSpec((UNITS, D), lambda i, at: (at[0] * tiles + i, 0)),
            ],
            out_specs=[once_spec((D, UNITS))] * tiles + [once_spec((2, length // 2, D))] * 2,
            scratch_shapes=[
                pltpu.VMEM((2 * length, D), F32),
                pltpu.VMEM((2 * length, UNITS), F32),
            ],
        ),
        compiler_params=params(60),
        cost_estimate=cost(12 * length * D * block, 30_000_000),
    )(at, n_own, n_oth, s_own, s_oth, slope, w_in, w_out)


def out_kernel(at_ref, act_ref, w_ref, low_ref, full_ref, low, high):
    step = pl.program_id(0)

    @pl.when(step == 0)
    def _():
        low[...] = jnp.zeros_like(low)
        high[...] = jnp.zeros_like(high)

    def add(into, cut):
        into[...] += dot(act_ref[:, cut], w_ref[cut, :])

    def mixed():
        add(low, slice(0, UNITS // 2))
        add(high, slice(UNITS // 2, UNITS))

    by_border(at_ref, lambda: add(low, slice(0, UNITS)), lambda: add(high, slice(0, UNITS)), mixed)

    @pl.when(step == pl.num_programs(0) - 1)
    def _():
        low_ref[...] = low[...].astype(BF16)
        full_ref[...] = (low[...] + high[...]).astype(BF16)


def feed_out(at, act, w_out, block):
    rows = act.shape[0]
    tiles = block // UNITS
    return pl.pallas_call(
        out_kernel,
        out_shape=[jax.ShapeDtypeStruct((rows, D), BF16)] * 2,
        grid_spec=pltpu.PrefetchScalarGridSpec(
            num_scalar_prefetch=1,
            grid=(tiles,),
            in_specs=[
                pl.BlockSpec((rows, UNITS), lambda i, at: (0, i)),
                pl.BlockSpec((UNITS, D), lambda i, at: (at[0] * tiles + i, 0)),
            ],
            out_specs=[once_spec((rows, D))] * 2,
            scratch_shapes=[pltpu.VMEM((rows, D), F32)] * 2,
        ),
        compiler_params=params(),
        cost_estimate=cost(2 * rows * D * block, 10_000_000),
    )(at, act, w_out)


def norm_back_kernel(dout_ref, x_ref, rest_ref, gain_ref, d_ref, low_ref, gain_out, bias_out):
    unit, scale = norm_parts(x_ref[...].astype(F32))
    dout = dout_ref[...]
    total = rest_ref[...] + norm_back(dout, unit, scale, gain_ref[...])
    d_ref[...] = total
    low_ref[...] = total.astype(BF16)
    gain_out[...] = jnp.sum(dout * unit, axis=0, keepdims=True)
    bias_out[...] = jnp.sum(dout, axis=0, keepdims=True)


def norm_backward(dout, rows, rest, gain):
    return pl.pallas_call(
        norm_back_kernel,
        out_shape=[
            jax.ShapeDtypeStruct(dout.shape, F32),
            jax.ShapeDtypeStruct(dout.shape, BF16),
            jax.ShapeDtypeStruct((1, D), F32),
            jax.ShapeDtypeStruct((1, D), F32),
        ],
        compiler_params=params(32),
        cost_estimate=cost(0, 4_000_000),
    )(dout, rows, rest, gain)


def attend_back_kernel(
    at_ref, b0, b1, b2, b3, a0, a1, a2, a3, w_ref, qkv_ref, n1_ref, cos_ref, sin_ref,
    dqkv_ref, keep_ref, send_ref, branch, block,
):
    length, part = a0.shape
    quarter = b0.shape[0]
    hid, gran = at_ref[8], at_ref[0]
    for k, ref in enumerate((b0, b1, b2, b3)):
        branch[pl.ds(pl.multiple_of(at_ref[4 + k] * quarter, quarter), quarter), :] = ref[...]
    dattended = dot_nt(branch[...], w_ref[...]).astype(BF16)
    half = length // 2
    scale = 1.0 / math.sqrt(HD)
    for head in range(part // HD):
        q_cut = slice(head * HD, (head + 1) * HD)
        k_cut = slice(part + head * HD, part + (head + 1) * HD)
        v_cut = slice(2 * part + head * HD, 2 * part + (head + 1) * HD)
        sums = {}
        for row in range(2):
            rows, seen = slice(row * half, (row + 1) * half), slice(0, (row + 1) * half)
            query, key, value = qkv_ref[rows, q_cut], qkv_ref[seen, k_cut], qkv_ref[seen, v_cut]
            probs = probs_of(query, key, row * half)
            dvec = dattended[rows, q_cut]
            dprobs = dot_nt(dvec, value)
            inner = jnp.sum(probs * dprobs, axis=-1, keepdims=True)
            dscores = (probs * (dprobs - inner)).astype(BF16)
            dquery = dot(dscores, key) * scale
            dquery = dquery * cos_ref[rows, :] - pltpu.roll(dquery, HD // 2, 1) * sin_ref[rows, :]
            dqkv_ref[rows, q_cut] = dquery.astype(BF16)
            sums[row] = dot_tn(dscores, query) * scale, dot_tn(probs.astype(BF16), dvec)
        for row in range(2):
            rows = slice(row * half, (row + 1) * half)
            dkey, dvalue = (sums[1][i][rows] + (sums[0][i] if row == 0 else 0.0) for i in range(2))
            dkey = dkey * cos_ref[rows, :] - pltpu.roll(dkey, HD // 2, 1) * sin_ref[rows, :]
            dqkv_ref[rows, k_cut] = dkey.astype(BF16)
            dqkv_ref[rows, v_cut] = dvalue.astype(BF16)
    piece = keep_ref.shape[1]
    mine = pl.multiple_of(hid * piece, 16)
    theirs = pl.multiple_of((1 - hid) * piece, 16)
    for line in range(4):
        rows = slice(line * 2 * piece, (line + 1) * 2 * piece)
        block[...] = dot_tn(n1_ref[:, rows], dqkv_ref[...])
        keep_ref[line, :, : 3 * part] = block[pl.ds(mine, piece), :].astype(BF16)
        send_ref[line, :, : 3 * part] = block[pl.ds(theirs, piece), :].astype(BF16)
    own_columns = branch[:, pl.ds(pl.multiple_of(gran * part, HD), part)]
    for k, ref in enumerate((a0, a1, a2, a3)):
        block[:, :part] = dot_tn(ref[...], own_columns)
        keep_ref[at_ref[k], :, 3 * part :] = block[pl.ds(mine, piece), :part].astype(BF16)
        send_ref[at_ref[k], :, 3 * part :] = block[pl.ds(theirs, piece), :part].astype(BF16)


def attend_back(at, branches, attended, w_attn, qkv, n1, cosine, sine):
    length, part = attended[0].shape
    piece = D // 8
    quarter = branches[0].shape[0]
    out = jax.ShapeDtypeStruct((4, piece, 4 * part), BF16)
    return pl.pallas_call(
        attend_back_kernel,
        out_shape=[jax.ShapeDtypeStruct((length, 3 * part), BF16), out, out],
        grid_spec=pltpu.PrefetchScalarGridSpec(
            num_scalar_prefetch=1,
            grid=(1,),
            in_specs=[once_spec((quarter, D))] * 4
            + [once_spec((length, part))] * 4
            + [
                pl.BlockSpec((part, D), lambda i, at: (at[0], 0)),
                once_spec((length, 3 * part)),
                once_spec((length, D)),
                once_spec((length, HD)),
                once_spec((length, HD)),
            ],
            out_specs=[once_spec((length, 3 * part))] + [once_spec((4, piece, 4 * part))] * 2,
            scratch_shapes=[
                pltpu.VMEM((length, D), BF16),
                pltpu.VMEM((2 * piece, 3 * part), F32),
            ],
        ),
        compiler_params=params(),
        cost_estimate=cost(12 * length * D * part, 20_000_000),
    )(at, *branches, *attended, w_attn, qkv, n1, cosine, sine)


def normed_back_kernel(at_ref, dqkv_ref, w_ref, keep_ref, send_ref, total):
    half = keep_ref.shape[0]
    total[...] = dot_nt(dqkv_ref[...], w_ref[:, : dqkv_ref.shape[1]])
    core = at_ref[2]
    keep_ref[...] = total[pl.ds(pl.multiple_of(core * half, half), half), :]
    send_ref[...] = total[pl.ds(pl.multiple_of((1 - core) * half, half), half), :].astype(BF16)


def normed_back(at, dqkv, weights):
    length = dqkv.shape[0]
    return pl.pallas_call(
        normed_back_kernel,
        out_shape=[
            jax.ShapeDtypeStruct((length // 2, D), F32),
            jax.ShapeDtypeStruct((length // 2, D), BF16),
        ],
        grid_spec=pltpu.PrefetchScalarGridSpec(
            num_scalar_prefetch=1,
            grid=(1,),
            in_specs=[once_spec(dqkv.shape), once_spec(weights.shape)],
            out_specs=[once_spec((length // 2, D))] * 2,
            scratch_shapes=[pltpu.VMEM((length, D), F32)],
        ),
        compiler_params=params(),
        cost_estimate=cost(2 * length * D * dqkv.shape[1], 10_000_000),
    )(at, dqkv, weights)


def sum_lines(pieces, dp_index, lag=3):
    middle = (dp_index == 1) | (dp_index == 2)
    totals, done = [], []
    for t, own in enumerate(pieces):
        if t >= lag:
            own = after(own, totals[t - lag])
        inward = lax.ppermute(own, "dp", ((0, 1), (3, 2)))
        pair = round_low(own.astype(F32) + inward.astype(F32))
        other = lax.ppermute(pair, "dp", ((1, 2), (2, 1)))
        total = round_low(pair.astype(F32) + other.astype(F32))
        totals.append(total)
        outward = lax.ppermute(total, "dp", ((1, 0), (2, 3)))
        done.append(share(jnp.where(middle, total, outward)))
    return done


def scatter_lines(keep, send, dp_index):
    middle = (dp_index == 1) | (dp_index == 2)
    blocks = []
    for places in ([3, 3, 0, 0], [2, 2, 1, 1], [1, 0, 3, 2], [0, 1, 2, 3]):
        place_now = pick(dp_index, [jnp.int32(p) for p in places])
        arrived = swap_hid(lax.dynamic_index_in_dim(send, place_now, axis=0, keepdims=False))
        mine = lax.dynamic_index_in_dim(keep, place_now, axis=0, keepdims=False)
        blocks.append(round_low(mine.astype(F32) + arrived.astype(F32)))

    def plus(block, carry):
        return round_low(block.astype(F32) + carry.astype(F32))

    ends, inner = ((0, 1), (3, 2)), ((1, 2), (2, 1))
    first = lax.ppermute(blocks[0], "dp", ends)
    second = lax.ppermute(blocks[1], "dp", ends)
    across = lax.ppermute(plus(blocks[0], first), "dp", inner)
    outer = lax.ppermute(plus(blocks[2], across), "dp", ends + ((1, 0), (2, 3)))
    met = lax.ppermute(plus(blocks[1], second), "dp", inner)
    return round_low(blocks[3].astype(F32) + outer.astype(F32) + met.astype(F32))


def local_pairs(
    tokens,
    ln1_gain,
    ln1_bias,
    w_qkv,
    w_attn,
    ln2_gain,
    ln2_bias,
    w_in,
    w_out,
    cotangent,
    active_units,
):
    length = tokens.shape[0]
    grans = active_units.shape[0]
    gran_index = lax.axis_index("gran")
    dp_index = lax.axis_index("dp")
    hid_index = lax.axis_index("hid")
    core, side = gran_index % 2, gran_index // 2
    part = D // grans
    quarter = length // grans
    slab = w_in.shape[1]
    block = slab // grans
    tiles = block // UNITS
    order = [gran_index, gran_index ^ 1, gran_index ^ 2, gran_index ^ 3]
    row_of = lambda index: 2 * (index % 2) + index // 2
    quarters = [row_of(index) for index in order]
    first_unit = hid_index * slab + gran_index * block
    level = jnp.where(hid_index == 1, grans - 1, jnp.minimum(gran_index, 2))
    border = jnp.sum(jnp.where(jnp.arange(grans) == level, active_units, 0)) - first_unit
    heads_at = jnp.stack(order + quarters + [hid_index]).astype(jnp.int32)
    units_at = jnp.stack([gran_index, border, core]).astype(jnp.int32)

    def rows_at(array, index, count):
        return lax.dynamic_slice_in_dim(array, index * count, count, axis=0)

    def head_columns(array, start):
        return lax.dynamic_slice_in_dim(array, start + gran_index * part, part, axis=1)

    vectors = jnp.stack([ln1_gain, ln1_bias, ln2_gain, ln2_bias], axis=1)
    own_rows = jnp.concatenate(
        [head_columns(w_qkv, 0), head_columns(w_qkv, D), head_columns(w_qkv, 2 * D)]
        + [jnp.pad(vectors, ((0, 0), (0, HD - 4)))],
        axis=1,
    )
    slots, places = rows_of_line(own_rows, dp_index)
    blocks, at = [], []
    for rows, index in zip([own_rows] + slots, [dp_index] + places):
        blocks += [rows, swap_hid(rows)]
        at += [2 * index + hid_index, 2 * index + 1 - hid_index]
    columns = own_rows.shape[1]
    qkv_cols = place(blocks, at, (D, columns), BF16, lambda at, t: (at, t))
    gains = qkv_cols[:, 3 * part : 3 * part + 4].astype(F32).T
    gain_one, bias_one, gain_two, bias_two = (gains[i : i + 1] for i in range(4))

    out_grad = cotangent[0]
    far_hid = hid_index == 1

    def mixed(flag, value):
        return value.astype(F32) * flag.astype(F32)

    def cot_sums(cot):
        mate = swap_near(cot)
        even, odd = jnp.where(core == 0, cot, mate), jnp.where(core == 0, mate, cot)
        pair = round_low(even.astype(F32) + odd.astype(F32))
        upper = rows_at(jnp.where(far_hid, odd, pair), core, length // 2)
        upper = lax.ppermute(upper, "gran", ((2, 0), (3, 1)))
        near = swap_near(upper)
        upper = jnp.concatenate(
            [jnp.where(core == 0, upper, near), jnp.where(core == 0, near, upper)], axis=0
        )
        low = (
            mixed(~far_hid & ((side == 1) | (core == 0)), even)
            + mixed(~far_hid | (side == 1), odd)
            + mixed(side == 0, upper)
        )
        high = mixed((side == 1) | (~far_hid & (core == 0)), odd) + mixed(side == 0, upper)
        return jnp.stack([low.astype(BF16), high.astype(BF16)]), pair

    cot_own, pair = cot_sums(out_grad)
    dsum = rows_at(pair, quarters[0], quarter).astype(F32)
    dsum = dsum + swap_far(rows_at(pair, quarters[2], quarter)).astype(F32)

    half_dim = HD // 2
    freqs = 10000.0 ** (-(jnp.arange(half_dim, dtype=F32) * 2.0 / HD))
    angles = jnp.arange(length, dtype=F32)[:, None] * freqs[None, :]
    cosine = jnp.concatenate([jnp.cos(angles)] * 2, axis=1)
    sine = jnp.concatenate([-jnp.sin(angles), jnp.sin(angles)], axis=1)
    normed_one, qkv, attended = attend(
        tokens, gain_one, bias_one, qkv_cols, cosine, sine, part
    )
    across = share(swap_hid(attended))
    attended = share(attended)

    cot_oth, _ = cot_sums(swap_hid(after(out_grad, slots[2])))
    tokens_oth = place(
        share(swap_hid(rows_at(tokens, quarters[0], quarter))),
        quarters, (length, D), BF16, lambda at, t: (at, t),
    )
    attn_own = head_columns(w_attn, 0)
    attn_oth = swap_hid(attn_own)
    attn_own = jnp.concatenate(
        [jnp.where(far_hid, attn_oth, attn_own), jnp.where(far_hid, attn_own, attn_oth)], axis=0
    )
    attn_rows, places = rows_of_line(attn_own, dp_index)
    attn_cols = place(
        [attn_own] + attn_rows, [dp_index] + places, (D, part), BF16, lambda at, t: (at, t)
    )
    attn_full = place(share(attn_cols), order, (D, D), BF16, lambda at, t: (t, at))

    normed_own, hidden = hidden_and_norm(
        attended, heads_at, attn_full, tokens, gain_two, bias_two, True
    )
    (normed_oth,) = hidden_and_norm(
        across, heads_at, attn_full, tokens_oth, gain_two, bias_two, False
    )

    act, slope, *out_pieces = feed_up(
        units_at, normed_own, normed_oth, cot_own, cot_oth, w_in, block
    )
    *in_pieces, keep, send = feed_down(
        units_at, normed_own, normed_oth, cot_own, cot_oth, slope, w_in, w_out, block
    )
    sums = sum_lines(out_pieces + in_pieces, dp_index)
    w_out_grad = w_in_grad = None
    for k in range(tiles):
        w_out_grad = place(
            sums[k], order, w_out.shape, F32, lambda at, t, k=k: (at * tiles + k, t), w_out_grad
        )
    for k in range(tiles):
        w_in_grad = place(
            sums[tiles + k], order, w_in.shape, F32, lambda at, t, k=k: (t, at * tiles + k), w_in_grad
        )

    rows = keep + swap_near(send).astype(F32)
    rows = rows.reshape(2, 2, quarter, D)

    def one_of(array, index, axis):
        return lax.dynamic_index_in_dim(array, index, axis=axis, keepdims=False)

    rows = one_of(rows, side, 1) + swap_far(round_low(one_of(rows, 1 - side, 1))).astype(F32)
    dnormed_two = rows[0] + swap_hid(round_low(rows[1])).astype(F32)
    dhidden, dlow, gain_two_term, bias_two_term = norm_backward(
        dnormed_two, rows_at(hidden, quarters[0], quarter), dsum, gain_two
    )
    branches = share(dlow)

    dqkv, keep, send = attend_back(
        heads_at, branches, attended, attn_full, qkv, normed_one, cosine, sine
    )
    terms = share(scatter_lines(keep, send, dp_index))
    qkv_grad = place([term[:, : 3 * part] for term in terms], order, w_qkv.shape, F32,
                     lambda at, t: (0, t * grans + at), None, 3)
    attn_grad = place([term[:, 3 * part :] for term in terms], order, w_attn.shape, F32,
                      lambda at, t: (t, at))

    keep, send = normed_back(units_at, dqkv, qkv_cols)
    rows = (keep + swap_near(send).astype(F32)).reshape(2, quarter, D)
    dnormed_one = one_of(rows, side, 0) + swap_far(round_low(one_of(rows, 1 - side, 0))).astype(F32)
    _, dx, gain_one_term, bias_one_term = norm_backward(
        dnormed_one, rows_at(tokens, quarters[0], quarter), dhidden, gain_one
    )
    x_grad = place(share(dx), quarters, tokens.shape, F32, lambda at, t: (at, t))

    vector_terms = jnp.concatenate(
        [gain_one_term, bias_one_term, gain_two_term, bias_two_term], axis=0
    )
    for swap in (swap_near, swap_far, swap_hid):
        vector_terms = vector_terms + swap(vector_terms)
    for hops in (((0, 1), (1, 0), (2, 3), (3, 2)), ((0, 2), (2, 0), (1, 3), (3, 1))):
        vector_terms = vector_terms + lax.ppermute(vector_terms, "dp", hops)
    width = ln1_gain.shape[0]
    vector_grads = lax.dynamic_slice_in_dim(
        vector_terms, (2 * dp_index + hid_index) * width, width, axis=1
    )

    low, full = feed_out(units_at, act, w_out, block)
    near = swap_near(jnp.where(core == 0, full, low)).astype(F32)
    below = lax.ppermute(round_low(near + full.astype(F32)), "gran", ((1, 3),))
    below = below + lax.ppermute(below, "gran", ((3, 2),))
    total = jnp.where((core == 1) & (side == 1), full, low).astype(F32)
    total = total + jnp.where(gran_index == 0, 0.0, near) + below.astype(F32)
    total = jnp.where(far_hid & (gran_index < grans - 1), 0.0, total)
    ffn = total[:length] + swap_hid(round_low(total[length:])).astype(F32)
    outputs = (hidden + ffn).astype(BF16)[None]

    return (
        outputs,
        x_grad,
        vector_grads[0],
        vector_grads[1],
        qkv_grad,
        attn_grad,
        vector_grads[2],
        vector_grads[3],
        w_in_grad,
        w_out_grad,
    )


def local_any(
    tokens,
    ln1_gain,
    ln1_bias,
    w_qkv,
    w_attn,
    ln2_gain,
    ln2_bias,
    w_in,
    w_out,
    cotangent,
    active_units,
):
    length = tokens.shape[0]
    grans = active_units.shape[0]
    hids = lax.axis_size("hid")
    gran_index = lax.axis_index("gran")
    hid_index = lax.axis_index("hid")
    heads = HEADS // grans
    part = heads * HD
    quarter = length // grans

    def head_columns(array, start):
        return lax.dynamic_slice_in_dim(array, start + gran_index * part, part, axis=1)

    vectors = jnp.stack([ln1_gain, ln1_bias, ln2_gain, ln2_bias], axis=1)
    qkv_rows = jnp.concatenate(
        [head_columns(w_qkv, 0), head_columns(w_qkv, D), head_columns(w_qkv, 2 * D), vectors], axis=1
    )
    qkv_all = lax.all_gather(qkv_rows, ALL_ROWS, axis=0, tiled=True)
    qkv_cols = qkv_all[:, : 3 * part]
    gains = qkv_all[:, 3 * part :].astype(F32).T
    gain_one, bias_one, gain_two, bias_two = (gains[i : i + 1] for i in range(4))
    attn_cols = lax.all_gather(head_columns(w_attn, 0), ALL_ROWS, axis=0, tiled=True)
    attn_full = lax.all_gather(attn_cols, "gran", axis=1, tiled=True)

    all_tokens = lax.all_gather(tokens, "hid", axis=0, tiled=True)
    out_grad = cotangent[0]
    all_cot = lax.all_gather(out_grad, LAYER, axis=0).reshape(hids, grans, length, D)
    slab = w_in.shape[1]
    block = slab // grans
    first_unit = hid_index * slab + gran_index * block
    total_units = slab * hids
    level = jnp.int32(0)
    for step in range(1, grans):
        bound = total_units * 2 ** (step - 1) // 8
        level = level + (first_unit >= bound).astype(jnp.int32)
    above = jnp.minimum(level + 1, grans - 1)

    def sum_from(start):
        keep = (jnp.arange(grans) >= start).astype(F32)[None, :, None, None]
        return jnp.sum(all_cot.astype(F32) * keep, axis=1).reshape(hids * length, D).astype(BF16)

    cot_lo, cot_hi = sum_from(level), sum_from(above)
    border = jnp.sum(jnp.where(jnp.arange(grans) == level, active_units, 0))
    low_unit = (first_unit + jnp.arange(block, dtype=jnp.int32)) < border
    cot_own = lax.psum_scatter(out_grad, "gran", scatter_dimension=0, tiled=True).astype(F32)

    x_rows = tokens.astype(F32)
    unit_one, scale_one = norm_parts(x_rows)
    normed_one = (unit_one * gain_one + bias_one).astype(BF16)
    qkv = dot(normed_one, qkv_cols)
    cosine, sine = rotary_tables(length)
    causal = jnp.arange(length)[:, None] >= jnp.arange(length)[None, :]
    kept, attended = [], []
    for head in range(heads):
        at = head * HD
        query = turn(qkv[:, at : at + HD], cosine, sine).astype(BF16)
        key = turn(qkv[:, part + at : part + at + HD], cosine, sine).astype(BF16)
        value = qkv[:, 2 * part + at : 2 * part + at + HD].astype(BF16)
        scores = jnp.where(causal, dot_nt(query, key) / math.sqrt(HD), -1000000000.0)
        exponent = jnp.exp(scores - jnp.max(scores, axis=-1, keepdims=True))
        probs = exponent / jnp.sum(exponent, axis=-1, keepdims=True)
        probs_low = probs.astype(BF16)
        attended.append(dot(probs_low, value).astype(BF16))
        kept.append((query, key, value, probs))
    attended = jnp.concatenate(attended, axis=1)
    everyone = lax.all_gather(attended, LAYER, axis=0).reshape(hids, grans, length, part)
    all_attended = everyone.transpose(0, 2, 1, 3).reshape(hids * length, D)
    hidden = all_tokens.astype(F32) + dot(all_attended, attn_full)
    unit_two, scale_two = norm_parts(hidden)
    normed_two = (unit_two * gain_two + bias_two).astype(BF16)

    w_in_block = lax.dynamic_slice_in_dim(w_in, gran_index * block, block, axis=1)
    w_out_block = lax.dynamic_slice_in_dim(w_out, gran_index * block, block, axis=0)
    pre = dot(normed_two, w_in_block)
    act, slope = gelu_both(pre)
    act = act.astype(BF16)
    dact = jnp.where(low_unit[None], dot_nt(cot_lo, w_out_block), dot_nt(cot_hi, w_out_block))
    dpre = (dact * slope).astype(BF16)
    out_term = jnp.where(low_unit[:, None], dot_tn(act, cot_lo), dot_tn(act, cot_hi))
    in_term = dot_tn(normed_two, dpre)
    dnormed_two = dot_nt(dpre, w_in_block).astype(BF16)

    out_term, in_term = lax.psum((out_term.astype(BF16), in_term.astype(BF16)), "dp")
    w_out_grad = lax.all_gather(out_term, "gran", axis=0, tiled=True)
    w_in_grad = lax.all_gather(in_term, "gran", axis=1, tiled=True)

    dnormed_two = lax.psum_scatter(dnormed_two, LAYER, scatter_dimension=0, tiled=True).astype(F32)
    row = hid_index * length + gran_index * quarter

    def own_rows(array):
        return lax.dynamic_slice_in_dim(array, row, quarter, axis=0)

    unit_two, scale_two = own_rows(unit_two), own_rows(scale_two)
    dhidden = cot_own + norm_back(dnormed_two, unit_two, scale_two, gain_two)
    gain_two_term = jnp.sum(dnormed_two * unit_two, axis=0)
    bias_two_term = jnp.sum(dnormed_two, axis=0)
    dbranch = lax.all_gather(dhidden.astype(BF16), "gran", axis=0, tiled=True)

    attn_rows = lax.dynamic_slice_in_dim(attn_full, gran_index * part, part, axis=0)
    dattended = dot_nt(dbranch, attn_rows).astype(BF16)
    own_attended = lax.dynamic_slice_in_dim(all_attended, hid_index * length, length, axis=0)
    dbranch_cols = lax.dynamic_slice_in_dim(dbranch, gran_index * part, part, axis=1)
    attn_term = dot_tn(own_attended, dbranch_cols)
    dqueries, dkeys, dvalues = [], [], []
    for head in range(heads):
        query, key, value, probs = kept[head]
        dvec = dattended[:, head * HD : (head + 1) * HD]
        dprobs = dot_nt(dvec, value)
        inner = jnp.sum(probs * dprobs, axis=-1, keepdims=True)
        dscores = (probs * (dprobs - inner)).astype(BF16)
        dqueries.append(turn_back(dot(dscores, key) / math.sqrt(HD), cosine, sine).astype(BF16))
        dkeys.append(turn_back(dot_tn(dscores, query) / math.sqrt(HD), cosine, sine).astype(BF16))
        dvalues.append(dot_tn(probs.astype(BF16), dvec).astype(BF16))
    dqkv = jnp.concatenate(dqueries + dkeys + dvalues, axis=1)
    qkv_term = dot_tn(normed_one, dqkv)
    dnormed_one = lax.psum_scatter(
        dot_nt(dqkv, qkv_cols).astype(BF16), "gran", scatter_dimension=0, tiled=True
    ).astype(F32)

    unit_one = lax.dynamic_slice_in_dim(unit_one, gran_index * quarter, quarter, axis=0)
    scale_one = lax.dynamic_slice_in_dim(scale_one, gran_index * quarter, quarter, axis=0)
    dx = dhidden + norm_back(dnormed_one, unit_one, scale_one, gain_one)
    gain_one_term = jnp.sum(dnormed_one * unit_one, axis=0)
    bias_one_term = jnp.sum(dnormed_one, axis=0)
    x_grad = lax.all_gather(dx.astype(BF16), "gran", axis=0, tiled=True).astype(F32)

    vector_terms = jnp.stack([gain_one_term, bias_one_term, gain_two_term, bias_two_term], axis=1)
    terms = jnp.concatenate([qkv_term, attn_term, vector_terms], axis=1).astype(BF16)
    terms = lax.psum_scatter(terms, ALL_ROWS, scatter_dimension=0, tiled=True)
    terms = lax.all_gather(terms, "gran", axis=0).astype(F32)

    def grads_of(start):
        return [terms[k, :, start : start + part] for k in range(grans)]

    qkv_grad = jnp.concatenate(grads_of(0) + grads_of(part) + grads_of(2 * part), axis=1)
    attn_grad = jnp.concatenate(grads_of(3 * part), axis=1)
    vector_grads = jnp.sum(terms[:, :, 4 * part :], axis=0).T

    act_low = jnp.where(low_unit[None], act, 0)
    part_low = dot(act_low, w_out_block)
    part_all = part_low + dot(act - act_low, w_out_block)
    shares = []
    for k in range(grans):
        share = jnp.where(level < k, part_all, jnp.where(level == k, part_low, 0.0))
        shares.append(share.astype(BF16).reshape(hids, length, D))
    shares = jnp.stack(shares, axis=1).reshape(hids * grans * length, D)
    ffn = lax.psum_scatter(shares, LAYER, scatter_dimension=0, tiled=True).astype(F32)
    own_hidden = lax.dynamic_slice_in_dim(hidden, hid_index * length, length, axis=0)
    outputs = (own_hidden + ffn).astype(BF16)[None]

    return (
        outputs,
        x_grad,
        vector_grads[0],
        vector_grads[1],
        qkv_grad,
        attn_grad,
        vector_grads[2],
        vector_grads[3],
        w_in_grad.astype(F32),
        w_out_grad.astype(F32),
    )


def solution(mesh):
    pairs = (mesh.shape["gran"], mesh.shape["dp"], mesh.shape["hid"]) == (4, 4, 2)
    return jax.shard_map(
        local_pairs if pairs else local_any,
        mesh=mesh,
        in_specs=(
            P(("dp", "hid"), None),
            P(("dp", "hid")),
            P(("dp", "hid")),
            P(("dp", "hid"), None),
            P(("dp", "hid"), None),
            P(("dp", "hid")),
            P(("dp", "hid")),
            P(None, "hid"),
            P("hid", None),
            P("gran", ("dp", "hid"), None),
            P(),
        ),
        out_specs=(
            P("gran", ("dp", "hid"), None),
            P(("dp", "hid"), None),
            P(("dp", "hid")),
            P(("dp", "hid")),
            P(("dp", "hid"), None),
            P(("dp", "hid"), None),
            P(("dp", "hid")),
            P(("dp", "hid")),
            P(None, "hid"),
            P("hid", None),
        ),
        check_vma=False,
    )
```

```python
import functools
import math

import jax
import jax.numpy as jnp
from jax import lax
from jax.experimental import pallas as pl
from jax.experimental.pallas import tpu as pltpu
from jax.sharding import PartitionSpec as P

D = 1536
HEADS = 12
HD = 128

EPS = 1e-05
GELU_C = 0.7978845608028654
GELU_A = 0.044715
BF16 = jnp.bfloat16
F32 = jnp.float32

ALL_ROWS = ("dp", "hid")
LAYER = ("hid", "gran")


def round_low(values):
    return lax.reduce_precision(values, 8, 7).astype(BF16)


def dot(left, right, contract=((1,), (0,))):
    return lax.dot_general(left, right, (contract, ((), ())), preferred_element_type=F32)


def dot_nt(left, right):
    return dot(left, right, ((1,), (1,)))


def dot_tn(left, right):
    return dot(left, right, ((0,), (0,)))


def norm_parts(values):
    centred = values - jnp.mean(values, axis=-1, keepdims=True)
    scale = lax.rsqrt(jnp.mean(centred * centred, axis=-1, keepdims=True) + EPS)
    return centred * scale, scale


def norm_back(dout, unit, scale, gain):
    inner = dout * gain
    return scale * (
        inner
        - jnp.mean(inner, axis=-1, keepdims=True)
        - unit * jnp.mean(inner * unit, axis=-1, keepdims=True)
    )


def gelu_both(values):
    square = values * values
    bent = jnp.tanh(GELU_C * values * (1.0 + GELU_A * square))
    half = 0.5 * (1.0 + bent)
    slope = half + 0.5 * values * (1.0 - bent * bent) * (GELU_C * (1.0 + 3.0 * GELU_A * square))
    return values * half, slope


def rotary_tables(length):
    half_dim = HD // 2
    freqs = 10000.0 ** (-(jnp.arange(half_dim, dtype=F32) * 2.0 / HD))
    angles = jnp.arange(length, dtype=F32)[:, None] * freqs[None, :]
    return jnp.cos(angles), jnp.sin(angles)


def turn(block, cosine, sine):
    lower, upper = block[:, : HD // 2], block[:, HD // 2 :]
    return jnp.concatenate([lower * cosine - upper * sine, upper * cosine + lower * sine], axis=1)


def turn_back(block, cosine, sine):
    return turn(block, cosine, -sine)


def after(value, *others):
    return lax.optimization_barrier((value,) + others)[0]


class Line:
    def __init__(self):
        self.last = None

    def wait(self, value):
        if self.last is not None:
            value = after(value, self.last)
        self.last = value
        return value

    def made(self, value):
        self.last = value
        return value


def swap_hid(value):
    return lax.ppermute(value, "hid", ((0, 1), (1, 0)))


def swap_near(value):
    return lax.ppermute(value, "gran", ((0, 1), (1, 0), (2, 3), (3, 2)))


def swap_far(value):
    return lax.ppermute(value, "gran", ((0, 2), (2, 0), (1, 3), (3, 1)))


def share(own):
    far = swap_far(own)
    return own, swap_near(own), far, swap_near(far)


def pick(index, options):
    chosen = options[-1]
    for k in range(len(options) - 2, -1, -1):
        chosen = jnp.where(index == k, options[k], chosen)
    return chosen


def params(vmem_mib=56):
    return pltpu.CompilerParams(vmem_limit_bytes=vmem_mib * 1024 * 1024)


def cost(flops, moved):
    return pl.CostEstimate(flops=flops, bytes_accessed=moved, transcendentals=0)


def whole_spec(shape):
    return pl.BlockSpec(shape, lambda *_: (0,) * len(shape))


def once_spec(shape):
    return pl.BlockSpec(shape, lambda *_: (0,) * len(shape), pipeline_mode=pl.Buffered(1))


def place_kernel(count, flip, at_ref, *refs):
    out_ref = refs[-1]
    for k in range(count):

        @pl.when(pl.program_id(0) == k)
        def _(k=k):
            block = refs[k][...].astype(out_ref.dtype)
            out_ref[...] = block.T if flip else block


def place(pieces, at, shape, dtype, where, whole=None, parts=1, flip=False):
    count = len(pieces)
    rows, columns = pieces[0].shape
    block = (rows, columns // parts)
    out_block = block[::-1] if flip else block
    specs = [pl.BlockSpec(block, lambda k, t, at: (0, t))] * count
    operands = list(pieces)
    aliases = {}
    if whole is not None:
        specs.append(pl.BlockSpec(memory_space=pl.ANY))
        operands.append(whole)
        aliases = {count + 1: 0}
    size = rows * columns * count * (2 + jnp.dtype(dtype).itemsize)
    return pl.pallas_call(
        functools.partial(place_kernel, count, flip),
        out_shape=jax.ShapeDtypeStruct(shape, dtype),
        grid_spec=pltpu.PrefetchScalarGridSpec(
            num_scalar_prefetch=1,
            grid=(count, parts),
            in_specs=specs,
            out_specs=pl.BlockSpec(out_block, lambda k, t, at: where(at[k], t)),
        ),
        input_output_aliases=aliases,
        compiler_params=params(40),
        cost_estimate=cost(0, size),
    )(jnp.stack(at).astype(jnp.int32), *operands)


def rotate(block, cos_ref, sin_ref, sign):
    return block * cos_ref[...] + pltpu.roll(block, HD // 2, 1) * (sign * sin_ref[...])


def probs_of(query, key, first_row):
    scores = dot_nt(query, key) * (1.0 / math.sqrt(HD))
    rows = first_row + lax.broadcasted_iota(jnp.int32, scores.shape, 0)
    scores = jnp.where(rows >= lax.broadcasted_iota(jnp.int32, scores.shape, 1), scores, -1e9)
    exponent = jnp.exp(scores - jnp.max(scores, axis=-1, keepdims=True))
    return exponent / jnp.sum(exponent, axis=-1, keepdims=True)


def attend_kernel(x_ref, gain_ref, bias_ref, w_ref, cos_ref, sin_ref, n1_ref, qkv_ref, att_ref):
    length, part = att_ref.shape
    unit, _ = norm_parts(x_ref[...].astype(F32))
    normed = (unit * gain_ref[...] + bias_ref[...]).astype(BF16)
    n1_ref[...] = normed
    for kind in range(3):
        product = dot(normed, w_ref[:, kind * part : (kind + 1) * part])
        for head in range(part // HD):
            block = product[:, head * HD : (head + 1) * HD]
            if kind < 2:
                block = rotate(block, cos_ref, sin_ref, 1.0)
            start = kind * part + head * HD
            qkv_ref[:, start : start + HD] = block.astype(BF16)
    half = length // 2
    for head in range(part // HD):
        cut = slice(head * HD, (head + 1) * HD)
        for row in range(2):
            rows, seen = slice(row * half, (row + 1) * half), slice(0, (row + 1) * half)
            query = qkv_ref[rows, cut]
            key = qkv_ref[seen, part + head * HD : part + (head + 1) * HD]
            value = qkv_ref[seen, 2 * part + head * HD : 2 * part + (head + 1) * HD]
            probs = probs_of(query, key, row * half).astype(BF16)
            att_ref[rows, cut] = dot(probs, value).astype(BF16)


def attend(tokens, gain, bias, weights, cosine, sine, part):
    length = tokens.shape[0]
    return pl.pallas_call(
        attend_kernel,
        out_shape=[
            jax.ShapeDtypeStruct((length, D), BF16),
            jax.ShapeDtypeStruct((length, 3 * part), BF16),
            jax.ShapeDtypeStruct((length, part), BF16),
        ],
        compiler_params=params(),
        cost_estimate=cost(2 * length * D * 3 * part * 2, 10_000_000),
    )(tokens, gain, bias, weights, cosine, sine)


def flip_kernel(in_ref, out_ref):
    out_ref[...] = in_ref[...].T


def flip(array):
    return pl.pallas_call(
        flip_kernel,
        out_shape=jax.ShapeDtypeStruct(array.shape[::-1], array.dtype),
        compiler_params=params(32),
        cost_estimate=cost(0, 2 * array.size * array.dtype.itemsize),
    )(array)


def hidden_kernel(keep, at_ref, a0, a1, a2, a3, w_ref, x_ref, gain_ref, bias_ref, *rest):
    out_refs, all_ref = rest[:-1], rest[-1]
    part = a0.shape[1]
    for k, ref in enumerate((a0, a1, a2, a3)):
        all_ref[:, pl.ds(pl.multiple_of(at_ref[k] * part, HD), part)] = ref[...]
    hidden = x_ref[...].astype(F32) + dot(all_ref[...], w_ref[...])
    unit, _ = norm_parts(hidden)
    out_refs[0][...] = (unit * gain_ref[...] + bias_ref[...]).astype(BF16)
    if keep:
        out_refs[1][...] = hidden


def hidden_and_norm(pieces, order, w_attn, tokens, gain, bias, keep):
    length = tokens.shape[0]
    rows, part = length // 2, pieces[0].shape[1]
    by_row = lambda columns: pl.BlockSpec((rows, columns), lambda i, at: (i, 0))
    types = [BF16, F32] if keep else [BF16]
    return pl.pallas_call(
        functools.partial(hidden_kernel, keep),
        out_shape=[jax.ShapeDtypeStruct((length, D), kind) for kind in types],
        grid_spec=pltpu.PrefetchScalarGridSpec(
            num_scalar_prefetch=1,
            grid=(2,),
            in_specs=[by_row(part)] * 4
            + [once_spec((D, D)), by_row(D), once_spec((1, D)), once_spec((1, D))],
            out_specs=[by_row(D)] * len(types),
            scratch_shapes=[pltpu.VMEM((rows, D), BF16)],
        ),
        compiler_params=params(),
        cost_estimate=cost(2 * length * D * D, 10_000_000),
    )(order, *pieces, w_attn, tokens, gain, bias)


UNITS = 256


def by_border(at_ref, low, high, mixed):
    border = at_ref[1] - pl.program_id(0) * UNITS
    pl.when(border >= UNITS)(low)
    pl.when(border <= 0)(high)
    pl.when((border > 0) & (border < UNITS))(mixed)


def up_kernel(at_ref, n_own, n_oth, s_own, s_oth, w_ref, act_ref, slope_ref, *out_refs):
    length = n_own.shape[0]
    for k, ref in enumerate((n_own, n_oth)):
        act, slope = gelu_both(dot(ref[...], w_ref[...]))
        act_ref[k * length : (k + 1) * length, :] = act.astype(BF16)
        slope_ref[k * length : (k + 1) * length, :] = slope

    def term(columns, which):
        return dot_tn(act_ref[:length, columns], s_own[which]) + dot_tn(
            act_ref[length:, columns], s_oth[which]
        )

    for k, ref in enumerate(out_refs):

        @pl.when(pl.program_id(0) == k)
        def _(ref=ref):
            def plain(which):
                def run():
                    ref[...] = term(slice(0, UNITS), which).astype(BF16)

                return run

            def mixed():
                ref[: UNITS // 2, :] = term(slice(0, UNITS // 2), 0).astype(BF16)
                ref[UNITS // 2 :, :] = term(slice(UNITS // 2, UNITS), 1).astype(BF16)

            by_border(at_ref, plain(0), plain(1), mixed)


def feed_up(at, n_own, n_oth, s_own, s_oth, w_in, block):
    length = n_own.shape[0]
    tiles = block // UNITS
    return pl.pallas_call(
        up_kernel,
        out_shape=[
            jax.ShapeDtypeStruct((2 * length, block), BF16),
            jax.ShapeDtypeStruct((2 * length, block), F32),
        ]
        + [jax.ShapeDtypeStruct((UNITS, D), BF16)] * tiles,
        grid_spec=pltpu.PrefetchScalarGridSpec(
            num_scalar_prefetch=1,
            grid=(tiles,),
            in_specs=[once_spec((length, D))] * 2
            + [once_spec((2, length, D))] * 2
            + [pl.BlockSpec((D, UNITS), lambda i, at: (0, at[0] * tiles + i))],
            out_specs=[pl.BlockSpec((2 * length, UNITS), lambda i, at: (0, i))] * 2
            + [whole_spec((UNITS, D))] * tiles,
        ),
        compiler_params=params(),
        cost_estimate=cost(8 * length * D * block, 20_000_000),
    )(at, n_own, n_oth, s_own, s_oth, w_in)


def down_kernel(at_ref, n_own, n_oth, s_own, s_oth, slope_ref, w_in, w_out, *rest):
    in_refs, (keep_ref, send_ref, total, dact) = rest[:-4], rest[-4:]
    length = n_own.shape[0]
    half = length // 2
    step = pl.program_id(0)

    def fill(columns, which):
        for k, ref in enumerate((s_own, s_oth)):
            dact[k * length : (k + 1) * length, columns] = dot_nt(ref[which], w_out[columns, :])

    def mixed():
        fill(slice(0, UNITS // 2), 0)
        fill(slice(UNITS // 2, UNITS), 1)

    by_border(
        at_ref, lambda: fill(slice(0, UNITS), 0), lambda: fill(slice(0, UNITS), 1), mixed
    )
    dpre = (dact[...] * slope_ref[...]).astype(BF16)
    term = dot_tn(dpre[:length], n_own[...]) + dot_tn(dpre[length:], n_oth[...])
    for k, ref in enumerate(in_refs):

        @pl.when(step == k)
        def _(ref=ref):
            ref[...] = term.astype(BF16)

    product = dot_nt(dpre, w_in[...])

    @pl.when(step == 0)
    def _():
        total[...] = product

    @pl.when(step > 0)
    def _():
        total[...] += product

    @pl.when(step == len(in_refs) - 1)
    def _():
        core = at_ref[2]
        for k in range(2):
            mine = pl.multiple_of(k * length + core * half, half)
            theirs = pl.multiple_of(k * length + (1 - core) * half, half)
            keep_ref[k] = total[pl.ds(mine, half), :]
            send_ref[k] = total[pl.ds(theirs, half), :].astype(BF16)


def feed_down(at, n_own, n_oth, s_own, s_oth, slope, w_in, w_out, block):
    length = n_own.shape[0]
    tiles = block // UNITS
    return pl.pallas_call(
        down_kernel,
        out_shape=[jax.ShapeDtypeStruct((UNITS, D), BF16)] * tiles
        + [
            jax.ShapeDtypeStruct((2, length // 2, D), F32),
            jax.ShapeDtypeStruct((2, length // 2, D), BF16),
        ],
        grid_spec=pltpu.PrefetchScalarGridSpec(
            num_scalar_prefetch=1,
            grid=(tiles,),
            in_specs=[once_spec((length, D))] * 2
            + [once_spec((2, length, D))] * 2
            + [
                pl.BlockSpec((2 * length, UNITS), lambda i, at: (0, i)),
                pl.BlockSpec((D, UNITS), lambda i, at: (0, at[0] * tiles + i)),
                pl.BlockSpec((UNITS, D), lambda i, at: (at[0] * tiles + i, 0)),
            ],
            out_specs=[once_spec((UNITS, D))] * tiles + [once_spec((2, length // 2, D))] * 2,
            scratch_shapes=[
                pltpu.VMEM((2 * length, D), F32),
                pltpu.VMEM((2 * length, UNITS), F32),
            ],
        ),
        compiler_params=params(60),
        cost_estimate=cost(12 * length * D * block, 30_000_000),
    )(at, n_own, n_oth, s_own, s_oth, slope, w_in, w_out)


def out_kernel(at_ref, act_ref, w_ref, low_ref, full_ref, low, high):
    step = pl.program_id(0)

    @pl.when(step == 0)
    def _():
        low[...] = jnp.zeros_like(low)
        high[...] = jnp.zeros_like(high)

    def add(into, cut):
        into[...] += dot(act_ref[:, cut], w_ref[cut, :])

    def mixed():
        add(low, slice(0, UNITS // 2))
        add(high, slice(UNITS // 2, UNITS))

    by_border(at_ref, lambda: add(low, slice(0, UNITS)), lambda: add(high, slice(0, UNITS)), mixed)

    @pl.when(step == pl.num_programs(0) - 1)
    def _():
        low_ref[...] = low[...].astype(BF16)
        full_ref[...] = (low[...] + high[...]).astype(BF16)


def feed_out(at, act, w_out, block):
    rows = act.shape[0]
    tiles = block // UNITS
    return pl.pallas_call(
        out_kernel,
        out_shape=[jax.ShapeDtypeStruct((rows, D), BF16)] * 2,
        grid_spec=pltpu.PrefetchScalarGridSpec(
            num_scalar_prefetch=1,
            grid=(tiles,),
            in_specs=[
                pl.BlockSpec((rows, UNITS), lambda i, at: (0, i)),
                pl.BlockSpec((UNITS, D), lambda i, at: (at[0] * tiles + i, 0)),
            ],
            out_specs=[once_spec((rows, D))] * 2,
            scratch_shapes=[pltpu.VMEM((rows, D), F32)] * 2,
        ),
        compiler_params=params(),
        cost_estimate=cost(2 * rows * D * block, 10_000_000),
    )(at, act, w_out)


def norm_back_kernel(dout_ref, x_ref, rest_ref, gain_ref, d_ref, low_ref, gain_out, bias_out):
    unit, scale = norm_parts(x_ref[...].astype(F32))
    dout = dout_ref[...]
    total = rest_ref[...] + norm_back(dout, unit, scale, gain_ref[...])
    d_ref[...] = total
    low_ref[...] = total.astype(BF16)
    gain_out[...] = jnp.sum(dout * unit, axis=0, keepdims=True)
    bias_out[...] = jnp.sum(dout, axis=0, keepdims=True)


def norm_backward(dout, rows, rest, gain):
    return pl.pallas_call(
        norm_back_kernel,
        out_shape=[
            jax.ShapeDtypeStruct(dout.shape, F32),
            jax.ShapeDtypeStruct(dout.shape, BF16),
            jax.ShapeDtypeStruct((1, D), F32),
            jax.ShapeDtypeStruct((1, D), F32),
        ],
        compiler_params=params(32),
        cost_estimate=cost(0, 4_000_000),
    )(dout, rows, rest, gain)


def attend_back_kernel(
    at_ref, b0, b1, b2, b3, a0, a1, a2, a3, w_ref, qkv_ref, n1_ref, cos_ref, sin_ref,
    dqkv_ref, keep_ref, send_ref, branch, block,
):
    length, part = a0.shape
    quarter = b0.shape[0]
    hid, gran = at_ref[8], at_ref[0]
    for k, ref in enumerate((b0, b1, b2, b3)):
        branch[pl.ds(pl.multiple_of(at_ref[4 + k] * quarter, quarter), quarter), :] = ref[...]
    dattended = dot_nt(branch[...], w_ref[...]).astype(BF16)
    half = length // 2
    scale = 1.0 / math.sqrt(HD)
    for head in range(part // HD):
        q_cut = slice(head * HD, (head + 1) * HD)
        k_cut = slice(part + head * HD, part + (head + 1) * HD)
        v_cut = slice(2 * part + head * HD, 2 * part + (head + 1) * HD)
        sums = {}
        for row in range(2):
            rows, seen = slice(row * half, (row + 1) * half), slice(0, (row + 1) * half)
            query, key, value = qkv_ref[rows, q_cut], qkv_ref[seen, k_cut], qkv_ref[seen, v_cut]
            probs = probs_of(query, key, row * half)
            dvec = dattended[rows, q_cut]
            dprobs = dot_nt(dvec, value)
            inner = jnp.sum(probs * dprobs, axis=-1, keepdims=True)
            dscores = (probs * (dprobs - inner)).astype(BF16)
            dquery = dot(dscores, key) * scale
            dquery = dquery * cos_ref[rows, :] - pltpu.roll(dquery, HD // 2, 1) * sin_ref[rows, :]
            dqkv_ref[rows, q_cut] = dquery.astype(BF16)
            sums[row] = dot_tn(dscores, query) * scale, dot_tn(probs.astype(BF16), dvec)
        for row in range(2):
            rows = slice(row * half, (row + 1) * half)
            dkey, dvalue = (sums[1][i][rows] + (sums[0][i] if row == 0 else 0.0) for i in range(2))
            dkey = dkey * cos_ref[rows, :] - pltpu.roll(dkey, HD // 2, 1) * sin_ref[rows, :]
            dqkv_ref[rows, k_cut] = dkey.astype(BF16)
            dqkv_ref[rows, v_cut] = dvalue.astype(BF16)
    piece = keep_ref.shape[1]
    mine = pl.multiple_of(hid * piece, 16)
    theirs = pl.multiple_of((1 - hid) * piece, 16)
    for line in range(4):
        rows = slice(line * 2 * piece, (line + 1) * 2 * piece)
        block[...] = dot(n1_ref[rows, :], dqkv_ref[...])
        keep_ref[line, :, : 3 * part] = block[pl.ds(mine, piece), :].astype(BF16)
        send_ref[line, :, : 3 * part] = block[pl.ds(theirs, piece), :].astype(BF16)
    own_columns = branch[:, pl.ds(pl.multiple_of(gran * part, HD), part)]
    for k, ref in enumerate((a0, a1, a2, a3)):
        block[:, :part] = dot_tn(ref[...], own_columns)
        keep_ref[at_ref[k], :, 3 * part :] = block[pl.ds(mine, piece), :part].astype(BF16)
        send_ref[at_ref[k], :, 3 * part :] = block[pl.ds(theirs, piece), :part].astype(BF16)


def attend_back(at, branches, attended, w_attn, qkv, n1, cosine, sine):
    length, part = attended[0].shape
    piece = D // 8
    quarter = branches[0].shape[0]
    out = jax.ShapeDtypeStruct((4, piece, 4 * part), BF16)
    return pl.pallas_call(
        attend_back_kernel,
        out_shape=[jax.ShapeDtypeStruct((length, 3 * part), BF16), out, out],
        grid_spec=pltpu.PrefetchScalarGridSpec(
            num_scalar_prefetch=1,
            grid=(1,),
            in_specs=[once_spec((quarter, D))] * 4
            + [once_spec((length, part))] * 4
            + [
                pl.BlockSpec((part, D), lambda i, at: (at[0], 0)),
                once_spec((length, 3 * part)),
                once_spec((D, length)),
                once_spec((length, HD)),
                once_spec((length, HD)),
            ],
            out_specs=[once_spec((length, 3 * part))] + [once_spec((4, piece, 4 * part))] * 2,
            scratch_shapes=[
                pltpu.VMEM((length, D), BF16),
                pltpu.VMEM((2 * piece, 3 * part), F32),
            ],
        ),
        compiler_params=params(),
        cost_estimate=cost(12 * length * D * part, 20_000_000),
    )(at, *branches, *attended, w_attn, qkv, n1, cosine, sine)


def normed_back_kernel(at_ref, dqkv_ref, w_ref, keep_ref, send_ref, total):
    half = keep_ref.shape[0]
    total[...] = dot_nt(dqkv_ref[...], w_ref[:, : dqkv_ref.shape[1]])
    core = at_ref[2]
    keep_ref[...] = total[pl.ds(pl.multiple_of(core * half, half), half), :]
    send_ref[...] = total[pl.ds(pl.multiple_of((1 - core) * half, half), half), :].astype(BF16)


def normed_back(at, dqkv, weights):
    length = dqkv.shape[0]
    return pl.pallas_call(
        normed_back_kernel,
        out_shape=[
            jax.ShapeDtypeStruct((length // 2, D), F32),
            jax.ShapeDtypeStruct((length // 2, D), BF16),
        ],
        grid_spec=pltpu.PrefetchScalarGridSpec(
            num_scalar_prefetch=1,
            grid=(1,),
            in_specs=[once_spec(dqkv.shape), once_spec(weights.shape)],
            out_specs=[once_spec((length // 2, D))] * 2,
            scratch_shapes=[pltpu.VMEM((length, D), F32)],
        ),
        compiler_params=params(),
        cost_estimate=cost(2 * length * D * dqkv.shape[1], 10_000_000),
    )(at, dqkv, weights)


def local_pairs(
    tokens,
    ln1_gain,
    ln1_bias,
    w_qkv,
    w_attn,
    ln2_gain,
    ln2_bias,
    w_in,
    w_out,
    cotangent,
    active_units,
):
    length = tokens.shape[0]
    grans = active_units.shape[0]
    gran_index = lax.axis_index("gran")
    dp_index = lax.axis_index("dp")
    hid_index = lax.axis_index("hid")
    core, side = gran_index % 2, gran_index // 2
    part = D // grans
    quarter = length // grans
    slab = w_in.shape[1]
    block = slab // grans
    tiles = block // UNITS
    order = [gran_index, gran_index ^ 1, gran_index ^ 2, gran_index ^ 3]
    row_of = lambda index: 2 * (index % 2) + index // 2
    quarters = [row_of(index) for index in order]
    first_unit = hid_index * slab + gran_index * block
    level = jnp.where(hid_index == 1, grans - 1, jnp.minimum(gran_index, 2))
    border = jnp.sum(jnp.where(jnp.arange(grans) == level, active_units, 0)) - first_unit
    heads_at = jnp.stack(order + quarters + [hid_index]).astype(jnp.int32)
    units_at = jnp.stack([gran_index, border, core]).astype(jnp.int32)

    def rows_at(array, index, count):
        return lax.dynamic_slice_in_dim(array, index * count, count, axis=0)

    def head_columns(array, start):
        return lax.dynamic_slice_in_dim(array, start + gran_index * part, part, axis=1)

    line = Line()
    wait = line.wait
    end = (dp_index == 0) | (dp_index == 3)
    all_hops = ((0, 1), (1, 0), (2, 3), (3, 2))
    inner_hops, outward_hops, inward_hops = ((1, 2), (2, 1)), ((1, 0), (2, 3)), ((0, 1), (3, 2))

    def hop(value, hops):
        return lax.ppermute(value, "dp", hops)

    def by_line(*options):
        return pick(dp_index, [jnp.int32(k) for k in options])

    def plus(block, carry):
        return round_low(block.astype(F32) + carry.astype(F32))

    def one_of(array, index, axis):
        return lax.dynamic_index_in_dim(array, index, axis=axis, keepdims=False)

    vectors = jnp.stack([ln1_gain, ln1_bias, ln2_gain, ln2_bias], axis=1)
    own_rows = jnp.concatenate(
        [head_columns(w_qkv, 0), head_columns(w_qkv, D), head_columns(w_qkv, 2 * D)]
        + [jnp.pad(vectors, ((0, 0), (0, HD - 4)))],
        axis=1,
    )
    out_grad = cotangent[0]
    far_hid = hid_index == 1

    one = hop(own_rows, all_hops)
    inner = hop(own_rows, inner_hops)
    own_swap = swap_hid(own_rows)
    attn_own = head_columns(w_attn, 0)
    attn_oth = swap_hid(attn_own)

    def mixed(flag, value):
        return value.astype(F32) * flag.astype(F32)

    def core_pair(cot, mate):
        even, odd = jnp.where(core == 0, cot, mate), jnp.where(core == 0, mate, cot)
        return odd, round_low(even.astype(F32) + odd.astype(F32))

    def upper_half(odd, pair):
        rows = rows_at(jnp.where(far_hid, odd, pair), core, odd.shape[0] // 2)
        return lax.ppermute(rows, "gran", ((2, 0), (3, 1)))

    def cot_sums(odd, pair, upper, near):
        upper = jnp.concatenate(
            [jnp.where(core == 0, upper, near), jnp.where(core == 0, near, upper)], axis=0
        )
        whole = ~far_hid & ((side == 1) | (core == 0))
        low = (
            mixed(whole, pair)
            + mixed(~whole & (~far_hid | (side == 1)), odd)
            + mixed(side == 0, upper)
        )
        high = mixed((side == 1) | (~far_hid & (core == 0)), odd) + mixed(side == 0, upper)
        return low.astype(BF16), high.astype(BF16)

    odd_own, pair_own = core_pair(out_grad, wait(swap_near(out_grad)))
    line.made(pair_own)
    upper_own = upper_half(odd_own, pair_own)
    dsum_far = swap_far(rows_at(pair_own, quarters[2], quarter))

    attn_oth = wait(attn_oth)
    attn_own = line.made(
        jnp.concatenate(
            [jnp.where(far_hid, attn_oth, attn_own), jnp.where(far_hid, attn_own, attn_oth)], axis=0
        )
    )
    one = wait(one)
    one_swap = swap_hid(one)
    across = hop(one, inner_hops)
    inner = wait(inner)
    outer = hop(inner, outward_hops)
    upper_own = wait(upper_own)
    near_own = swap_near(upper_own)
    outer, across = wait(outer), wait(across)
    two = line.made(jnp.where(end, outer, inner))
    two_swap = swap_hid(two)
    last = hop(across, outward_hops)
    attn_own = after(attn_own, two)
    attn_one = hop(attn_own, all_hops)
    attn_inner = hop(attn_own, inner_hops)
    low, high = cot_sums(odd_own, pair_own, upper_own, wait(near_own))
    cot_own = line.made(jnp.stack([low, high]))
    dsum = rows_at(pair_own, quarters[0], quarter).astype(F32) + wait(dsum_far).astype(F32)
    last = wait(last)
    three = line.made(jnp.where(end, last, across))
    three_swap = swap_hid(three)
    tokens_swap = swap_hid(rows_at(after(tokens, three), quarters[0], quarter))
    first_half = swap_hid(after(rows_at(out_grad, 0, length // 2), three))
    attn_one, attn_inner = wait(attn_one), wait(attn_inner)
    attn_across = hop(attn_one, inner_hops)
    attn_outer = hop(attn_inner, outward_hops)

    blocks, at = [], []
    for rows, other, index in (
        (own_rows, own_swap, dp_index),
        (one, one_swap, by_line(1, 0, 3, 2)),
        (two, two_swap, by_line(2, 2, 1, 1)),
        (three, three_swap, by_line(3, 3, 0, 0)),
    ):
        blocks += [rows, wait(other)]
        at += [2 * index + hid_index, 2 * index + 1 - hid_index]
    columns = own_rows.shape[1]
    qkv_cols = place(blocks, at, (D, columns), BF16, lambda at, t: (at, t))
    gains = qkv_cols[:, 3 * part : 3 * part + 4].astype(F32).T
    gain_one, bias_one, gain_two, bias_two = (gains[i : i + 1] for i in range(4))
    half_dim = HD // 2
    freqs = 10000.0 ** (-(jnp.arange(half_dim, dtype=F32) * 2.0 / HD))
    angles = jnp.arange(length, dtype=F32)[:, None] * freqs[None, :]
    cosine = jnp.concatenate([jnp.cos(angles)] * 2, axis=1)
    sine = jnp.concatenate([-jnp.sin(angles), jnp.sin(angles)], axis=1)
    normed_one, qkv, attended = attend(
        tokens, gain_one, bias_one, qkv_cols, cosine, sine, part
    )
    line.made(attended)
    attended_far, attended_near = swap_far(attended), swap_near(attended)
    across_own = swap_hid(attended)
    second_half = swap_hid(after(rows_at(out_grad, 1, length // 2), attended))

    attn_across, attn_outer = wait(attn_across), wait(attn_outer)
    attn_last = hop(attn_across, outward_hops)
    attn_two = line.made(jnp.where(end, attn_outer, attn_inner))
    tokens_swap = wait(tokens_swap)
    tokens_far, tokens_near = swap_far(tokens_swap), swap_near(tokens_swap)
    attn_three = line.made(jnp.where(end, wait(attn_last), attn_across))
    attn_cols = line.made(
        place(
            [attn_own, attn_one, attn_two, attn_three],
            [dp_index, by_line(1, 0, 3, 2), by_line(2, 2, 1, 1), by_line(3, 3, 0, 0)],
            (D, part), BF16, lambda at, t: (at, t),
        )
    )
    attn_far, attn_near = swap_far(attn_cols), swap_near(attn_cols)
    attended_far = wait(attended_far)
    attended_last = swap_near(attended_far)
    odd_a, pair_a = core_pair(wait(first_half), wait(swap_near(first_half)))
    line.made(pair_a)
    upper_a = upper_half(odd_a, pair_a)
    normed_flip = line.made(flip(after(normed_one, pair_a)))
    across_own = wait(across_own)
    across_far, across_near = swap_far(across_own), swap_near(across_own)
    tokens_far = wait(tokens_far)
    tokens_last = swap_near(tokens_far)
    attn_far = wait(attn_far)
    attn_last = swap_near(attn_far)
    tokens_oth = line.made(
        place(
            [tokens_swap, wait(tokens_near), tokens_far, wait(tokens_last)],
            quarters, (length, D), BF16, lambda at, t: (at, t),
        )
    )
    upper_a = wait(upper_a)
    near_a = swap_near(upper_a)
    attended = [attended, wait(attended_near), attended_far, wait(attended_last)]
    attn_full = line.made(
        place(
            [attn_cols, wait(attn_near), attn_far, wait(attn_last)],
            order, (D, D), BF16, lambda at, t: (t, at),
        )
    )
    across_far = wait(across_far)
    across_last = swap_near(across_far)
    second_half = wait(second_half)
    second_mate = swap_near(second_half)
    normed_own, hidden = hidden_and_norm(
        attended, heads_at, attn_full, tokens, gain_two, bias_two, True
    )
    line.made(normed_own)
    odd_b, pair_b = core_pair(second_half, wait(second_mate))
    line.made(pair_b)
    upper_b = upper_half(odd_b, pair_b)
    across_all = [across_own, wait(across_near), across_far, wait(across_last)]
    (normed_oth,) = hidden_and_norm(
        across_all, heads_at, attn_full, tokens_oth, gain_two, bias_two, False
    )
    line.made(normed_oth)
    upper_b = wait(upper_b)
    near_b = swap_near(upper_b)
    low_a, high_a = cot_sums(odd_a, pair_a, upper_a, wait(near_a))
    low_b, high_b = cot_sums(odd_b, pair_b, upper_b, wait(near_b))
    cot_oth = jnp.stack(
        [jnp.concatenate([low_a, low_b], axis=0), jnp.concatenate([high_a, high_b], axis=0)]
    )

    act, slope, *out_pieces = feed_up(
        units_at, normed_own, normed_oth, cot_own, cot_oth, w_in, block
    )
    line.made(out_pieces[0])
    inward = [hop(piece, inward_hops) for piece in out_pieces]
    *in_pieces, keep, send = feed_down(
        units_at, normed_own, normed_oth, cot_own, cot_oth, slope, w_in, w_out, block
    )
    line.made(keep)
    rows_near = swap_near(send)
    inward += [hop(piece, inward_hops) for piece in in_pieces]
    pieces = out_pieces + in_pieces
    low, full = feed_out(units_at, after(act, keep), w_out, block)
    line.made(low)
    out_near = swap_near(jnp.where(core == 0, full, low))

    pairs, others, totals, outward, finals, shared = {}, {}, {}, {}, {}, {}

    def chain_in(t):
        pairs[t] = line.made(plus(pieces[t], wait(inward[t])))
        others[t] = hop(pairs[t], inner_hops)

    def chain_mid(t):
        totals[t] = line.made(plus(pairs[t], wait(others[t])))
        outward[t] = hop(totals[t], outward_hops)

    def chain_out(t):
        finals[t] = line.made(jnp.where(end, wait(outward[t]), totals[t]))
        shared[t] = [swap_near(finals[t]), swap_far(finals[t])]

    def chain_far(t):
        shared[t][1] = wait(shared[t][1])
        shared[t].append(swap_near(shared[t][1]))

    grads = {"out": None, "in": None}

    def chain_place(t):
        near, far, last = shared[t]
        blocks = [finals[t], wait(near), far, wait(last)]
        if t < tiles:
            grads["out"] = place(
                blocks, order, w_out.shape, F32, lambda at, p: (at * tiles + t, p), grads["out"]
            )
            line.made(grads["out"])
        else:
            grads["in"] = place(
                blocks, order, w_in.shape, F32, lambda at, p: (p, at * tiles + t - tiles),
                grads["in"], flip=True,
            )
            line.made(grads["in"])

    rows = line.made((keep + wait(rows_near).astype(F32)).reshape(2, 2, quarter, D))
    rows_far = swap_far(round_low(one_of(rows, 1 - side, 1)))
    out_near = wait(out_near).astype(F32)
    below = round_low(out_near + full.astype(F32))
    below_own = lax.ppermute(line.made(below)[:length], "gran", ((1, 3),))
    chain_in(0)
    rows = line.made(one_of(rows, side, 1) + wait(rows_far).astype(F32))
    rows_hid = swap_hid(round_low(rows[1]))
    chain_in(1)
    chain_mid(0)
    dnormed_two = rows[0] + wait(rows_hid).astype(F32)
    dhidden, dlow, gain_two_term, bias_two_term = norm_backward(
        dnormed_two, rows_at(hidden, quarters[0], quarter), dsum, gain_two
    )
    line.made(dlow)
    dlow_far, dlow_near = swap_far(dlow), swap_near(dlow)
    below_oth = lax.ppermute(after(below, dlow)[length:], "gran", ((1, 3),))
    chain_in(2)
    chain_mid(1)
    chain_out(0)
    dlow_far = wait(dlow_far)
    dlow_last = swap_near(dlow_far)
    branches = [dlow, wait(dlow_near), dlow_far, wait(dlow_last)]

    dqkv, keep, send = attend_back(
        heads_at, branches, attended, attn_full, qkv, normed_flip, cosine, sine
    )
    line.made(dqkv)
    slots = [by_line(3, 3, 0, 0), by_line(2, 2, 1, 1), by_line(1, 0, 3, 2), dp_index]
    arrived = [swap_hid(one_of(send, index, 0)) for index in slots]
    chain_in(3)
    chain_mid(2)
    chain_out(1)
    chain_far(0)
    keep_one, send_one = normed_back(units_at, dqkv, qkv_cols)
    line.made(keep_one)
    rows_near = swap_near(send_one)

    def scatter_block(k):
        return line.made(plus(one_of(keep, slots[k], 0), wait(arrived[k])))

    block_a = scatter_block(0)
    first = hop(block_a, inward_hops)
    rows = line.made((keep_one + wait(rows_near).astype(F32)).reshape(2, quarter, D))
    rows_far = swap_far(round_low(one_of(rows, 1 - side, 0)))
    chain_place(0)
    chain_in(4)
    chain_mid(3)
    chain_out(2)
    chain_far(1)
    below_own = wait(below_own)
    below_own_near = lax.ppermute(below_own, "gran", ((3, 2),))
    below_oth = wait(below_oth)
    below_oth_near = lax.ppermute(below_oth, "gran", ((3, 2),))
    block_b = scatter_block(1)
    second = hop(block_b, inward_hops)
    block_c = scatter_block(2)
    block_d = scatter_block(3)

    dnormed_one = one_of(rows, side, 0) + wait(rows_far).astype(F32)
    _, dx, gain_one_term, bias_one_term = norm_backward(
        dnormed_one, rows_at(tokens, quarters[0], quarter), dhidden, gain_one
    )
    line.made(dx)
    dx_far, dx_near = swap_far(dx), swap_near(dx)
    vector_terms = jnp.concatenate(
        [gain_one_term, bias_one_term, gain_two_term, bias_two_term], axis=0
    )
    vector_near = swap_near(vector_terms)
    chain_in(5)
    chain_mid(4)
    chain_out(3)
    chain_far(2)
    chain_place(1)

    def out_share(part_of, below, below_near):
        total = jnp.where((core == 1) & (side == 1), part_of(full), part_of(low)).astype(F32)
        total = total + jnp.where(gran_index == 0, 0.0, part_of(out_near))
        total = total + below.astype(F32) + below_near.astype(F32)
        return jnp.where(far_hid & (gran_index < grans - 1), 0.0, total)

    share_oth = out_share(lambda array: array[length:], below_oth, wait(below_oth_near))
    share_oth = swap_hid(line.made(round_low(share_oth)))
    share_own = out_share(lambda array: array[:length], below_own, wait(below_own_near))
    vector_terms = vector_terms + wait(vector_near)
    vector_far = swap_far(vector_terms)
    chain_mid(5)
    chain_out(4)
    chain_far(3)
    chain_place(2)
    dx_far = wait(dx_far)
    dx_last = swap_near(dx_far)
    through = hop(line.made(plus(block_a, wait(first))), inner_hops)
    vector_terms = vector_terms + wait(vector_far)
    vector_hid = swap_hid(vector_terms)
    chain_out(5)
    chain_far(4)
    met = hop(line.made(plus(block_b, wait(second))), inner_hops)
    chain_place(3)
    outward_last = hop(line.made(plus(block_c, wait(through))), all_hops)
    x_grad = place(
        [dx, wait(dx_near), dx_far, wait(dx_last)],
        quarters, tokens.shape, F32, lambda at, t: (at, t),
    )
    line.made(x_grad)
    vector_terms = vector_terms + wait(vector_hid)
    vector_dp = hop(vector_terms, all_hops)
    outputs = (hidden + share_own + wait(share_oth).astype(F32)).astype(BF16)[None]
    line.made(outputs)
    chain_far(5)
    chain_place(4)
    vector_terms = vector_terms + wait(vector_dp)
    vector_dp = hop(vector_terms, ((0, 2), (2, 0), (1, 3), (3, 1)))
    term = block_d.astype(F32) + wait(outward_last).astype(F32)
    term = line.made(round_low(term + wait(met).astype(F32)))
    term_far, term_near = swap_far(term), swap_near(term)
    vector_terms = vector_terms + wait(vector_dp)
    width = ln1_gain.shape[0]
    vector_grads = lax.dynamic_slice_in_dim(
        vector_terms, (2 * dp_index + hid_index) * width, width, axis=1
    )
    chain_place(5)
    term_far = wait(term_far)
    term_last = swap_near(term_far)
    terms = [term, wait(term_near), term_far, wait(term_last)]
    qkv_grad = place(
        [term[:, : 3 * part] for term in terms], order, w_qkv.shape, F32,
        lambda at, t: (0, t * grans + at), None, 3,
    )
    attn_grad = place(
        [term[:, 3 * part :] for term in terms], order, w_attn.shape, F32, lambda at, t: (t, at)
    )

    return (
        outputs,
        x_grad,
        vector_grads[0],
        vector_grads[1],
        qkv_grad,
        attn_grad,
        vector_grads[2],
        vector_grads[3],
        grads["in"],
        grads["out"],
    )


def local_any(
    tokens,
    ln1_gain,
    ln1_bias,
    w_qkv,
    w_attn,
    ln2_gain,
    ln2_bias,
    w_in,
    w_out,
    cotangent,
    active_units,
):
    length = tokens.shape[0]
    grans = active_units.shape[0]
    hids = lax.axis_size("hid")
    gran_index = lax.axis_index("gran")
    hid_index = lax.axis_index("hid")
    heads = HEADS // grans
    part = heads * HD
    quarter = length // grans

    def head_columns(array, start):
        return lax.dynamic_slice_in_dim(array, start + gran_index * part, part, axis=1)

    vectors = jnp.stack([ln1_gain, ln1_bias, ln2_gain, ln2_bias], axis=1)
    qkv_rows = jnp.concatenate(
        [head_columns(w_qkv, 0), head_columns(w_qkv, D), head_columns(w_qkv, 2 * D), vectors], axis=1
    )
    qkv_all = lax.all_gather(qkv_rows, ALL_ROWS, axis=0, tiled=True)
    qkv_cols = qkv_all[:, : 3 * part]
    gains = qkv_all[:, 3 * part :].astype(F32).T
    gain_one, bias_one, gain_two, bias_two = (gains[i : i + 1] for i in range(4))
    attn_cols = lax.all_gather(head_columns(w_attn, 0), ALL_ROWS, axis=0, tiled=True)
    attn_full = lax.all_gather(attn_cols, "gran", axis=1, tiled=True)

    all_tokens = lax.all_gather(tokens, "hid", axis=0, tiled=True)
    out_grad = cotangent[0]
    all_cot = lax.all_gather(out_grad, LAYER, axis=0).reshape(hids, grans, length, D)
    slab = w_in.shape[1]
    block = slab // grans
    first_unit = hid_index * slab + gran_index * block
    total_units = slab * hids
    level = jnp.int32(0)
    for step in range(1, grans):
        bound = total_units * 2 ** (step - 1) // 8
        level = level + (first_unit >= bound).astype(jnp.int32)
    above = jnp.minimum(level + 1, grans - 1)

    def sum_from(start):
        keep = (jnp.arange(grans) >= start).astype(F32)[None, :, None, None]
        return jnp.sum(all_cot.astype(F32) * keep, axis=1).reshape(hids * length, D).astype(BF16)

    cot_lo, cot_hi = sum_from(level), sum_from(above)
    border = jnp.sum(jnp.where(jnp.arange(grans) == level, active_units, 0))
    low_unit = (first_unit + jnp.arange(block, dtype=jnp.int32)) < border
    cot_own = lax.psum_scatter(out_grad, "gran", scatter_dimension=0, tiled=True).astype(F32)

    x_rows = tokens.astype(F32)
    unit_one, scale_one = norm_parts(x_rows)
    normed_one = (unit_one * gain_one + bias_one).astype(BF16)
    qkv = dot(normed_one, qkv_cols)
    cosine, sine = rotary_tables(length)
    causal = jnp.arange(length)[:, None] >= jnp.arange(length)[None, :]
    kept, attended = [], []
    for head in range(heads):
        at = head * HD
        query = turn(qkv[:, at : at + HD], cosine, sine).astype(BF16)
        key = turn(qkv[:, part + at : part + at + HD], cosine, sine).astype(BF16)
        value = qkv[:, 2 * part + at : 2 * part + at + HD].astype(BF16)
        scores = jnp.where(causal, dot_nt(query, key) / math.sqrt(HD), -1000000000.0)
        exponent = jnp.exp(scores - jnp.max(scores, axis=-1, keepdims=True))
        probs = exponent / jnp.sum(exponent, axis=-1, keepdims=True)
        probs_low = probs.astype(BF16)
        attended.append(dot(probs_low, value).astype(BF16))
        kept.append((query, key, value, probs))
    attended = jnp.concatenate(attended, axis=1)
    everyone = lax.all_gather(attended, LAYER, axis=0).reshape(hids, grans, length, part)
    all_attended = everyone.transpose(0, 2, 1, 3).reshape(hids * length, D)
    hidden = all_tokens.astype(F32) + dot(all_attended, attn_full)
    unit_two, scale_two = norm_parts(hidden)
    normed_two = (unit_two * gain_two + bias_two).astype(BF16)

    w_in_block = lax.dynamic_slice_in_dim(w_in, gran_index * block, block, axis=1)
    w_out_block = lax.dynamic_slice_in_dim(w_out, gran_index * block, block, axis=0)
    pre = dot(normed_two, w_in_block)
    act, slope = gelu_both(pre)
    act = act.astype(BF16)
    dact = jnp.where(low_unit[None], dot_nt(cot_lo, w_out_block), dot_nt(cot_hi, w_out_block))
    dpre = (dact * slope).astype(BF16)
    out_term = jnp.where(low_unit[:, None], dot_tn(act, cot_lo), dot_tn(act, cot_hi))
    in_term = dot_tn(normed_two, dpre)
    dnormed_two = dot_nt(dpre, w_in_block).astype(BF16)

    out_term, in_term = lax.psum((out_term.astype(BF16), in_term.astype(BF16)), "dp")
    w_out_grad = lax.all_gather(out_term, "gran", axis=0, tiled=True)
    w_in_grad = lax.all_gather(in_term, "gran", axis=1, tiled=True)

    dnormed_two = lax.psum_scatter(dnormed_two, LAYER, scatter_dimension=0, tiled=True).astype(F32)
    row = hid_index * length + gran_index * quarter

    def own_rows(array):
        return lax.dynamic_slice_in_dim(array, row, quarter, axis=0)

    unit_two, scale_two = own_rows(unit_two), own_rows(scale_two)
    dhidden = cot_own + norm_back(dnormed_two, unit_two, scale_two, gain_two)
    gain_two_term = jnp.sum(dnormed_two * unit_two, axis=0)
    bias_two_term = jnp.sum(dnormed_two, axis=0)
    dbranch = lax.all_gather(dhidden.astype(BF16), "gran", axis=0, tiled=True)

    attn_rows = lax.dynamic_slice_in_dim(attn_full, gran_index * part, part, axis=0)
    dattended = dot_nt(dbranch, attn_rows).astype(BF16)
    own_attended = lax.dynamic_slice_in_dim(all_attended, hid_index * length, length, axis=0)
    dbranch_cols = lax.dynamic_slice_in_dim(dbranch, gran_index * part, part, axis=1)
    attn_term = dot_tn(own_attended, dbranch_cols)
    dqueries, dkeys, dvalues = [], [], []
    for head in range(heads):
        query, key, value, probs = kept[head]
        dvec = dattended[:, head * HD : (head + 1) * HD]
        dprobs = dot_nt(dvec, value)
        inner = jnp.sum(probs * dprobs, axis=-1, keepdims=True)
        dscores = (probs * (dprobs - inner)).astype(BF16)
        dqueries.append(turn_back(dot(dscores, key) / math.sqrt(HD), cosine, sine).astype(BF16))
        dkeys.append(turn_back(dot_tn(dscores, query) / math.sqrt(HD), cosine, sine).astype(BF16))
        dvalues.append(dot_tn(probs.astype(BF16), dvec).astype(BF16))
    dqkv = jnp.concatenate(dqueries + dkeys + dvalues, axis=1)
    qkv_term = dot_tn(normed_one, dqkv)
    dnormed_one = lax.psum_scatter(
        dot_nt(dqkv, qkv_cols).astype(BF16), "gran", scatter_dimension=0, tiled=True
    ).astype(F32)

    unit_one = lax.dynamic_slice_in_dim(unit_one, gran_index * quarter, quarter, axis=0)
    scale_one = lax.dynamic_slice_in_dim(scale_one, gran_index * quarter, quarter, axis=0)
    dx = dhidden + norm_back(dnormed_one, unit_one, scale_one, gain_one)
    gain_one_term = jnp.sum(dnormed_one * unit_one, axis=0)
    bias_one_term = jnp.sum(dnormed_one, axis=0)
    x_grad = lax.all_gather(dx.astype(BF16), "gran", axis=0, tiled=True).astype(F32)

    vector_terms = jnp.stack([gain_one_term, bias_one_term, gain_two_term, bias_two_term], axis=1)
    terms = jnp.concatenate([qkv_term, attn_term, vector_terms], axis=1).astype(BF16)
    terms = lax.psum_scatter(terms, ALL_ROWS, scatter_dimension=0, tiled=True)
    terms = lax.all_gather(terms, "gran", axis=0).astype(F32)

    def grads_of(start):
        return [terms[k, :, start : start + part] for k in range(grans)]

    qkv_grad = jnp.concatenate(grads_of(0) + grads_of(part) + grads_of(2 * part), axis=1)
    attn_grad = jnp.concatenate(grads_of(3 * part), axis=1)
    vector_grads = jnp.sum(terms[:, :, 4 * part :], axis=0).T

    act_low = jnp.where(low_unit[None], act, 0)
    part_low = dot(act_low, w_out_block)
    part_all = part_low + dot(act - act_low, w_out_block)
    shares = []
    for k in range(grans):
        share = jnp.where(level < k, part_all, jnp.where(level == k, part_low, 0.0))
        shares.append(share.astype(BF16).reshape(hids, length, D))
    shares = jnp.stack(shares, axis=1).reshape(hids * grans * length, D)
    ffn = lax.psum_scatter(shares, LAYER, scatter_dimension=0, tiled=True).astype(F32)
    own_hidden = lax.dynamic_slice_in_dim(hidden, hid_index * length, length, axis=0)
    outputs = (own_hidden + ffn).astype(BF16)[None]

    return (
        outputs,
        x_grad,
        vector_grads[0],
        vector_grads[1],
        qkv_grad,
        attn_grad,
        vector_grads[2],
        vector_grads[3],
        w_in_grad.astype(F32),
        w_out_grad.astype(F32),
    )


def solution(mesh):
    pairs = (mesh.shape["gran"], mesh.shape["dp"], mesh.shape["hid"]) == (4, 4, 2)
    return jax.shard_map(
        local_pairs if pairs else local_any,
        mesh=mesh,
        in_specs=(
            P(("dp", "hid"), None),
            P(("dp", "hid")),
            P(("dp", "hid")),
            P(("dp", "hid"), None),
            P(("dp", "hid"), None),
            P(("dp", "hid")),
            P(("dp", "hid")),
            P(None, "hid"),
            P("hid", None),
            P("gran", ("dp", "hid"), None),
            P(),
        ),
        out_specs=(
            P("gran", ("dp", "hid"), None),
            P(("dp", "hid"), None),
            P(("dp", "hid")),
            P(("dp", "hid")),
            P(("dp", "hid"), None),
            P(("dp", "hid"), None),
            P(("dp", "hid")),
            P(("dp", "hid")),
            P(None, "hid"),
            P("hid", None),
        ),
        check_vma=False,
    )
```

```python
import functools
import math

import jax
import jax.numpy as jnp
from jax import lax
from jax.experimental import pallas as pl
from jax.experimental.pallas import tpu as pltpu
from jax.sharding import PartitionSpec as P

D = 1536
HEADS = 12
HD = 128

EPS = 1e-05
GELU_C = 0.7978845608028654
GELU_A = 0.044715
BF16 = jnp.bfloat16
F32 = jnp.float32

ALL_ROWS = ("dp", "hid")
LAYER = ("hid", "gran")


def round_low(values):
    return lax.reduce_precision(values, 8, 7).astype(BF16)


def dot(left, right, contract=((1,), (0,))):
    return lax.dot_general(left, right, (contract, ((), ())), preferred_element_type=F32)


def dot_nt(left, right):
    return dot(left, right, ((1,), (1,)))


def dot_tn(left, right):
    return dot(left, right, ((0,), (0,)))


def norm_parts(values):
    centred = values - jnp.mean(values, axis=-1, keepdims=True)
    scale = lax.rsqrt(jnp.mean(centred * centred, axis=-1, keepdims=True) + EPS)
    return centred * scale, scale


def norm_back(dout, unit, scale, gain):
    inner = dout * gain
    return scale * (
        inner
        - jnp.mean(inner, axis=-1, keepdims=True)
        - unit * jnp.mean(inner * unit, axis=-1, keepdims=True)
    )


def gelu_both(values):
    square = values * values
    bent = jnp.tanh(GELU_C * values * (1.0 + GELU_A * square))
    half = 0.5 * (1.0 + bent)
    slope = half + 0.5 * values * (1.0 - bent * bent) * (GELU_C * (1.0 + 3.0 * GELU_A * square))
    return values * half, slope


def rotary_tables(length):
    half_dim = HD // 2
    freqs = 10000.0 ** (-(jnp.arange(half_dim, dtype=F32) * 2.0 / HD))
    angles = jnp.arange(length, dtype=F32)[:, None] * freqs[None, :]
    return jnp.cos(angles), jnp.sin(angles)


def turn(block, cosine, sine):
    lower, upper = block[:, : HD // 2], block[:, HD // 2 :]
    return jnp.concatenate([lower * cosine - upper * sine, upper * cosine + lower * sine], axis=1)


def turn_back(block, cosine, sine):
    return turn(block, cosine, -sine)


def after(value, *others):
    return lax.optimization_barrier((value,) + others)[0]


class Line:
    def __init__(self):
        self.last = None

    def wait(self, value):
        if self.last is not None:
            value = after(value, self.last)
        self.last = value
        return value

    def made(self, value):
        self.last = value
        return value


def swap_hid(value):
    return lax.ppermute(value, "hid", ((0, 1), (1, 0)))


def swap_near(value):
    return lax.ppermute(value, "gran", ((0, 1), (1, 0), (2, 3), (3, 2)))


def swap_far(value):
    return lax.ppermute(value, "gran", ((0, 2), (2, 0), (1, 3), (3, 1)))


def share(own):
    far = swap_far(own)
    return own, swap_near(own), far, swap_near(far)


def pick(index, options):
    chosen = options[-1]
    for k in range(len(options) - 2, -1, -1):
        chosen = jnp.where(index == k, options[k], chosen)
    return chosen


def params(vmem_mib=56):
    return pltpu.CompilerParams(vmem_limit_bytes=vmem_mib * 1024 * 1024)


def cost(flops, moved):
    return pl.CostEstimate(flops=flops, bytes_accessed=moved, transcendentals=0)


def whole_spec(shape):
    return pl.BlockSpec(shape, lambda *_: (0,) * len(shape))


def once_spec(shape):
    return pl.BlockSpec(shape, lambda *_: (0,) * len(shape), pipeline_mode=pl.Buffered(1))


def place_kernel(count, flip, at_ref, *refs):
    out_ref = refs[-1]
    for k in range(count):

        @pl.when(pl.program_id(0) == k)
        def _(k=k):
            block = refs[k][...].astype(out_ref.dtype)
            out_ref[...] = block.T if flip else block


def place(pieces, at, shape, dtype, where, whole=None, parts=1, flip=False):
    count = len(pieces)
    rows, columns = pieces[0].shape
    block = (rows, columns // parts)
    out_block = block[::-1] if flip else block
    specs = [pl.BlockSpec(block, lambda k, t, at: (0, t))] * count
    operands = list(pieces)
    aliases = {}
    if whole is not None:
        specs.append(pl.BlockSpec(memory_space=pl.ANY))
        operands.append(whole)
        aliases = {count + 1: 0}
    size = rows * columns * count * (2 + jnp.dtype(dtype).itemsize)
    return pl.pallas_call(
        functools.partial(place_kernel, count, flip),
        out_shape=jax.ShapeDtypeStruct(shape, dtype),
        grid_spec=pltpu.PrefetchScalarGridSpec(
            num_scalar_prefetch=1,
            grid=(count, parts),
            in_specs=specs,
            out_specs=pl.BlockSpec(out_block, lambda k, t, at: where(at[k], t)),
        ),
        input_output_aliases=aliases,
        compiler_params=params(40),
        cost_estimate=cost(0, size),
    )(jnp.stack(at).astype(jnp.int32), *operands)


def widen_kernel(in_ref, out_ref):
    out_ref[...] = in_ref[...].astype(F32)


def widen(array, steps=8):
    spec = pl.BlockSpec((array.shape[0] // steps, array.shape[1]), lambda i: (i, 0))
    return pl.pallas_call(
        widen_kernel,
        out_shape=jax.ShapeDtypeStruct(array.shape, F32),
        grid=(steps,),
        in_specs=[spec],
        out_specs=spec,
        compiler_params=params(32),
        cost_estimate=cost(0, array.size * 6),
    )(array)


def rotate(block, cos_ref, sin_ref, sign):
    return block * cos_ref[...] + pltpu.roll(block, HD // 2, 1) * (sign * sin_ref[...])


def probs_of(query, key, first_row):
    scores = dot_nt(query, key) * (1.0 / math.sqrt(HD))
    rows = first_row + lax.broadcasted_iota(jnp.int32, scores.shape, 0)
    scores = jnp.where(rows >= lax.broadcasted_iota(jnp.int32, scores.shape, 1), scores, -1e9)
    exponent = jnp.exp(scores - jnp.max(scores, axis=-1, keepdims=True))
    return exponent / jnp.sum(exponent, axis=-1, keepdims=True)


def attend_kernel(x_ref, gain_ref, bias_ref, w_ref, cos_ref, sin_ref, n1_ref, qkv_ref, att_ref):
    length, part = att_ref.shape
    unit, _ = norm_parts(x_ref[...].astype(F32))
    normed = (unit * gain_ref[...] + bias_ref[...]).astype(BF16)
    n1_ref[...] = normed
    for kind in range(3):
        product = dot(normed, w_ref[:, kind * part : (kind + 1) * part])
        for head in range(part // HD):
            block = product[:, head * HD : (head + 1) * HD]
            if kind < 2:
                block = rotate(block, cos_ref, sin_ref, 1.0)
            start = kind * part + head * HD
            qkv_ref[:, start : start + HD] = block.astype(BF16)
    half = length // 2
    for head in range(part // HD):
        cut = slice(head * HD, (head + 1) * HD)
        for row in range(2):
            rows, seen = slice(row * half, (row + 1) * half), slice(0, (row + 1) * half)
            query = qkv_ref[rows, cut]
            key = qkv_ref[seen, part + head * HD : part + (head + 1) * HD]
            value = qkv_ref[seen, 2 * part + head * HD : 2 * part + (head + 1) * HD]
            probs = probs_of(query, key, row * half).astype(BF16)
            att_ref[rows, cut] = dot(probs, value).astype(BF16)


def attend(tokens, gain, bias, weights, cosine, sine, part):
    length = tokens.shape[0]
    return pl.pallas_call(
        attend_kernel,
        out_shape=[
            jax.ShapeDtypeStruct((length, D), BF16),
            jax.ShapeDtypeStruct((length, 3 * part), BF16),
            jax.ShapeDtypeStruct((length, part), BF16),
        ],
        compiler_params=params(),
        cost_estimate=cost(2 * length * D * 3 * part * 2, 10_000_000),
    )(tokens, gain, bias, weights, cosine, sine)


def flip_kernel(in_ref, out_ref):
    out_ref[...] = in_ref[...].T


def flip(array):
    return pl.pallas_call(
        flip_kernel,
        out_shape=jax.ShapeDtypeStruct(array.shape[::-1], array.dtype),
        compiler_params=params(32),
        cost_estimate=cost(0, 2 * array.size * array.dtype.itemsize),
    )(array)


def hidden_kernel(keep, at_ref, a0, a1, a2, a3, w_ref, x_ref, gain_ref, bias_ref, *rest):
    out_refs, all_ref = rest[:-1], rest[-1]
    part = a0.shape[1]
    for k, ref in enumerate((a0, a1, a2, a3)):
        all_ref[:, pl.ds(pl.multiple_of(at_ref[k] * part, HD), part)] = ref[...]
    hidden = x_ref[...].astype(F32) + dot(all_ref[...], w_ref[...])
    unit, _ = norm_parts(hidden)
    out_refs[0][...] = (unit * gain_ref[...] + bias_ref[...]).astype(BF16)
    if keep:
        out_refs[1][...] = hidden


def hidden_and_norm(pieces, order, w_attn, tokens, gain, bias, keep):
    length = tokens.shape[0]
    rows, part = length // 2, pieces[0].shape[1]
    by_row = lambda columns: pl.BlockSpec((rows, columns), lambda i, at: (i, 0))
    types = [BF16, F32] if keep else [BF16]
    return pl.pallas_call(
        functools.partial(hidden_kernel, keep),
        out_shape=[jax.ShapeDtypeStruct((length, D), kind) for kind in types],
        grid_spec=pltpu.PrefetchScalarGridSpec(
            num_scalar_prefetch=1,
            grid=(2,),
            in_specs=[by_row(part)] * 4
            + [once_spec((D, D)), by_row(D), once_spec((1, D)), once_spec((1, D))],
            out_specs=[by_row(D)] * len(types),
            scratch_shapes=[pltpu.VMEM((rows, D), BF16)],
        ),
        compiler_params=params(),
        cost_estimate=cost(2 * length * D * D, 10_000_000),
    )(order, *pieces, w_attn, tokens, gain, bias)


UNITS = 256


def by_border(at_ref, low, high, mixed):
    border = at_ref[1] - pl.program_id(0) * UNITS
    pl.when(border >= UNITS)(low)
    pl.when(border <= 0)(high)
    pl.when((border > 0) & (border < UNITS))(mixed)


def up_kernel(at_ref, n_own, n_oth, s_own, s_oth, w_ref, act_ref, slope_ref, *out_refs):
    length = n_own.shape[0]
    for k, ref in enumerate((n_own, n_oth)):
        act, slope = gelu_both(dot(ref[...], w_ref[...]))
        act_ref[k * length : (k + 1) * length, :] = act.astype(BF16)
        slope_ref[k * length : (k + 1) * length, :] = slope

    def term(columns, which):
        return dot_tn(act_ref[:length, columns], s_own[which]) + dot_tn(
            act_ref[length:, columns], s_oth[which]
        )

    for k, ref in enumerate(out_refs):

        @pl.when(pl.program_id(0) == k)
        def _(ref=ref):
            def plain(which):
                def run():
                    ref[...] = term(slice(0, UNITS), which).astype(BF16)

                return run

            def mixed():
                ref[: UNITS // 2, :] = term(slice(0, UNITS // 2), 0).astype(BF16)
                ref[UNITS // 2 :, :] = term(slice(UNITS // 2, UNITS), 1).astype(BF16)

            by_border(at_ref, plain(0), plain(1), mixed)


def feed_up(at, n_own, n_oth, s_own, s_oth, w_in, block):
    length = n_own.shape[0]
    tiles = block // UNITS
    return pl.pallas_call(
        up_kernel,
        out_shape=[
            jax.ShapeDtypeStruct((2 * length, block), BF16),
            jax.ShapeDtypeStruct((2 * length, block), F32),
        ]
        + [jax.ShapeDtypeStruct((UNITS, D), BF16)] * tiles,
        grid_spec=pltpu.PrefetchScalarGridSpec(
            num_scalar_prefetch=1,
            grid=(tiles,),
            in_specs=[once_spec((length, D))] * 2
            + [once_spec((2, length, D))] * 2
            + [pl.BlockSpec((D, UNITS), lambda i, at: (0, at[0] * tiles + i))],
            out_specs=[pl.BlockSpec((2 * length, UNITS), lambda i, at: (0, i))] * 2
            + [whole_spec((UNITS, D))] * tiles,
        ),
        compiler_params=params(),
        cost_estimate=cost(8 * length * D * block, 20_000_000),
    )(at, n_own, n_oth, s_own, s_oth, w_in)


def down_kernel(at_ref, n_own, n_oth, s_own, s_oth, slope_ref, w_out, w_in, *rest):
    in_refs, (keep_ref, send_ref, dact, dpre_all) = rest[:-4], rest[-4:]
    length = n_own.shape[0]
    half = length // 2
    step = pl.program_id(0)

    def fill(columns, which):
        for k, ref in enumerate((s_own, s_oth)):
            dact[k * length : (k + 1) * length, columns] = dot_nt(ref[which], w_out[columns, :])

    def mixed():
        fill(slice(0, UNITS // 2), 0)
        fill(slice(UNITS // 2, UNITS), 1)

    by_border(
        at_ref, lambda: fill(slice(0, UNITS), 0), lambda: fill(slice(0, UNITS), 1), mixed
    )
    dpre = (dact[...] * slope_ref[...]).astype(BF16)
    term = dot_tn(dpre[:length], n_own[...]) + dot_tn(dpre[length:], n_oth[...])
    for k, ref in enumerate(in_refs):

        @pl.when(step == k)
        def _(k=k, ref=ref):
            dpre_all[:, k * UNITS : (k + 1) * UNITS] = dpre
            ref[...] = term.astype(BF16)

    @pl.when(step == len(in_refs) - 1)
    def _():
        core = at_ref[2]
        for k in range(2):
            theirs = pl.multiple_of(k * length + (1 - core) * half, half)
            send_ref[k] = dot_nt(dpre_all[pl.ds(theirs, half), :], w_in[...]).astype(BF16)
            mine = pl.multiple_of(k * length + core * half, half)
            keep_ref[k] = dot_nt(dpre_all[pl.ds(mine, half), :], w_in[...])


def feed_down(at, n_own, n_oth, s_own, s_oth, slope, w_in, w_out, block):
    length = n_own.shape[0]
    tiles = block // UNITS
    return pl.pallas_call(
        down_kernel,
        out_shape=[jax.ShapeDtypeStruct((UNITS, D), BF16)] * tiles
        + [
            jax.ShapeDtypeStruct((2, length // 2, D), F32),
            jax.ShapeDtypeStruct((2, length // 2, D), BF16),
        ],
        grid_spec=pltpu.PrefetchScalarGridSpec(
            num_scalar_prefetch=1,
            grid=(tiles,),
            in_specs=[once_spec((length, D))] * 2
            + [once_spec((2, length, D))] * 2
            + [
                pl.BlockSpec((2 * length, UNITS), lambda i, at: (0, i)),
                pl.BlockSpec((UNITS, D), lambda i, at: (at[0] * tiles + i, 0)),
                pl.BlockSpec(
                    (D, block), lambda i, at: (0, at[0]), pipeline_mode=pl.Buffered(1)
                ),
            ],
            out_specs=[once_spec((UNITS, D))] * tiles + [once_spec((2, length // 2, D))] * 2,
            scratch_shapes=[
                pltpu.VMEM((2 * length, UNITS), F32),
                pltpu.VMEM((2 * length, block), BF16),
            ],
        ),
        compiler_params=params(),
        cost_estimate=cost(12 * length * D * block, 30_000_000),
    )(at, n_own, n_oth, s_own, s_oth, slope, w_out, w_in)


def out_kernel(at_ref, n_own, n_oth, act_ref, w_ref, w_in, w_out, low_ref, full_ref, low, high):
    length = n_own.shape[0]
    step = pl.program_id(0)

    @pl.when(step == 0)
    def _():
        low[...] = jnp.zeros_like(low)
        high[...] = jnp.zeros_like(high)

    def add(into, cut):
        into[...] += dot(act_ref[:, cut], w_ref[cut, :])

    def mixed():
        add(low, slice(0, UNITS // 2))
        add(high, slice(UNITS // 2, UNITS))

    by_border(at_ref, lambda: add(low, slice(0, UNITS)), lambda: add(high, slice(0, UNITS)), mixed)

    @pl.when(at_ref[0] >= 2)
    def _():
        for k, ref in enumerate((n_own, n_oth)):
            act, _ = gelu_both(dot(ref[...], w_in[...]))
            rows = slice(k * length, (k + 1) * length)
            low[rows, :] += dot(act.astype(BF16), w_out[...])

    @pl.when(step == pl.num_programs(0) - 1)
    def _():
        low_ref[...] = low[...].astype(BF16)
        full_ref[...] = (low[...] + high[...]).astype(BF16)


def feed_out(at, n_own, n_oth, act, w_in, w_out, block):
    rows = act.shape[0]
    length = n_own.shape[0]
    tiles = block // UNITS
    return pl.pallas_call(
        out_kernel,
        out_shape=[jax.ShapeDtypeStruct((rows, D), BF16)] * 2,
        grid_spec=pltpu.PrefetchScalarGridSpec(
            num_scalar_prefetch=1,
            grid=(tiles,),
            in_specs=[once_spec((length, D))] * 2
            + [
                pl.BlockSpec((rows, UNITS), lambda i, at: (0, i)),
                pl.BlockSpec((UNITS, D), lambda i, at: (at[0] * tiles + i, 0)),
                pl.BlockSpec((D, UNITS), lambda i, at: (0, (at[0] % 2) * tiles + i)),
                pl.BlockSpec((UNITS, D), lambda i, at: ((at[0] % 2) * tiles + i, 0)),
            ],
            out_specs=[once_spec((rows, D))] * 2,
            scratch_shapes=[pltpu.VMEM((rows, D), F32)] * 2,
        ),
        compiler_params=params(),
        cost_estimate=cost(6 * rows * D * block, 10_000_000),
    )(at, n_own, n_oth, act, w_out, w_in, w_out)


def norm_back_kernel(dout_ref, x_ref, rest_ref, gain_ref, d_ref, low_ref, gain_out, bias_out):
    unit, scale = norm_parts(x_ref[...].astype(F32))
    dout = dout_ref[...]
    total = rest_ref[...] + norm_back(dout, unit, scale, gain_ref[...])
    d_ref[...] = total
    low_ref[...] = total.astype(BF16)
    gain_out[...] = jnp.sum(dout * unit, axis=0, keepdims=True)
    bias_out[...] = jnp.sum(dout, axis=0, keepdims=True)


def norm_backward(dout, rows, rest, gain):
    return pl.pallas_call(
        norm_back_kernel,
        out_shape=[
            jax.ShapeDtypeStruct(dout.shape, F32),
            jax.ShapeDtypeStruct(dout.shape, BF16),
            jax.ShapeDtypeStruct((1, D), F32),
            jax.ShapeDtypeStruct((1, D), F32),
        ],
        compiler_params=params(32),
        cost_estimate=cost(0, 4_000_000),
    )(dout, rows, rest, gain)


def attend_back_kernel(
    at_ref, b0, b1, b2, b3, a0, a1, a2, a3, w_ref, qkv_ref, n1_ref, cos_ref, sin_ref,
    dqkv_ref, keep_ref, send_ref, branch, block,
):
    length, part = a0.shape
    quarter = b0.shape[0]
    hid, gran = at_ref[8], at_ref[0]
    for k, ref in enumerate((b0, b1, b2, b3)):
        branch[pl.ds(pl.multiple_of(at_ref[4 + k] * quarter, quarter), quarter), :] = ref[...]
    dattended = dot_nt(branch[...], w_ref[...]).astype(BF16)
    half = length // 2
    scale = 1.0 / math.sqrt(HD)
    for head in range(part // HD):
        q_cut = slice(head * HD, (head + 1) * HD)
        k_cut = slice(part + head * HD, part + (head + 1) * HD)
        v_cut = slice(2 * part + head * HD, 2 * part + (head + 1) * HD)
        sums = {}
        for row in range(2):
            rows, seen = slice(row * half, (row + 1) * half), slice(0, (row + 1) * half)
            query, key, value = qkv_ref[rows, q_cut], qkv_ref[seen, k_cut], qkv_ref[seen, v_cut]
            probs = probs_of(query, key, row * half)
            dvec = dattended[rows, q_cut]
            dprobs = dot_nt(dvec, value)
            inner = jnp.sum(probs * dprobs, axis=-1, keepdims=True)
            dscores = (probs * (dprobs - inner)).astype(BF16)
            dquery = dot(dscores, key) * scale
            dquery = dquery * cos_ref[rows, :] - pltpu.roll(dquery, HD // 2, 1) * sin_ref[rows, :]
            dqkv_ref[rows, q_cut] = dquery.astype(BF16)
            sums[row] = dot_tn(dscores, query) * scale, dot_tn(probs.astype(BF16), dvec)
        for row in range(2):
            rows = slice(row * half, (row + 1) * half)
            dkey, dvalue = (sums[1][i][rows] + (sums[0][i] if row == 0 else 0.0) for i in range(2))
            dkey = dkey * cos_ref[rows, :] - pltpu.roll(dkey, HD // 2, 1) * sin_ref[rows, :]
            dqkv_ref[rows, k_cut] = dkey.astype(BF16)
            dqkv_ref[rows, v_cut] = dvalue.astype(BF16)
    piece = keep_ref.shape[1]
    mine = pl.multiple_of(hid * piece, 16)
    theirs = pl.multiple_of((1 - hid) * piece, 16)
    for line in range(4):
        rows = slice(line * 2 * piece, (line + 1) * 2 * piece)
        block[...] = dot(n1_ref[rows, :], dqkv_ref[...])
        keep_ref[line, :, : 3 * part] = block[pl.ds(mine, piece), :].astype(BF16)
        send_ref[line, :, : 3 * part] = block[pl.ds(theirs, piece), :].astype(BF16)
    own_columns = branch[:, pl.ds(pl.multiple_of(gran * part, HD), part)]
    for k, ref in enumerate((a0, a1, a2, a3)):
        block[:, :part] = dot_tn(ref[...], own_columns)
        keep_ref[at_ref[k], :, 3 * part :] = block[pl.ds(mine, piece), :part].astype(BF16)
        send_ref[at_ref[k], :, 3 * part :] = block[pl.ds(theirs, piece), :part].astype(BF16)


def attend_back(at, branches, attended, w_attn, qkv, n1, cosine, sine):
    length, part = attended[0].shape
    piece = D // 8
    quarter = branches[0].shape[0]
    out = jax.ShapeDtypeStruct((4, piece, 4 * part), BF16)
    return pl.pallas_call(
        attend_back_kernel,
        out_shape=[jax.ShapeDtypeStruct((length, 3 * part), BF16), out, out],
        grid_spec=pltpu.PrefetchScalarGridSpec(
            num_scalar_prefetch=1,
            grid=(1,),
            in_specs=[once_spec((quarter, D))] * 4
            + [once_spec((length, part))] * 4
            + [
                pl.BlockSpec((part, D), lambda i, at: (at[0], 0)),
                once_spec((length, 3 * part)),
                once_spec((D, length)),
                once_spec((length, HD)),
                once_spec((length, HD)),
            ],
            out_specs=[once_spec((length, 3 * part))] + [once_spec((4, piece, 4 * part))] * 2,
            scratch_shapes=[
                pltpu.VMEM((length, D), BF16),
                pltpu.VMEM((2 * piece, 3 * part), F32),
            ],
        ),
        compiler_params=params(),
        cost_estimate=cost(12 * length * D * part, 20_000_000),
    )(at, *branches, *attended, w_attn, qkv, n1, cosine, sine)


def normed_back_kernel(at_ref, dqkv_ref, w_ref, keep_ref, send_ref, total):
    half = keep_ref.shape[0]
    total[...] = dot_nt(dqkv_ref[...], w_ref[:, : dqkv_ref.shape[1]])
    core = at_ref[2]
    keep_ref[...] = total[pl.ds(pl.multiple_of(core * half, half), half), :]
    send_ref[...] = total[pl.ds(pl.multiple_of((1 - core) * half, half), half), :].astype(BF16)


def normed_back(at, dqkv, weights):
    length = dqkv.shape[0]
    return pl.pallas_call(
        normed_back_kernel,
        out_shape=[
            jax.ShapeDtypeStruct((length // 2, D), F32),
            jax.ShapeDtypeStruct((length // 2, D), BF16),
        ],
        grid_spec=pltpu.PrefetchScalarGridSpec(
            num_scalar_prefetch=1,
            grid=(1,),
            in_specs=[once_spec(dqkv.shape), once_spec(weights.shape)],
            out_specs=[once_spec((length // 2, D))] * 2,
            scratch_shapes=[pltpu.VMEM((length, D), F32)],
        ),
        compiler_params=params(),
        cost_estimate=cost(2 * length * D * dqkv.shape[1], 10_000_000),
    )(at, dqkv, weights)


def local_pairs(
    tokens,
    ln1_gain,
    ln1_bias,
    w_qkv,
    w_attn,
    ln2_gain,
    ln2_bias,
    w_in,
    w_out,
    cotangent,
    active_units,
):
    length = tokens.shape[0]
    grans = active_units.shape[0]
    gran_index = lax.axis_index("gran")
    dp_index = lax.axis_index("dp")
    hid_index = lax.axis_index("hid")
    core, side = gran_index % 2, gran_index // 2
    part = D // grans
    quarter = length // grans
    slab = w_in.shape[1]
    block = slab // grans
    tiles = block // UNITS
    order = [gran_index, gran_index ^ 1, gran_index ^ 2, gran_index ^ 3]
    row_of = lambda index: 2 * (index % 2) + index // 2
    quarters = [row_of(index) for index in order]
    first_unit = hid_index * slab + gran_index * block
    level = jnp.where(hid_index == 1, grans - 1, jnp.minimum(gran_index, 2))
    border = jnp.sum(jnp.where(jnp.arange(grans) == level, active_units, 0)) - first_unit
    heads_at = jnp.stack(order + quarters + [hid_index]).astype(jnp.int32)
    units_at = jnp.stack([gran_index, border, core]).astype(jnp.int32)

    def rows_at(array, index, count):
        return lax.dynamic_slice_in_dim(array, index * count, count, axis=0)

    def head_columns(array, start):
        return lax.dynamic_slice_in_dim(array, start + gran_index * part, part, axis=1)

    line = Line()
    wait = line.wait
    end = (dp_index == 0) | (dp_index == 3)
    all_hops = ((0, 1), (1, 0), (2, 3), (3, 2))
    inner_hops, outward_hops, inward_hops = ((1, 2), (2, 1)), ((1, 0), (2, 3)), ((0, 1), (3, 2))

    def hop(value, hops):
        return lax.ppermute(value, "dp", hops)

    def by_line(*options):
        return pick(dp_index, [jnp.int32(k) for k in options])

    def plus(block, carry):
        return round_low(block.astype(F32) + carry.astype(F32))

    def one_of(array, index, axis):
        return lax.dynamic_index_in_dim(array, index, axis=axis, keepdims=False)

    vectors = jnp.stack([ln1_gain, ln1_bias, ln2_gain, ln2_bias], axis=1)
    own_rows = jnp.concatenate(
        [head_columns(w_qkv, 0), head_columns(w_qkv, D), head_columns(w_qkv, 2 * D)]
        + [jnp.pad(vectors, ((0, 0), (0, HD - 4)))],
        axis=1,
    )
    out_grad = cotangent[0]
    far_hid = hid_index == 1

    one = hop(own_rows, all_hops)
    inner = hop(own_rows, inner_hops)
    own_swap = swap_hid(own_rows)
    attn_cols = lax.all_gather(head_columns(w_attn, 0), ALL_ROWS, axis=0, tiled=True)

    def mixed(flag, value):
        return value.astype(F32) * flag.astype(F32)

    def core_pair(cot, mate):
        even, odd = jnp.where(core == 0, cot, mate), jnp.where(core == 0, mate, cot)
        return odd, round_low(even.astype(F32) + odd.astype(F32))

    def upper_half(odd, pair):
        rows = rows_at(jnp.where(far_hid, odd, pair), core, odd.shape[0] // 2)
        return lax.ppermute(rows, "gran", ((2, 0), (3, 1)))

    def cot_sums(odd, pair, upper, near):
        upper = jnp.concatenate(
            [jnp.where(core == 0, upper, near), jnp.where(core == 0, near, upper)], axis=0
        )
        whole = ~far_hid & ((side == 1) | (core == 0))
        low = (
            mixed(whole, pair)
            + mixed(~whole & (~far_hid | (side == 1)), odd)
            + mixed(side == 0, upper)
        )
        high = mixed((side == 1) | (~far_hid & (core == 0)), odd) + mixed(side == 0, upper)
        return low.astype(BF16), high.astype(BF16)

    odd_own, pair_own = core_pair(out_grad, wait(swap_near(out_grad)))
    line.made(pair_own)
    upper_own = upper_half(odd_own, pair_own)
    one = wait(one)
    across = hop(one, inner_hops)
    one_swap = swap_hid(one)
    inner = wait(inner)
    outer = hop(inner, outward_hops)
    own_swap = wait(own_swap)
    upper_own = wait(upper_own)
    near_own = swap_near(upper_own)
    outer, across = wait(outer), wait(across)
    two = line.made(jnp.where(end, outer, inner))
    last = hop(across, outward_hops)
    two_swap = swap_hid(two)
    low, high = cot_sums(odd_own, pair_own, upper_own, wait(near_own))
    cot_own = line.made(jnp.stack([low, high]))
    dsum_far = swap_far(rows_at(after(pair_own, cot_own), quarters[2], quarter))
    one_swap = wait(one_swap)
    last = wait(last)
    three = line.made(jnp.where(end, last, across))
    three_swap = swap_hid(three)
    tokens_swap = swap_hid(rows_at(after(tokens, three), quarters[0], quarter))
    first_half = swap_hid(after(rows_at(out_grad, 0, length // 2), three))
    dsum = rows_at(pair_own, quarters[0], quarter).astype(F32) + wait(dsum_far).astype(F32)
    line.made(dsum)
    two_swap = wait(two_swap)
    three_swap = wait(three_swap)

    blocks, at = [], []
    for rows, other, index in (
        (own_rows, own_swap, dp_index),
        (one, one_swap, by_line(1, 0, 3, 2)),
        (two, two_swap, by_line(2, 2, 1, 1)),
        (three, three_swap, by_line(3, 3, 0, 0)),
    ):
        blocks += [rows, other]
        at += [2 * index + hid_index, 2 * index + 1 - hid_index]
    columns = own_rows.shape[1]
    qkv_cols = place(blocks, at, (D, columns), BF16, lambda at, t: (at, t))
    gains = qkv_cols[:, 3 * part : 3 * part + 4].astype(F32).T
    gain_one, bias_one, gain_two, bias_two = (gains[i : i + 1] for i in range(4))
    half_dim = HD // 2
    freqs = 10000.0 ** (-(jnp.arange(half_dim, dtype=F32) * 2.0 / HD))
    angles = jnp.arange(length, dtype=F32)[:, None] * freqs[None, :]
    cosine = jnp.concatenate([jnp.cos(angles)] * 2, axis=1)
    sine = jnp.concatenate([-jnp.sin(angles), jnp.sin(angles)], axis=1)
    normed_one, qkv, attended = attend(
        tokens, gain_one, bias_one, qkv_cols, cosine, sine, part
    )
    line.made(attended)
    across_own = swap_hid(attended)
    attended_far, attended_near = swap_far(attended), swap_near(attended)
    attn_cols = after(attn_cols, attended)
    attn_far = swap_far(attn_cols)

    attended_near = wait(attended_near)
    attended_far = wait(attended_far)
    attended_last = swap_near(attended_far)
    tokens_swap = wait(tokens_swap)
    tokens_far = swap_far(tokens_swap)
    tokens_near = swap_near(tokens_swap)
    attended = [attended, attended_near, attended_far, wait(attended_last)]
    first_half = wait(first_half)
    first_mate = swap_near(first_half)
    second_half = swap_hid(after(rows_at(out_grad, 1, length // 2), first_half))
    attn_near = swap_near(attn_cols)
    tokens_near = wait(tokens_near)
    odd_a, pair_a = core_pair(first_half, wait(first_mate))
    line.made(pair_a)
    upper_a = upper_half(odd_a, pair_a)
    across_own = wait(across_own)
    across_far, across_near = swap_far(across_own), swap_near(across_own)
    attn_far = wait(attn_far)
    attn_last = swap_near(attn_far)
    tokens_far = wait(tokens_far)
    tokens_last = swap_near(tokens_far)
    attn_near = wait(attn_near)
    upper_a = wait(upper_a)
    near_a = swap_near(upper_a)
    across_near = wait(across_near)
    attn_full = line.made(
        place(
            [attn_cols, attn_near, attn_far, wait(attn_last)],
            order, (D, D), BF16, lambda at, t: (t, at),
        )
    )
    across_far = wait(across_far)
    across_last = swap_near(across_far)
    normed_own, hidden = hidden_and_norm(
        attended, heads_at, attn_full, tokens, gain_two, bias_two, True
    )
    line.made(normed_own)
    second_half = wait(second_half)
    second_mate = swap_near(second_half)
    tokens_oth = line.made(
        place(
            [tokens_swap, tokens_near, tokens_far, wait(tokens_last)],
            quarters, (length, D), BF16, lambda at, t: (at, t),
        )
    )
    across_all = [across_own, across_near, across_far, wait(across_last)]
    odd_b, pair_b = core_pair(second_half, wait(second_mate))
    line.made(pair_b)
    upper_b = upper_half(odd_b, pair_b)
    (normed_oth,) = hidden_and_norm(
        across_all, heads_at, attn_full, tokens_oth, gain_two, bias_two, False
    )
    line.made(normed_oth)
    upper_b = wait(upper_b)
    near_b = swap_near(upper_b)
    low_a, high_a = cot_sums(odd_a, pair_a, upper_a, wait(near_a))
    low_b, high_b = cot_sums(odd_b, pair_b, upper_b, wait(near_b))
    cot_oth = jnp.stack(
        [jnp.concatenate([low_a, low_b], axis=0), jnp.concatenate([high_a, high_b], axis=0)]
    )

    act, slope, *out_pieces = feed_up(
        units_at, normed_own, normed_oth, cot_own, cot_oth, w_in, block
    )
    line.made(out_pieces[0])
    pieces = out_pieces

    inward, pairs, others, totals, outward, finals, shared = {}, {}, {}, {}, {}, {}, {}

    def chain_start(t):
        piece = pieces[t]
        if t >= 2:
            piece = after(piece, pairs[t - 2])
        inward[t] = hop(piece, inward_hops)

    def chain_in(t):
        pairs[t] = line.made(plus(pieces[t], wait(inward[t])))
        others[t] = hop(pairs[t], inner_hops)

    def chain_mid(t):
        totals[t] = line.made(plus(pairs[t], wait(others[t])))
        outward[t] = hop(totals[t], outward_hops)

    def chain_out(t):
        finals[t] = line.made(jnp.where(end, wait(outward[t]), totals[t]))

    def chain_share(t):
        shared[t] = [swap_near(finals[t]), swap_far(finals[t])]

    def chain_far(t):
        shared[t][1] = wait(shared[t][1])
        shared[t].append(swap_near(shared[t][1]))

    grads = {"out": None, "in": None}

    def chain_place(t):
        near, far, last = shared[t]
        blocks = [finals[t], wait(near), far, wait(last)]
        grads["in"] = place(
            blocks, order, w_in.shape, F32, lambda at, p: (p, at * tiles + t - tiles),
            grads["in"], flip=True,
        )
        line.made(grads["in"])

    chain_start(0)
    chain_start(1)
    *in_pieces, keep, send = feed_down(
        units_at, normed_own, normed_oth, cot_own, cot_oth, slope, w_in, w_out, block
    )
    line.made(keep)
    pieces = out_pieces + in_pieces
    rows_near = swap_near(send)
    chain_in(0)
    chain_start(2)

    rows = line.made((keep + wait(rows_near).astype(F32)).reshape(2, 2, quarter, D))
    rows_far = swap_far(round_low(one_of(rows, 1 - side, 1)))
    chain_in(1)
    chain_mid(0)
    chain_start(3)
    normed_flip = line.made(flip(after(normed_one, totals[0])))
    rows = line.made(one_of(rows, side, 1) + wait(rows_far).astype(F32))
    rows_hid = swap_hid(round_low(rows[1]))
    dnormed_two = rows[0] + wait(rows_hid).astype(F32)
    dhidden, dlow, gain_two_term, bias_two_term = norm_backward(
        dnormed_two, rows_at(hidden, quarters[0], quarter), dsum, gain_two
    )
    line.made(dlow)
    dlow_far, dlow_near = swap_far(dlow), swap_near(dlow)
    chain_in(2)
    chain_mid(1)
    chain_out(0)
    dlow_far = wait(dlow_far)
    dlow_last = swap_near(dlow_far)
    chain_start(4)
    dlow_near = wait(dlow_near)
    branches = [dlow, dlow_near, dlow_far, wait(dlow_last)]

    dqkv, keep, send = attend_back(
        heads_at, branches, attended, attn_full, qkv, normed_flip, cosine, sine
    )
    line.made(dqkv)
    slots = [by_line(3, 3, 0, 0), by_line(2, 2, 1, 1), by_line(1, 0, 3, 2), dp_index]

    def scatter_start(k):
        block = one_of(send, slots[k], 0)
        return swap_hid(after(block, line.last))

    def scatter_block(k, arrived):
        return line.made(plus(one_of(keep, slots[k], 0), wait(arrived)))

    arrived_a = scatter_start(0)
    chain_in(3)
    chain_mid(2)
    chain_out(1)
    chain_start(5)
    keep_one, send_one = normed_back(units_at, after(dqkv, finals[1]), qkv_cols)
    line.made(keep_one)
    rows_near = swap_near(send_one)
    block_a = scatter_block(0, arrived_a)
    arrived_b = scatter_start(1)
    rows = line.made((keep_one + wait(rows_near).astype(F32)).reshape(2, quarter, D))
    rows_far = swap_far(round_low(one_of(rows, 1 - side, 0)))
    chain_in(4)
    chain_mid(3)
    chain_out(2)
    out_all = lax.all_gather(
        jnp.concatenate([finals[0], finals[1], finals[2]], axis=0), "gran", axis=0, tiled=True
    )
    block_b = scatter_block(1, arrived_b)
    arrived_c = scatter_start(2)

    dnormed_one = one_of(rows, side, 0) + wait(rows_far).astype(F32)
    _, dx, gain_one_term, bias_one_term = norm_backward(
        dnormed_one, rows_at(tokens, quarters[0], quarter), dhidden, gain_one
    )
    line.made(dx)
    vector_terms = jnp.concatenate(
        [gain_one_term, bias_one_term, gain_two_term, bias_two_term], axis=0
    )
    vector_near = swap_near(vector_terms)
    low, full = feed_out(
        units_at, normed_own, normed_oth, after(act, dx), w_in, w_out, block
    )
    line.made(low)
    chain_in(5)
    chain_mid(4)
    chain_out(3)
    chain_share(3)
    vector_terms = vector_terms + wait(vector_near)
    block_c = scatter_block(2, arrived_c)
    arrived_d = scatter_start(3)
    first = hop(block_a, inward_hops)
    out_near = swap_near(jnp.where(core == 0, full, low))
    chain_mid(5)
    chain_out(4)
    chain_far(3)
    first = wait(first)
    through = hop(line.made(plus(block_a, first)), inner_hops)
    second = hop(after(block_b, first), inward_hops)
    chain_share(4)

    total = jnp.where((core == 1) & (side == 1), full, low).astype(F32)
    total = total + jnp.where(core == 0, jnp.where(side == 0, 0.0, 1.0), 1.0) * wait(
        out_near
    ).astype(F32)
    total = jnp.where(far_hid & (gran_index < grans - 1), 0.0, total)
    share_oth = swap_hid(line.made(round_low(total[length:])))
    chain_out(5)
    chain_place(3)
    chain_far(4)
    block_d = scatter_block(3, arrived_d)
    through = wait(through)
    outward_last = hop(line.made(plus(block_c, through)), all_hops)
    second = wait(second)
    met = hop(line.made(plus(block_b, second)), inner_hops)
    chain_share(5)
    outputs = (hidden + total[:length] + wait(share_oth).astype(F32)).astype(BF16)[None]
    line.made(outputs)
    vector_far = swap_far(vector_terms)
    chain_place(4)
    out_all = line.wait(out_all)
    grads["out"] = line.made(widen(out_all))
    x_all = lax.all_gather(dx, "gran", axis=0)
    vector_terms = vector_terms + wait(vector_far)
    vector_hid = swap_hid(vector_terms)
    chain_far(5)
    term = block_d.astype(F32) + wait(outward_last).astype(F32)
    term = line.made(round_low(term + wait(met).astype(F32)))
    term_far, term_near = swap_far(term), swap_near(term)
    vector_terms = vector_terms + wait(vector_hid)
    vector_dp = hop(vector_terms, all_hops)
    chain_place(5)
    term_near = wait(term_near)
    vector_terms = vector_terms + wait(vector_dp)
    vector_dp = hop(vector_terms, ((0, 2), (2, 0), (1, 3), (3, 1)))
    x_grad = wait(x_all).reshape(2, 2, quarter, D).transpose(1, 0, 2, 3)
    x_grad = line.made(x_grad.reshape(length, D).astype(F32))
    term_far = wait(term_far)
    term_last = swap_near(term_far)
    vector_terms = vector_terms + wait(vector_dp)
    width = ln1_gain.shape[0]
    vector_grads = lax.dynamic_slice_in_dim(
        vector_terms, (2 * dp_index + hid_index) * width, width, axis=1
    )
    terms = [term, term_near, term_far, wait(term_last)]
    qkv_grad = place(
        [term[:, : 3 * part] for term in terms], order, w_qkv.shape, F32,
        lambda at, t: (0, t * grans + at), None, 3,
    )
    attn_grad = place(
        [term[:, 3 * part :] for term in terms], order, w_attn.shape, F32, lambda at, t: (t, at)
    )

    return (
        outputs,
        x_grad,
        vector_grads[0],
        vector_grads[1],
        qkv_grad,
        attn_grad,
        vector_grads[2],
        vector_grads[3],
        grads["in"],
        grads["out"],
    )


def local_any(
    tokens,
    ln1_gain,
    ln1_bias,
    w_qkv,
    w_attn,
    ln2_gain,
    ln2_bias,
    w_in,
    w_out,
    cotangent,
    active_units,
):
    length = tokens.shape[0]
    grans = active_units.shape[0]
    hids = lax.axis_size("hid")
    gran_index = lax.axis_index("gran")
    hid_index = lax.axis_index("hid")
    heads = HEADS // grans
    part = heads * HD
    quarter = length // grans

    def head_columns(array, start):
        return lax.dynamic_slice_in_dim(array, start + gran_index * part, part, axis=1)

    vectors = jnp.stack([ln1_gain, ln1_bias, ln2_gain, ln2_bias], axis=1)
    qkv_rows = jnp.concatenate(
        [head_columns(w_qkv, 0), head_columns(w_qkv, D), head_columns(w_qkv, 2 * D), vectors], axis=1
    )
    qkv_all = lax.all_gather(qkv_rows, ALL_ROWS, axis=0, tiled=True)
    qkv_cols = qkv_all[:, : 3 * part]
    gains = qkv_all[:, 3 * part :].astype(F32).T
    gain_one, bias_one, gain_two, bias_two = (gains[i : i + 1] for i in range(4))
    attn_cols = lax.all_gather(head_columns(w_attn, 0), ALL_ROWS, axis=0, tiled=True)
    attn_full = lax.all_gather(attn_cols, "gran", axis=1, tiled=True)

    all_tokens = lax.all_gather(tokens, "hid", axis=0, tiled=True)
    out_grad = cotangent[0]
    all_cot = lax.all_gather(out_grad, LAYER, axis=0).reshape(hids, grans, length, D)
    slab = w_in.shape[1]
    block = slab // grans
    first_unit = hid_index * slab + gran_index * block
    total_units = slab * hids
    level = jnp.int32(0)
    for step in range(1, grans):
        bound = total_units * 2 ** (step - 1) // 8
        level = level + (first_unit >= bound).astype(jnp.int32)
    above = jnp.minimum(level + 1, grans - 1)

    def sum_from(start):
        keep = (jnp.arange(grans) >= start).astype(F32)[None, :, None, None]
        return jnp.sum(all_cot.astype(F32) * keep, axis=1).reshape(hids * length, D).astype(BF16)

    cot_lo, cot_hi = sum_from(level), sum_from(above)
    border = jnp.sum(jnp.where(jnp.arange(grans) == level, active_units, 0))
    low_unit = (first_unit + jnp.arange(block, dtype=jnp.int32)) < border
    cot_own = lax.psum_scatter(out_grad, "gran", scatter_dimension=0, tiled=True).astype(F32)

    x_rows = tokens.astype(F32)
    unit_one, scale_one = norm_parts(x_rows)
    normed_one = (unit_one * gain_one + bias_one).astype(BF16)
    qkv = dot(normed_one, qkv_cols)
    cosine, sine = rotary_tables(length)
    causal = jnp.arange(length)[:, None] >= jnp.arange(length)[None, :]
    kept, attended = [], []
    for head in range(heads):
        at = head * HD
        query = turn(qkv[:, at : at + HD], cosine, sine).astype(BF16)
        key = turn(qkv[:, part + at : part + at + HD], cosine, sine).astype(BF16)
        value = qkv[:, 2 * part + at : 2 * part + at + HD].astype(BF16)
        scores = jnp.where(causal, dot_nt(query, key) / math.sqrt(HD), -1000000000.0)
        exponent = jnp.exp(scores - jnp.max(scores, axis=-1, keepdims=True))
        probs = exponent / jnp.sum(exponent, axis=-1, keepdims=True)
        probs_low = probs.astype(BF16)
        attended.append(dot(probs_low, value).astype(BF16))
        kept.append((query, key, value, probs))
    attended = jnp.concatenate(attended, axis=1)
    everyone = lax.all_gather(attended, LAYER, axis=0).reshape(hids, grans, length, part)
    all_attended = everyone.transpose(0, 2, 1, 3).reshape(hids * length, D)
    hidden = all_tokens.astype(F32) + dot(all_attended, attn_full)
    unit_two, scale_two = norm_parts(hidden)
    normed_two = (unit_two * gain_two + bias_two).astype(BF16)

    w_in_block = lax.dynamic_slice_in_dim(w_in, gran_index * block, block, axis=1)
    w_out_block = lax.dynamic_slice_in_dim(w_out, gran_index * block, block, axis=0)
    pre = dot(normed_two, w_in_block)
    act, slope = gelu_both(pre)
    act = act.astype(BF16)
    dact = jnp.where(low_unit[None], dot_nt(cot_lo, w_out_block), dot_nt(cot_hi, w_out_block))
    dpre = (dact * slope).astype(BF16)
    out_term = jnp.where(low_unit[:, None], dot_tn(act, cot_lo), dot_tn(act, cot_hi))
    in_term = dot_tn(normed_two, dpre)
    dnormed_two = dot_nt(dpre, w_in_block).astype(BF16)

    out_term, in_term = lax.psum((out_term.astype(BF16), in_term.astype(BF16)), "dp")
    w_out_grad = lax.all_gather(out_term, "gran", axis=0, tiled=True)
    w_in_grad = lax.all_gather(in_term, "gran", axis=1, tiled=True)

    dnormed_two = lax.psum_scatter(dnormed_two, LAYER, scatter_dimension=0, tiled=True).astype(F32)
    row = hid_index * length + gran_index * quarter

    def own_rows(array):
        return lax.dynamic_slice_in_dim(array, row, quarter, axis=0)

    unit_two, scale_two = own_rows(unit_two), own_rows(scale_two)
    dhidden = cot_own + norm_back(dnormed_two, unit_two, scale_two, gain_two)
    gain_two_term = jnp.sum(dnormed_two * unit_two, axis=0)
    bias_two_term = jnp.sum(dnormed_two, axis=0)
    dbranch = lax.all_gather(dhidden.astype(BF16), "gran", axis=0, tiled=True)

    attn_rows = lax.dynamic_slice_in_dim(attn_full, gran_index * part, part, axis=0)
    dattended = dot_nt(dbranch, attn_rows).astype(BF16)
    own_attended = lax.dynamic_slice_in_dim(all_attended, hid_index * length, length, axis=0)
    dbranch_cols = lax.dynamic_slice_in_dim(dbranch, gran_index * part, part, axis=1)
    attn_term = dot_tn(own_attended, dbranch_cols)
    dqueries, dkeys, dvalues = [], [], []
    for head in range(heads):
        query, key, value, probs = kept[head]
        dvec = dattended[:, head * HD : (head + 1) * HD]
        dprobs = dot_nt(dvec, value)
        inner = jnp.sum(probs * dprobs, axis=-1, keepdims=True)
        dscores = (probs * (dprobs - inner)).astype(BF16)
        dqueries.append(turn_back(dot(dscores, key) / math.sqrt(HD), cosine, sine).astype(BF16))
        dkeys.append(turn_back(dot_tn(dscores, query) / math.sqrt(HD), cosine, sine).astype(BF16))
        dvalues.append(dot_tn(probs.astype(BF16), dvec).astype(BF16))
    dqkv = jnp.concatenate(dqueries + dkeys + dvalues, axis=1)
    qkv_term = dot_tn(normed_one, dqkv)
    dnormed_one = lax.psum_scatter(
        dot_nt(dqkv, qkv_cols).astype(BF16), "gran", scatter_dimension=0, tiled=True
    ).astype(F32)

    unit_one = lax.dynamic_slice_in_dim(unit_one, gran_index * quarter, quarter, axis=0)
    scale_one = lax.dynamic_slice_in_dim(scale_one, gran_index * quarter, quarter, axis=0)
    dx = dhidden + norm_back(dnormed_one, unit_one, scale_one, gain_one)
    gain_one_term = jnp.sum(dnormed_one * unit_one, axis=0)
    bias_one_term = jnp.sum(dnormed_one, axis=0)
    x_grad = lax.all_gather(dx.astype(BF16), "gran", axis=0, tiled=True).astype(F32)

    vector_terms = jnp.stack([gain_one_term, bias_one_term, gain_two_term, bias_two_term], axis=1)
    terms = jnp.concatenate([qkv_term, attn_term, vector_terms], axis=1).astype(BF16)
    terms = lax.psum_scatter(terms, ALL_ROWS, scatter_dimension=0, tiled=True)
    terms = lax.all_gather(terms, "gran", axis=0).astype(F32)

    def grads_of(start):
        return [terms[k, :, start : start + part] for k in range(grans)]

    qkv_grad = jnp.concatenate(grads_of(0) + grads_of(part) + grads_of(2 * part), axis=1)
    attn_grad = jnp.concatenate(grads_of(3 * part), axis=1)
    vector_grads = jnp.sum(terms[:, :, 4 * part :], axis=0).T

    act_low = jnp.where(low_unit[None], act, 0)
    part_low = dot(act_low, w_out_block)
    part_all = part_low + dot(act - act_low, w_out_block)
    shares = []
    for k in range(grans):
        share = jnp.where(level < k, part_all, jnp.where(level == k, part_low, 0.0))
        shares.append(share.astype(BF16).reshape(hids, length, D))
    shares = jnp.stack(shares, axis=1).reshape(hids * grans * length, D)
    ffn = lax.psum_scatter(shares, LAYER, scatter_dimension=0, tiled=True).astype(F32)
    own_hidden = lax.dynamic_slice_in_dim(hidden, hid_index * length, length, axis=0)
    outputs = (own_hidden + ffn).astype(BF16)[None]

    return (
        outputs,
        x_grad,
        vector_grads[0],
        vector_grads[1],
        qkv_grad,
        attn_grad,
        vector_grads[2],
        vector_grads[3],
        w_in_grad.astype(F32),
        w_out_grad.astype(F32),
    )


def solution(mesh):
    pairs = (mesh.shape["gran"], mesh.shape["dp"], mesh.shape["hid"]) == (4, 4, 2)
    return jax.shard_map(
        local_pairs if pairs else local_any,
        mesh=mesh,
        in_specs=(
            P(("dp", "hid"), None),
            P(("dp", "hid")),
            P(("dp", "hid")),
            P(("dp", "hid"), None),
            P(("dp", "hid"), None),
            P(("dp", "hid")),
            P(("dp", "hid")),
            P(None, "hid"),
            P("hid", None),
            P("gran", ("dp", "hid"), None),
            P(),
        ),
        out_specs=(
            P("gran", ("dp", "hid"), None),
            P(("dp", "hid"), None),
            P(("dp", "hid")),
            P(("dp", "hid")),
            P(("dp", "hid"), None),
            P(("dp", "hid"), None),
            P(("dp", "hid")),
            P(("dp", "hid")),
            P(None, "hid"),
            P("hid", None),
        ),
        check_vma=False,
    )
```

```python
import functools
import math

import jax
import jax.numpy as jnp
from jax import lax
from jax.experimental import pallas as pl
from jax.experimental.pallas import tpu as pltpu
from jax.sharding import PartitionSpec as P

D = 1536
HEADS = 12
HD = 128

EPS = 1e-05
GELU_C = 0.7978845608028654
GELU_A = 0.044715
BF16 = jnp.bfloat16
F32 = jnp.float32

ALL_ROWS = ("dp", "hid")
LAYER = ("hid", "gran")


def round_low(values):
    return lax.reduce_precision(values, 8, 7).astype(BF16)


def dot(left, right, contract=((1,), (0,))):
    return lax.dot_general(left, right, (contract, ((), ())), preferred_element_type=F32)


def dot_nt(left, right):
    return dot(left, right, ((1,), (1,)))


def dot_tn(left, right):
    return dot(left, right, ((0,), (0,)))


def norm_parts(values):
    centred = values - jnp.mean(values, axis=-1, keepdims=True)
    scale = lax.rsqrt(jnp.mean(centred * centred, axis=-1, keepdims=True) + EPS)
    return centred * scale, scale


def norm_back(dout, unit, scale, gain):
    inner = dout * gain
    return scale * (
        inner
        - jnp.mean(inner, axis=-1, keepdims=True)
        - unit * jnp.mean(inner * unit, axis=-1, keepdims=True)
    )


def gelu_both(values):
    square = values * values
    bent = jnp.tanh(GELU_C * values * (1.0 + GELU_A * square))
    half = 0.5 * (1.0 + bent)
    slope = half + 0.5 * values * (1.0 - bent * bent) * (GELU_C * (1.0 + 3.0 * GELU_A * square))
    return values * half, slope


def rotary_tables(length):
    half_dim = HD // 2
    freqs = 10000.0 ** (-(jnp.arange(half_dim, dtype=F32) * 2.0 / HD))
    angles = jnp.arange(length, dtype=F32)[:, None] * freqs[None, :]
    return jnp.cos(angles), jnp.sin(angles)


def turn(block, cosine, sine):
    lower, upper = block[:, : HD // 2], block[:, HD // 2 :]
    return jnp.concatenate([lower * cosine - upper * sine, upper * cosine + lower * sine], axis=1)


def turn_back(block, cosine, sine):
    return turn(block, cosine, -sine)


def after(value, *others):
    return lax.optimization_barrier((value,) + others)[0]


class Line:
    def __init__(self):
        self.last = None

    def wait(self, value):
        if self.last is not None:
            value = after(value, self.last)
        self.last = value
        return value

    def made(self, value):
        self.last = value
        return value


def swap_hid(value):
    return lax.ppermute(value, "hid", ((0, 1), (1, 0)))


def swap_near(value):
    return lax.ppermute(value, "gran", ((0, 1), (1, 0), (2, 3), (3, 2)))


def swap_far(value):
    return lax.ppermute(value, "gran", ((0, 2), (2, 0), (1, 3), (3, 1)))


def share(own):
    far = swap_far(own)
    return own, swap_near(own), far, swap_near(far)


def pick(index, options):
    chosen = options[-1]
    for k in range(len(options) - 2, -1, -1):
        chosen = jnp.where(index == k, options[k], chosen)
    return chosen


def params(vmem_mib=56):
    return pltpu.CompilerParams(vmem_limit_bytes=vmem_mib * 1024 * 1024)


def cost(flops, moved):
    return pl.CostEstimate(flops=flops, bytes_accessed=moved, transcendentals=0)


def whole_spec(shape):
    return pl.BlockSpec(shape, lambda *_: (0,) * len(shape))


def once_spec(shape):
    return pl.BlockSpec(shape, lambda *_: (0,) * len(shape), pipeline_mode=pl.Buffered(1))


def place_kernel(count, flip, at_ref, *refs):
    out_ref = refs[-1]
    for k in range(count):

        @pl.when(pl.program_id(0) == k)
        def _(k=k):
            block = refs[k][...].astype(out_ref.dtype)
            out_ref[...] = block.T if flip else block


def place(pieces, at, shape, dtype, where, whole=None, parts=1, flip=False):
    count = len(pieces)
    rows, columns = pieces[0].shape
    block = (rows, columns // parts)
    out_block = block[::-1] if flip else block
    specs = [pl.BlockSpec(block, lambda k, t, at: (0, t))] * count
    operands = list(pieces)
    aliases = {}
    if whole is not None:
        specs.append(pl.BlockSpec(memory_space=pl.ANY))
        operands.append(whole)
        aliases = {count + 1: 0}
    size = rows * columns * count * (2 + jnp.dtype(dtype).itemsize)
    return pl.pallas_call(
        functools.partial(place_kernel, count, flip),
        out_shape=jax.ShapeDtypeStruct(shape, dtype),
        grid_spec=pltpu.PrefetchScalarGridSpec(
            num_scalar_prefetch=1,
            grid=(count, parts),
            in_specs=specs,
            out_specs=pl.BlockSpec(out_block, lambda k, t, at: where(at[k], t)),
        ),
        input_output_aliases=aliases,
        compiler_params=params(40),
        cost_estimate=cost(0, size),
    )(jnp.stack(at).astype(jnp.int32), *operands)


def widen_kernel(in_ref, out_ref):
    out_ref[...] = in_ref[...].astype(F32)


def widen(array, steps=8):
    spec = pl.BlockSpec((array.shape[0] // steps, array.shape[1]), lambda i: (i, 0))
    return pl.pallas_call(
        widen_kernel,
        out_shape=jax.ShapeDtypeStruct(array.shape, F32),
        grid=(steps,),
        in_specs=[spec],
        out_specs=spec,
        compiler_params=params(32),
        cost_estimate=cost(0, array.size * 6),
    )(array)


def rotate(block, cos_ref, sin_ref, sign):
    return block * cos_ref[...] + pltpu.roll(block, HD // 2, 1) * (sign * sin_ref[...])


def probs_of(query, key, first_row):
    scores = dot_nt(query, key) * (1.0 / math.sqrt(HD))
    rows = first_row + lax.broadcasted_iota(jnp.int32, scores.shape, 0)
    scores = jnp.where(rows >= lax.broadcasted_iota(jnp.int32, scores.shape, 1), scores, -1e9)
    exponent = jnp.exp(scores - jnp.max(scores, axis=-1, keepdims=True))
    return exponent / jnp.sum(exponent, axis=-1, keepdims=True)


def attend_kernel(x_ref, gain_ref, bias_ref, w_ref, cos_ref, sin_ref, n1_ref, qkv_ref, att_ref):
    length, part = att_ref.shape
    unit, _ = norm_parts(x_ref[...].astype(F32))
    normed = (unit * gain_ref[...] + bias_ref[...]).astype(BF16)
    n1_ref[...] = normed
    for kind in range(3):
        product = dot(normed, w_ref[:, kind * part : (kind + 1) * part])
        for head in range(part // HD):
            block = product[:, head * HD : (head + 1) * HD]
            if kind < 2:
                block = rotate(block, cos_ref, sin_ref, 1.0)
            start = kind * part + head * HD
            qkv_ref[:, start : start + HD] = block.astype(BF16)
    half = length // 2
    for head in range(part // HD):
        cut = slice(head * HD, (head + 1) * HD)
        for row in range(2):
            rows, seen = slice(row * half, (row + 1) * half), slice(0, (row + 1) * half)
            query = qkv_ref[rows, cut]
            key = qkv_ref[seen, part + head * HD : part + (head + 1) * HD]
            value = qkv_ref[seen, 2 * part + head * HD : 2 * part + (head + 1) * HD]
            probs = probs_of(query, key, row * half).astype(BF16)
            att_ref[rows, cut] = dot(probs, value).astype(BF16)


def attend(tokens, gain, bias, weights, cosine, sine, part):
    length = tokens.shape[0]
    return pl.pallas_call(
        attend_kernel,
        out_shape=[
            jax.ShapeDtypeStruct((length, D), BF16),
            jax.ShapeDtypeStruct((length, 3 * part), BF16),
            jax.ShapeDtypeStruct((length, part), BF16),
        ],
        compiler_params=params(),
        cost_estimate=cost(2 * length * D * 3 * part * 2, 10_000_000),
    )(tokens, gain, bias, weights, cosine, sine)


def flip_kernel(in_ref, out_ref):
    out_ref[...] = in_ref[...].T


def flip(array):
    return pl.pallas_call(
        flip_kernel,
        out_shape=jax.ShapeDtypeStruct(array.shape[::-1], array.dtype),
        compiler_params=params(32),
        cost_estimate=cost(0, 2 * array.size * array.dtype.itemsize),
    )(array)


def project_kernel(at_ref, att_ref, mine_ref, other_ref, keep_ref, send_ref, w_ref, total):
    core, hid = at_ref[0], at_ref[1]
    piece = mine_ref.shape[0]
    quarter = keep_ref.shape[1]
    w_ref[pl.ds(pl.multiple_of(hid * piece, 16), piece), :] = mine_ref[...]
    w_ref[pl.ds(pl.multiple_of((1 - hid) * piece, 16), piece), :] = other_ref[...]
    total[...] = dot(att_ref[...], w_ref[...])
    for side in range(2):
        mine = pl.multiple_of((2 * side + core) * quarter, quarter)
        theirs = pl.multiple_of((2 * side + 1 - core) * quarter, quarter)
        keep_ref[side] = total[pl.ds(mine, quarter), :]
        send_ref[side] = total[pl.ds(theirs, quarter), :].astype(BF16)


def project(at, attended, mine, other):
    length, part = attended.shape
    quarter = length // 4
    return pl.pallas_call(
        project_kernel,
        out_shape=[
            jax.ShapeDtypeStruct((2, quarter, D), F32),
            jax.ShapeDtypeStruct((2, quarter, D), BF16),
            jax.ShapeDtypeStruct((part, D), BF16),
        ],
        grid_spec=pltpu.PrefetchScalarGridSpec(
            num_scalar_prefetch=1,
            grid=(1,),
            in_specs=[once_spec((length, part))] + [once_spec(mine.shape)] * 2,
            out_specs=[once_spec((2, quarter, D))] * 2 + [once_spec((part, D))],
            scratch_shapes=[pltpu.VMEM((length, D), F32)],
        ),
        compiler_params=params(40),
        cost_estimate=cost(2 * length * D * part, 5_000_000),
    )(at, attended, mine, other)


def norm_kernel(x_ref, keep_ref, got_ref, gain_ref, bias_ref, hidden_ref, out_ref):
    hidden = x_ref[...].astype(F32) + keep_ref[...] + got_ref[...].astype(F32)
    unit, _ = norm_parts(hidden)
    hidden_ref[...] = hidden
    out_ref[...] = (unit * gain_ref[...] + bias_ref[...]).astype(BF16)


def norm_rows(rows, keep, got, gain, bias):
    return pl.pallas_call(
        norm_kernel,
        out_shape=[
            jax.ShapeDtypeStruct(keep.shape, F32),
            jax.ShapeDtypeStruct(keep.shape, BF16),
        ],
        compiler_params=params(32),
        cost_estimate=cost(0, 3_000_000),
    )(rows, keep, got, gain, bias)


UNITS = 256


def by_border(at_ref, low, high, mixed):
    border = at_ref[1] - pl.program_id(0) * UNITS
    pl.when(border >= UNITS)(low)
    pl.when(border <= 0)(high)
    pl.when((border > 0) & (border < UNITS))(mixed)


def up_kernel(at_ref, n_ref, s_ref, w_ref, act_ref, slope_ref, *out_refs):
    act, slope = gelu_both(dot(n_ref[...], w_ref[...]))
    act_ref[...] = act.astype(BF16)
    slope_ref[...] = slope
    for k, ref in enumerate(out_refs):

        @pl.when(pl.program_id(0) == k)
        def _(ref=ref):
            def plain(which):
                def run():
                    ref[...] = dot_tn(act_ref[...], s_ref[which]).astype(BF16)

                return run

            def mixed():
                half = UNITS // 2
                ref[:half, :] = dot_tn(act_ref[:, :half], s_ref[0]).astype(BF16)
                ref[half:, :] = dot_tn(act_ref[:, half:], s_ref[1]).astype(BF16)

            by_border(at_ref, plain(0), plain(1), mixed)


def feed_up(at, normed, sums, w_in, block):
    rows = normed.shape[0]
    tiles = block // UNITS
    return pl.pallas_call(
        up_kernel,
        out_shape=[
            jax.ShapeDtypeStruct((rows, block), BF16),
            jax.ShapeDtypeStruct((rows, block), F32),
        ]
        + [jax.ShapeDtypeStruct((UNITS, D), BF16)] * tiles,
        grid_spec=pltpu.PrefetchScalarGridSpec(
            num_scalar_prefetch=1,
            grid=(tiles,),
            in_specs=[
                once_spec((rows, D)),
                once_spec((2, rows, D)),
                pl.BlockSpec((D, UNITS), lambda i, at: (0, at[0] * tiles + i)),
            ],
            out_specs=[pl.BlockSpec((rows, UNITS), lambda i, at: (0, i))] * 2
            + [whole_spec((UNITS, D))] * tiles,
        ),
        compiler_params=params(),
        cost_estimate=cost(4 * rows * D * block, 20_000_000),
    )(at, normed, sums, w_in)


def down_kernel(at_ref, n_ref, s_ref, slope_ref, w_out, w_in, *rest):
    in_refs, (total_ref, dact, dpre_all) = rest[:-3], rest[-3:]
    step = pl.program_id(0)

    def fill(columns, which):
        dact[:, columns] = dot_nt(s_ref[which], w_out[columns, :])

    def mixed():
        fill(slice(0, UNITS // 2), 0)
        fill(slice(UNITS // 2, UNITS), 1)

    by_border(
        at_ref, lambda: fill(slice(0, UNITS), 0), lambda: fill(slice(0, UNITS), 1), mixed
    )
    dpre = (dact[...] * slope_ref[...]).astype(BF16)
    term = dot_tn(dpre, n_ref[...])
    for k, ref in enumerate(in_refs):

        @pl.when(step == k)
        def _(k=k, ref=ref):
            dpre_all[:, k * UNITS : (k + 1) * UNITS] = dpre
            ref[...] = term.astype(BF16)

    @pl.when(step == len(in_refs) - 1)
    def _():
        rows = total_ref.shape[0] // 4
        for k in range(4):
            cut = slice(k * rows, (k + 1) * rows)
            total_ref[cut, :] = dot_nt(dpre_all[cut, :], w_in[...]).astype(BF16)


def feed_down(at, normed, sums, slope, w_in, w_out, block):
    rows = normed.shape[0]
    tiles = block // UNITS
    return pl.pallas_call(
        down_kernel,
        out_shape=[jax.ShapeDtypeStruct((UNITS, D), BF16)] * tiles
        + [jax.ShapeDtypeStruct((rows, D), BF16)],
        grid_spec=pltpu.PrefetchScalarGridSpec(
            num_scalar_prefetch=1,
            grid=(tiles,),
            in_specs=[
                once_spec((rows, D)),
                once_spec((2, rows, D)),
                pl.BlockSpec((rows, UNITS), lambda i, at: (0, i)),
                pl.BlockSpec((UNITS, D), lambda i, at: (at[0] * tiles + i, 0)),
                pl.BlockSpec(
                    (D, block), lambda i, at: (0, at[0]), pipeline_mode=pl.Buffered(1)
                ),
            ],
            out_specs=[once_spec((UNITS, D))] * tiles + [once_spec((rows, D))],
            scratch_shapes=[pltpu.VMEM((rows, UNITS), F32), pltpu.VMEM((rows, block), BF16)],
        ),
        compiler_params=params(),
        cost_estimate=cost(6 * rows * D * block, 30_000_000),
    )(at, normed, sums, slope, w_out, w_in)


def out_kernel(at_ref, n_ref, act_ref, w_ref, w_in, w_out, low_ref, full_ref, low, high):
    step = pl.program_id(0)

    @pl.when(step == 0)
    def _():
        low[...] = jnp.zeros_like(low)
        high[...] = jnp.zeros_like(high)

    def add(into, cut):
        into[...] += dot(act_ref[:, cut], w_ref[cut, :])

    def mixed():
        add(low, slice(0, UNITS // 2))
        add(high, slice(UNITS // 2, UNITS))

    by_border(at_ref, lambda: add(low, slice(0, UNITS)), lambda: add(high, slice(0, UNITS)), mixed)

    @pl.when(at_ref[0] >= 2)
    def _():
        act, _ = gelu_both(dot(n_ref[...], w_in[...]))
        low[...] += dot(act.astype(BF16), w_out[...])

    @pl.when(step == pl.num_programs(0) - 1)
    def _():
        low_ref[...] = low[...].astype(BF16)
        full_ref[...] = (low[...] + high[...]).astype(BF16)


def feed_out(at, normed, act, w_in, w_out, block):
    rows = act.shape[0]
    tiles = block // UNITS
    return pl.pallas_call(
        out_kernel,
        out_shape=[jax.ShapeDtypeStruct((rows, D), BF16)] * 2,
        grid_spec=pltpu.PrefetchScalarGridSpec(
            num_scalar_prefetch=1,
            grid=(tiles,),
            in_specs=[
                once_spec((rows, D)),
                pl.BlockSpec((rows, UNITS), lambda i, at: (0, i)),
                pl.BlockSpec((UNITS, D), lambda i, at: (at[0] * tiles + i, 0)),
                pl.BlockSpec((D, UNITS), lambda i, at: (0, (at[0] % 2) * tiles + i)),
                pl.BlockSpec((UNITS, D), lambda i, at: ((at[0] % 2) * tiles + i, 0)),
            ],
            out_specs=[once_spec((rows, D))] * 2,
            scratch_shapes=[pltpu.VMEM((rows, D), F32)] * 2,
        ),
        compiler_params=params(),
        cost_estimate=cost(6 * rows * D * block, 10_000_000),
    )(at, normed, act, w_out, w_in, w_out)


def norm_back_kernel(dout_ref, x_ref, rest_ref, gain_ref, d_ref, low_ref, gain_out, bias_out):
    unit, scale = norm_parts(x_ref[...].astype(F32))
    dout = dout_ref[...]
    total = rest_ref[...] + norm_back(dout, unit, scale, gain_ref[...])
    d_ref[...] = total
    low_ref[...] = total.astype(BF16)
    gain_out[...] = jnp.sum(dout * unit, axis=0, keepdims=True)
    bias_out[...] = jnp.sum(dout, axis=0, keepdims=True)


def norm_backward(dout, rows, rest, gain):
    return pl.pallas_call(
        norm_back_kernel,
        out_shape=[
            jax.ShapeDtypeStruct(dout.shape, F32),
            jax.ShapeDtypeStruct(dout.shape, BF16),
            jax.ShapeDtypeStruct((1, D), F32),
            jax.ShapeDtypeStruct((1, D), F32),
        ],
        compiler_params=params(32),
        cost_estimate=cost(0, 4_000_000),
    )(dout, rows, rest, gain)


def attend_back_kernel(
    at_ref, branch, att_ref, w_ref, qkv_ref, n1_ref, cos_ref, sin_ref, dqkv_ref, term_ref
):
    length, part = qkv_ref.shape[0], qkv_ref.shape[1] // 3
    dattended = dot_nt(branch[...], w_ref[...]).astype(BF16)
    half = length // 2
    scale = 1.0 / math.sqrt(HD)
    for head in range(part // HD):
        q_cut = slice(head * HD, (head + 1) * HD)
        k_cut = slice(part + head * HD, part + (head + 1) * HD)
        v_cut = slice(2 * part + head * HD, 2 * part + (head + 1) * HD)
        sums = {}
        for row in range(2):
            rows, seen = slice(row * half, (row + 1) * half), slice(0, (row + 1) * half)
            query, key, value = qkv_ref[rows, q_cut], qkv_ref[seen, k_cut], qkv_ref[seen, v_cut]
            probs = probs_of(query, key, row * half)
            dvec = dattended[rows, q_cut]
            dprobs = dot_nt(dvec, value)
            inner = jnp.sum(probs * dprobs, axis=-1, keepdims=True)
            dscores = (probs * (dprobs - inner)).astype(BF16)
            dquery = dot(dscores, key) * scale
            dquery = dquery * cos_ref[rows, :] - pltpu.roll(dquery, HD // 2, 1) * sin_ref[rows, :]
            dqkv_ref[rows, q_cut] = dquery.astype(BF16)
            sums[row] = dot_tn(dscores, query) * scale, dot_tn(probs.astype(BF16), dvec)
        for row in range(2):
            rows = slice(row * half, (row + 1) * half)
            dkey, dvalue = (sums[1][i][rows] + (sums[0][i] if row == 0 else 0.0) for i in range(2))
            dkey = dkey * cos_ref[rows, :] - pltpu.roll(dkey, HD // 2, 1) * sin_ref[rows, :]
            dqkv_ref[rows, k_cut] = dkey.astype(BF16)
            dqkv_ref[rows, v_cut] = dvalue.astype(BF16)
    own_columns = branch[:, pl.ds(pl.multiple_of(at_ref[0] * part, HD), part)]
    for k in range(D // part):
        rows = slice(k * part, (k + 1) * part)
        term_ref[rows, : 3 * part] = dot(n1_ref[rows, :], dqkv_ref[...]).astype(BF16)
        term_ref[rows, 3 * part :] = dot_tn(att_ref[k], own_columns).astype(BF16)


def attend_back(at, branch, attended, w_rows, qkv, n1, cosine, sine):
    length, part = attended.shape[1:]
    return pl.pallas_call(
        attend_back_kernel,
        out_shape=[
            jax.ShapeDtypeStruct((length, 3 * part), BF16),
            jax.ShapeDtypeStruct((D, 4 * part), BF16),
        ],
        grid_spec=pltpu.PrefetchScalarGridSpec(
            num_scalar_prefetch=1,
            grid=(1,),
            in_specs=[
                once_spec(array.shape)
                for array in (branch, attended, w_rows, qkv, n1, cosine, sine)
            ],
            out_specs=[once_spec((length, 3 * part)), once_spec((D, 4 * part))],
        ),
        compiler_params=params(),
        cost_estimate=cost(12 * length * D * part, 20_000_000),
    )(at, branch, attended, w_rows, qkv, n1, cosine, sine)


def normed_back_kernel(at_ref, dqkv_ref, w_ref, keep_ref, send_ref, total):
    total[...] = dot_nt(dqkv_ref[...], w_ref[:, : dqkv_ref.shape[1]])
    core = at_ref[2]
    quarter = keep_ref.shape[1]
    for side in range(2):
        mine = pl.multiple_of((2 * side + core) * quarter, quarter)
        theirs = pl.multiple_of((2 * side + 1 - core) * quarter, quarter)
        keep_ref[side] = total[pl.ds(mine, quarter), :]
        send_ref[side] = total[pl.ds(theirs, quarter), :].astype(BF16)


def normed_back(at, dqkv, weights):
    length = dqkv.shape[0]
    return pl.pallas_call(
        normed_back_kernel,
        out_shape=[
            jax.ShapeDtypeStruct((2, length // 4, D), F32),
            jax.ShapeDtypeStruct((2, length // 4, D), BF16),
        ],
        grid_spec=pltpu.PrefetchScalarGridSpec(
            num_scalar_prefetch=1,
            grid=(1,),
            in_specs=[once_spec(dqkv.shape), once_spec(weights.shape)],
            out_specs=[once_spec((2, length // 4, D))] * 2,
            scratch_shapes=[pltpu.VMEM((length, D), F32)],
        ),
        compiler_params=params(),
        cost_estimate=cost(2 * length * D * dqkv.shape[1], 10_000_000),
    )(at, dqkv, weights)


def local_pairs(
    tokens,
    ln1_gain,
    ln1_bias,
    w_qkv,
    w_attn,
    ln2_gain,
    ln2_bias,
    w_in,
    w_out,
    cotangent,
    active_units,
):
    length = tokens.shape[0]
    grans = active_units.shape[0]
    gran_index = lax.axis_index("gran")
    dp_index = lax.axis_index("dp")
    hid_index = lax.axis_index("hid")
    core, side = gran_index % 2, gran_index // 2
    far_hid = hid_index == 1
    end = (dp_index == 0) | (dp_index == 3)
    part = D // grans
    quarter = length // grans
    slab = w_in.shape[1]
    block = slab // grans
    tiles = block // UNITS
    order = [gran_index, gran_index ^ 1, gran_index ^ 2, gran_index ^ 3]
    first_unit = hid_index * slab + gran_index * block
    level = jnp.where(far_hid, grans - 1, jnp.minimum(gran_index, 2))
    border = jnp.sum(jnp.where(jnp.arange(grans) == level, active_units, 0)) - first_unit
    units_at = jnp.stack([gran_index, border, core]).astype(jnp.int32)
    core_at = jnp.stack([core, hid_index]).astype(jnp.int32)
    all_hops = ((0, 1), (1, 0), (2, 3), (3, 2))
    inner_hops, outward_hops, inward_hops = ((1, 2), (2, 1)), ((1, 0), (2, 3)), ((0, 1), (3, 2))
    line = Line()
    wait = line.wait

    def hop(value, hops):
        return lax.ppermute(value, "dp", hops)

    def by_line(*options):
        return pick(dp_index, [jnp.int32(k) for k in options])

    def plus(block, carry):
        return round_low(block.astype(F32) + carry.astype(F32))

    def one_of(array, index, axis):
        return lax.dynamic_index_in_dim(array, index, axis=axis, keepdims=False)

    def rows_at(array, index, count):
        return lax.dynamic_slice_in_dim(array, index * count, count, axis=0)

    def head_columns(array, start):
        return lax.dynamic_slice_in_dim(array, start + gran_index * part, part, axis=1)

    vectors = jnp.stack([ln1_gain, ln1_bias, ln2_gain, ln2_bias], axis=1)
    own_rows = jnp.concatenate(
        [head_columns(w_qkv, 0), head_columns(w_qkv, D), head_columns(w_qkv, 2 * D)]
        + [jnp.pad(vectors, ((0, 0), (0, HD - 4)))],
        axis=1,
    )
    out_grad = cotangent[0]

    def mixed(flag, value):
        return value.astype(F32) * flag.astype(F32)

    def core_pair(cot, mate):
        even, odd = jnp.where(core == 0, cot, mate), jnp.where(core == 0, mate, cot)
        return odd, round_low(even.astype(F32) + odd.astype(F32))

    def upper_half(odd, pair):
        rows = rows_at(jnp.where(far_hid, odd, pair), core, odd.shape[0] // 2)
        return lax.ppermute(rows, "gran", ((2, 0), (3, 1)))

    def cot_sums(odd, pair, upper, near):
        upper = jnp.concatenate(
            [jnp.where(core == 0, upper, near), jnp.where(core == 0, near, upper)], axis=0
        )
        whole = ~far_hid & ((side == 1) | (core == 0))
        low = (
            mixed(whole, pair)
            + mixed(~whole & (~far_hid | (side == 1)), odd)
            + mixed(side == 0, upper)
        )
        high = mixed((side == 1) | (~far_hid & (core == 0)), odd) + mixed(side == 0, upper)
        return jnp.stack([low.astype(BF16), high.astype(BF16)])

    one = hop(own_rows, all_hops)
    inner = hop(own_rows, inner_hops)
    own_swap = swap_hid(own_rows)
    odd_own, pair_own = core_pair(out_grad, wait(swap_near(out_grad)))
    line.made(pair_own)
    one = wait(one)
    inner = wait(inner)
    across = hop(one, inner_hops)
    outer = hop(inner, outward_hops)
    own_swap = wait(own_swap)
    one_swap = swap_hid(one)
    upper_own = upper_half(odd_own, pair_own)
    outer, across = wait(outer), wait(across)
    two = line.made(jnp.where(end, outer, inner))
    last = hop(across, outward_hops)
    one_swap = wait(one_swap)
    two_swap = swap_hid(two)
    upper_own = wait(upper_own)
    near_own = swap_near(upper_own)
    last = wait(last)
    three = line.made(jnp.where(end, last, across))
    two_swap = wait(two_swap)
    three_swap = swap_hid(three)
    attn_own = after(w_attn, three)
    attn_hop = lambda value, pairs: lax.ppermute(
        value, ("gran", "dp"), [(4 * g + a, 4 * g + b) for g, a, b in pairs]
    )
    attn_one = attn_hop(attn_own, ((0, 0, 1), (1, 1, 2), (2, 2, 1), (3, 3, 2)))
    cot_own = line.made(cot_sums(odd_own, pair_own, upper_own, wait(near_own)))
    dsum_far = swap_far(rows_at(after(pair_own, cot_own), order[2], quarter))
    three_swap = wait(three_swap)

    blocks, at = [], []
    for rows, other, index in (
        (own_rows, own_swap, dp_index),
        (one, one_swap, by_line(1, 0, 3, 2)),
        (two, two_swap, by_line(2, 2, 1, 1)),
        (three, three_swap, by_line(3, 3, 0, 0)),
    ):
        blocks += [rows, other]
        at += [2 * index + hid_index, 2 * index + 1 - hid_index]
    columns = own_rows.shape[1]
    qkv_cols = place(blocks, at, (D, columns), BF16, lambda at, t: (at, t))
    gains = qkv_cols[:, 3 * part : 3 * part + 4].astype(F32).T
    gain_one, bias_one, gain_two, bias_two = (gains[i : i + 1] for i in range(4))
    half_dim = HD // 2
    freqs = 10000.0 ** (-(jnp.arange(half_dim, dtype=F32) * 2.0 / HD))
    angles = jnp.arange(length, dtype=F32)[:, None] * freqs[None, :]
    cosine = jnp.concatenate([jnp.cos(angles)] * 2, axis=1)
    sine = jnp.concatenate([-jnp.sin(angles), jnp.sin(angles)], axis=1)
    attn_one = wait(attn_one)
    is_root = dp_index == gran_index
    attn_two = attn_hop(
        jnp.where(is_root, attn_own, attn_one),
        ((0, 1, 2), (1, 2, 3), (1, 1, 0), (2, 1, 0), (2, 2, 3), (3, 2, 1)),
    )
    line.made(qkv_cols)
    normed_one, qkv, attended = attend(
        tokens, gain_one, bias_one, qkv_cols, cosine, sine, part
    )
    line.made(attended)
    attn_two = wait(attn_two)
    attn_three = attn_hop(attn_two, ((0, 2, 3), (3, 1, 0)))
    dsum = rows_at(pair_own, order[0], quarter).astype(F32) + wait(dsum_far).astype(F32)
    attn_three = wait(attn_three)
    attn_rows = line.made(jnp.where(is_root, attn_own, attn_one + attn_two + attn_three))
    attn_other = swap_hid(attn_rows)
    cot_swap = swap_hid(after(out_grad, attn_rows))
    attn_other = wait(attn_other)
    keep, send, w_rows = project(core_at, attended, attn_rows, attn_other)
    line.made(keep)
    rows_near = swap_near(send)
    rows = line.made(keep + wait(rows_near).astype(F32))
    rows_far = swap_far(round_low(one_of(rows, 1 - side, 0)))
    all_attended = lax.all_gather(after(attended, rows), "gran", axis=0)
    normed_flip = line.made(flip(after(normed_one, rows)))
    hidden, normed_two = norm_rows(
        rows_at(tokens, gran_index, quarter), one_of(rows, side, 0), wait(rows_far),
        gain_two, bias_two,
    )
    line.made(hidden)
    normed = lax.all_gather(normed_two, LAYER, axis=0, tiled=True)
    cot_swap = wait(cot_swap)
    mate = swap_near(cot_swap)
    odd_oth, pair_oth = core_pair(cot_swap, wait(mate))
    line.made(pair_oth)
    upper_oth = wait(upper_half(odd_oth, pair_oth))
    cot_oth = line.made(cot_sums(odd_oth, pair_oth, upper_oth, wait(swap_near(upper_oth))))
    sums = jnp.concatenate(
        [jnp.where(far_hid, cot_oth, cot_own), jnp.where(far_hid, cot_own, cot_oth)], axis=1
    )
    line.made(sums)

    normed = wait(normed)
    all_hidden = lax.all_gather(after(hidden, normed), "gran", axis=0, tiled=True)
    act, slope, *out_pieces = feed_up(units_at, normed, sums, w_in, block)
    line.made(out_pieces[0])
    pieces = out_pieces

    moved, swapped, far, near = {}, {}, {}, {}
    pairs, totals, finals, joined = {}, {}, {}, {}
    count = 2 * tiles
    grads = {"out": None, "in": None}

    def chain_start(k):
        if k < 2:
            moved[k] = hop(pieces[k], inward_hops)
        elif k < count:
            moved[k] = hop(jnp.where(end, pieces[k], totals[k - 2]), all_hops)
        elif k < count + 2:
            moved[k] = hop(totals[k - 2], outward_hops)
        if 0 <= k - 1 < count:
            swapped[k - 1] = hop(pairs[k - 1], inner_hops)

    def chain_wait(k):
        if k < count + 2:
            moved[k] = wait(moved[k])
        if k < count:
            pairs[k] = line.made(plus(pieces[k], moved[k]))
        if 0 <= k - 1 < count:
            totals[k - 1] = line.made(plus(pairs[k - 1], wait(swapped[k - 1])))
        if 0 <= k - 2 < count:
            finals[k - 2] = jnp.where(end, moved[k], totals[k - 2])

    def share_start(k):
        if 0 <= k < count:
            far[k] = swap_far(finals[k])
        if 0 <= k - 1 < count:
            near[k - 1] = swap_near(joined[k - 1])

    def share_wait(k):
        if 0 <= k < count:
            joined[k] = line.made(jnp.stack([finals[k], wait(far[k])]))
        if 0 <= k - 1 < count:
            near[k - 1] = wait(near[k - 1])

    def chain_place(k):
        blocks = [finals[k], near[k][0], joined[k][1], near[k][1]]
        if k < tiles:
            grads["out"] = place(
                blocks, order, w_out.shape, F32, lambda at, p: (at * tiles + k, p), grads["out"]
            )
            line.made(grads["out"])
        else:
            grads["in"] = place(
                blocks, order, w_in.shape, F32, lambda at, p: (p, at * tiles + k - tiles),
                grads["in"], flip=True,
            )
            line.made(grads["in"])

    chain_start(0)
    *in_pieces, dnormed_two = feed_down(units_at, normed, sums, slope, w_in, w_out, block)
    pieces = out_pieces + in_pieces
    dnormed_two = lax.psum_scatter(dnormed_two, LAYER, scatter_dimension=0, tiled=True)
    line.made(in_pieces[0])
    chain_wait(0)
    chain_start(1)
    low, full = feed_out(units_at, normed, after(act, pairs[0]), w_in, w_out, block)
    line.made(low)
    chain_wait(1)
    chain_start(2)
    out_near = swap_near(jnp.where(core == 0, full, low))
    chain_wait(2)
    chain_start(3)

    dhidden, dlow, gain_two_term, bias_two_term = norm_backward(
        wait(dnormed_two).astype(F32), hidden, dsum, gain_two
    )
    line.made(dlow)
    branch = lax.all_gather(dlow, "gran", axis=0, tiled=True)
    out_near = wait(out_near)
    total = jnp.where((core == 1) & (side == 1), full, low).astype(F32)
    total = total + jnp.where(gran_index == 0, 0.0, 1.0) * out_near.astype(F32)
    total = jnp.where(far_hid & (gran_index < grans - 1), 0.0, total)
    total = total.reshape(2, length, D)
    share_oth = swap_hid(line.made(round_low(one_of(total, 1 - hid_index, 0))))
    chain_wait(3)
    chain_start(4)
    share_start(0)

    dqkv, terms = attend_back(
        units_at, wait(branch), all_attended, w_rows, qkv, normed_flip, cosine, sine
    )
    line.made(dqkv)
    terms = lax.psum_scatter(terms, ALL_ROWS, scatter_dimension=0, tiled=True)
    chain_wait(4)
    chain_start(5)
    share_wait(0)
    share_start(1)
    share_oth = wait(share_oth)
    outputs = (all_hidden + one_of(total, hid_index, 0) + share_oth.astype(F32)).astype(BF16)[None]
    keep, send = normed_back(units_at, after(dqkv, share_oth), qkv_cols)
    line.made(keep)
    rows_near = swap_near(send)
    chain_wait(5)
    chain_start(6)
    share_wait(1)
    share_start(2)
    rows = line.made(keep + wait(rows_near).astype(F32))
    rows_far = swap_far(round_low(one_of(rows, 1 - side, 0)))
    chain_place(0)
    chain_wait(6)
    chain_start(7)
    share_wait(2)
    share_start(3)

    dnormed_one = one_of(rows, side, 0) + wait(rows_far).astype(F32)
    _, dx, gain_one_term, bias_one_term = norm_backward(
        dnormed_one, rows_at(tokens, gran_index, quarter), dhidden, gain_one
    )
    line.made(dx)
    dx_far, dx_near = swap_far(dx), swap_near(dx)
    vector_terms = jnp.concatenate(
        [gain_one_term, bias_one_term, gain_two_term, bias_two_term], axis=0
    )
    chain_place(1)
    chain_wait(7)
    share_wait(3)
    share_start(4)
    dx_far = wait(dx_far)
    dx_last = swap_near(dx_far)
    vector_near = swap_near(vector_terms)
    chain_place(2)
    dx_near = wait(dx_near)
    dx_last = wait(dx_last)
    vector_terms = vector_terms + wait(vector_near)
    vector_far = swap_far(vector_terms)
    share_wait(4)
    share_start(5)
    chain_place(3)
    x_grad = line.made(
        place([dx, dx_near, dx_far, dx_last], order, tokens.shape, F32, lambda at, t: (at, t))
    )
    vector_terms = vector_terms + wait(vector_far)
    vector_hid = swap_hid(vector_terms)
    share_wait(5)
    share_start(6)
    vector_terms = vector_terms + wait(vector_hid)
    vector_dp = hop(vector_terms, all_hops)
    chain_place(4)
    share_wait(6)
    vector_terms = vector_terms + wait(vector_dp)
    vector_dp = hop(vector_terms, ((0, 2), (2, 0), (1, 3), (3, 1)))
    chain_place(5)
    vector_terms = vector_terms + wait(vector_dp)
    width = ln1_gain.shape[0]
    vector_grads = lax.dynamic_slice_in_dim(
        vector_terms, (2 * dp_index + hid_index) * width, width, axis=1
    )
    terms = wait(terms)
    terms_far, terms_near = swap_far(terms), swap_near(terms)
    terms_far = wait(terms_far)
    terms_last = swap_near(terms_far)
    terms = [terms, wait(terms_near), terms_far, wait(terms_last)]
    qkv_grad = place(
        [term[:, : 3 * part] for term in terms], order, w_qkv.shape, F32,
        lambda at, t: (0, t * grans + at), None, 3,
    )
    attn_grad = place(
        [term[:, 3 * part :] for term in terms], order, w_attn.shape, F32, lambda at, t: (t, at)
    )

    return (
        outputs,
        x_grad,
        vector_grads[0],
        vector_grads[1],
        qkv_grad,
        attn_grad,
        vector_grads[2],
        vector_grads[3],
        grads["in"],
        grads["out"],
    )


def local_any(
    tokens,
    ln1_gain,
    ln1_bias,
    w_qkv,
    w_attn,
    ln2_gain,
    ln2_bias,
    w_in,
    w_out,
    cotangent,
    active_units,
):
    length = tokens.shape[0]
    grans = active_units.shape[0]
    hids = lax.axis_size("hid")
    gran_index = lax.axis_index("gran")
    hid_index = lax.axis_index("hid")
    heads = HEADS // grans
    part = heads * HD
    quarter = length // grans

    def head_columns(array, start):
        return lax.dynamic_slice_in_dim(array, start + gran_index * part, part, axis=1)

    vectors = jnp.stack([ln1_gain, ln1_bias, ln2_gain, ln2_bias], axis=1)
    qkv_rows = jnp.concatenate(
        [head_columns(w_qkv, 0), head_columns(w_qkv, D), head_columns(w_qkv, 2 * D), vectors], axis=1
    )
    qkv_all = lax.all_gather(qkv_rows, ALL_ROWS, axis=0, tiled=True)
    qkv_cols = qkv_all[:, : 3 * part]
    gains = qkv_all[:, 3 * part :].astype(F32).T
    gain_one, bias_one, gain_two, bias_two = (gains[i : i + 1] for i in range(4))
    attn_cols = lax.all_gather(head_columns(w_attn, 0), ALL_ROWS, axis=0, tiled=True)
    attn_full = lax.all_gather(attn_cols, "gran", axis=1, tiled=True)

    all_tokens = lax.all_gather(tokens, "hid", axis=0, tiled=True)
    out_grad = cotangent[0]
    all_cot = lax.all_gather(out_grad, LAYER, axis=0).reshape(hids, grans, length, D)
    slab = w_in.shape[1]
    block = slab // grans
    first_unit = hid_index * slab + gran_index * block
    total_units = slab * hids
    level = jnp.int32(0)
    for step in range(1, grans):
        bound = total_units * 2 ** (step - 1) // 8
        level = level + (first_unit >= bound).astype(jnp.int32)
    above = jnp.minimum(level + 1, grans - 1)

    def sum_from(start):
        keep = (jnp.arange(grans) >= start).astype(F32)[None, :, None, None]
        return jnp.sum(all_cot.astype(F32) * keep, axis=1).reshape(hids * length, D).astype(BF16)

    cot_lo, cot_hi = sum_from(level), sum_from(above)
    border = jnp.sum(jnp.where(jnp.arange(grans) == level, active_units, 0))
    low_unit = (first_unit + jnp.arange(block, dtype=jnp.int32)) < border
    cot_own = lax.psum_scatter(out_grad, "gran", scatter_dimension=0, tiled=True).astype(F32)

    x_rows = tokens.astype(F32)
    unit_one, scale_one = norm_parts(x_rows)
    normed_one = (unit_one * gain_one + bias_one).astype(BF16)
    qkv = dot(normed_one, qkv_cols)
    cosine, sine = rotary_tables(length)
    causal = jnp.arange(length)[:, None] >= jnp.arange(length)[None, :]
    kept, attended = [], []
    for head in range(heads):
        at = head * HD
        query = turn(qkv[:, at : at + HD], cosine, sine).astype(BF16)
        key = turn(qkv[:, part + at : part + at + HD], cosine, sine).astype(BF16)
        value = qkv[:, 2 * part + at : 2 * part + at + HD].astype(BF16)
        scores = jnp.where(causal, dot_nt(query, key) / math.sqrt(HD), -1000000000.0)
        exponent = jnp.exp(scores - jnp.max(scores, axis=-1, keepdims=True))
        probs = exponent / jnp.sum(exponent, axis=-1, keepdims=True)
        probs_low = probs.astype(BF16)
        attended.append(dot(probs_low, value).astype(BF16))
        kept.append((query, key, value, probs))
    attended = jnp.concatenate(attended, axis=1)
    everyone = lax.all_gather(attended, LAYER, axis=0).reshape(hids, grans, length, part)
    all_attended = everyone.transpose(0, 2, 1, 3).reshape(hids * length, D)
    hidden = all_tokens.astype(F32) + dot(all_attended, attn_full)
    unit_two, scale_two = norm_parts(hidden)
    normed_two = (unit_two * gain_two + bias_two).astype(BF16)

    w_in_block = lax.dynamic_slice_in_dim(w_in, gran_index * block, block, axis=1)
    w_out_block = lax.dynamic_slice_in_dim(w_out, gran_index * block, block, axis=0)
    pre = dot(normed_two, w_in_block)
    act, slope = gelu_both(pre)
    act = act.astype(BF16)
    dact = jnp.where(low_unit[None], dot_nt(cot_lo, w_out_block), dot_nt(cot_hi, w_out_block))
    dpre = (dact * slope).astype(BF16)
    out_term = jnp.where(low_unit[:, None], dot_tn(act, cot_lo), dot_tn(act, cot_hi))
    in_term = dot_tn(normed_two, dpre)
    dnormed_two = dot_nt(dpre, w_in_block).astype(BF16)

    out_term, in_term = lax.psum((out_term.astype(BF16), in_term.astype(BF16)), "dp")
    w_out_grad = lax.all_gather(out_term, "gran", axis=0, tiled=True)
    w_in_grad = lax.all_gather(in_term, "gran", axis=1, tiled=True)

    dnormed_two = lax.psum_scatter(dnormed_two, LAYER, scatter_dimension=0, tiled=True).astype(F32)
    row = hid_index * length + gran_index * quarter

    def own_rows(array):
        return lax.dynamic_slice_in_dim(array, row, quarter, axis=0)

    unit_two, scale_two = own_rows(unit_two), own_rows(scale_two)
    dhidden = cot_own + norm_back(dnormed_two, unit_two, scale_two, gain_two)
    gain_two_term = jnp.sum(dnormed_two * unit_two, axis=0)
    bias_two_term = jnp.sum(dnormed_two, axis=0)
    dbranch = lax.all_gather(dhidden.astype(BF16), "gran", axis=0, tiled=True)

    attn_rows = lax.dynamic_slice_in_dim(attn_full, gran_index * part, part, axis=0)
    dattended = dot_nt(dbranch, attn_rows).astype(BF16)
    own_attended = lax.dynamic_slice_in_dim(all_attended, hid_index * length, length, axis=0)
    dbranch_cols = lax.dynamic_slice_in_dim(dbranch, gran_index * part, part, axis=1)
    attn_term = dot_tn(own_attended, dbranch_cols)
    dqueries, dkeys, dvalues = [], [], []
    for head in range(heads):
        query, key, value, probs = kept[head]
        dvec = dattended[:, head * HD : (head + 1) * HD]
        dprobs = dot_nt(dvec, value)
        inner = jnp.sum(probs * dprobs, axis=-1, keepdims=True)
        dscores = (probs * (dprobs - inner)).astype(BF16)
        dqueries.append(turn_back(dot(dscores, key) / math.sqrt(HD), cosine, sine).astype(BF16))
        dkeys.append(turn_back(dot_tn(dscores, query) / math.sqrt(HD), cosine, sine).astype(BF16))
        dvalues.append(dot_tn(probs.astype(BF16), dvec).astype(BF16))
    dqkv = jnp.concatenate(dqueries + dkeys + dvalues, axis=1)
    qkv_term = dot_tn(normed_one, dqkv)
    dnormed_one = lax.psum_scatter(
        dot_nt(dqkv, qkv_cols).astype(BF16), "gran", scatter_dimension=0, tiled=True
    ).astype(F32)

    unit_one = lax.dynamic_slice_in_dim(unit_one, gran_index * quarter, quarter, axis=0)
    scale_one = lax.dynamic_slice_in_dim(scale_one, gran_index * quarter, quarter, axis=0)
    dx = dhidden + norm_back(dnormed_one, unit_one, scale_one, gain_one)
    gain_one_term = jnp.sum(dnormed_one * unit_one, axis=0)
    bias_one_term = jnp.sum(dnormed_one, axis=0)
    x_grad = lax.all_gather(dx.astype(BF16), "gran", axis=0, tiled=True).astype(F32)

    vector_terms = jnp.stack([gain_one_term, bias_one_term, gain_two_term, bias_two_term], axis=1)
    terms = jnp.concatenate([qkv_term, attn_term, vector_terms], axis=1).astype(BF16)
    terms = lax.psum_scatter(terms, ALL_ROWS, scatter_dimension=0, tiled=True)
    terms = lax.all_gather(terms, "gran", axis=0).astype(F32)

    def grads_of(start):
        return [terms[k, :, start : start + part] for k in range(grans)]

    qkv_grad = jnp.concatenate(grads_of(0) + grads_of(part) + grads_of(2 * part), axis=1)
    attn_grad = jnp.concatenate(grads_of(3 * part), axis=1)
    vector_grads = jnp.sum(terms[:, :, 4 * part :], axis=0).T

    act_low = jnp.where(low_unit[None], act, 0)
    part_low = dot(act_low, w_out_block)
    part_all = part_low + dot(act - act_low, w_out_block)
    shares = []
    for k in range(grans):
        share = jnp.where(level < k, part_all, jnp.where(level == k, part_low, 0.0))
        shares.append(share.astype(BF16).reshape(hids, length, D))
    shares = jnp.stack(shares, axis=1).reshape(hids * grans * length, D)
    ffn = lax.psum_scatter(shares, LAYER, scatter_dimension=0, tiled=True).astype(F32)
    own_hidden = lax.dynamic_slice_in_dim(hidden, hid_index * length, length, axis=0)
    outputs = (own_hidden + ffn).astype(BF16)[None]

    return (
        outputs,
        x_grad,
        vector_grads[0],
        vector_grads[1],
        qkv_grad,
        attn_grad,
        vector_grads[2],
        vector_grads[3],
        w_in_grad.astype(F32),
        w_out_grad.astype(F32),
    )


def solution(mesh):
    pairs = (mesh.shape["gran"], mesh.shape["dp"], mesh.shape["hid"]) == (4, 4, 2)
    return jax.shard_map(
        local_pairs if pairs else local_any,
        mesh=mesh,
        in_specs=(
            P(("dp", "hid"), None),
            P(("dp", "hid")),
            P(("dp", "hid")),
            P(("dp", "hid"), None),
            P(("dp", "hid"), None),
            P(("dp", "hid")),
            P(("dp", "hid")),
            P(None, "hid"),
            P("hid", None),
            P("gran", ("dp", "hid"), None),
            P(),
        ),
        out_specs=(
            P("gran", ("dp", "hid"), None),
            P(("dp", "hid"), None),
            P(("dp", "hid")),
            P(("dp", "hid")),
            P(("dp", "hid"), None),
            P(("dp", "hid"), None),
            P(("dp", "hid")),
            P(("dp", "hid")),
            P(None, "hid"),
            P("hid", None),
        ),
        check_vma=False,
    )
```
